32 devices in a mesh: dp: 4 (over z), mp: 8 (over y, x, core).
Axes of the slice: x: 2, y: 2, z: 4, core: 2. Of those that a mesh axis runs over, the one named last changes fastest.
Arguments:
- tokens: bfloat16 [2, 1024, 4, 2048], P(None, 'mp', 'dp'), may hold values from -6 to 6
- lengths: int32 [2, 4], P(None, 'dp'), may hold values from 256 to 1024, as said below
- norm_gain: float32 [2048], replicated, may hold values from 0.1 to 1.9
- in_proj: bfloat16 [2048, 3, 2048], P(None, None, 'mp'), may hold values from -0.125 to 0.125
- short_taps: float32 [3, 3, 2048], P(None, None, 'mp'), may hold values from -3 to 3
- conv_skip: float32 [2048], P('mp'), may hold values from 0.5 to 1.5
- filter_residue: float32 [2048, 16], P('mp'), may hold values from -0.4 to 0.4
- filter_rate: float32 [2048, 16], P('mp'), may hold values from 0.002 to 0.05
- filter_freq: float32 [2048, 16], P('mp'), may hold values from 0 to 1
- out_proj: bfloat16 [2048, 2048], P('mp'), may hold values from -0.125 to 0.125
- mlp_gain: float32 [2048], replicated, may hold values from 0.1 to 1.9
- gate_proj: bfloat16 [2048, 5632], P(None, 'mp'), may hold values from -0.125 to 0.125
- up_proj: bfloat16 [2048, 5632], P(None, 'mp'), may hold values from -0.125 to 0.125
- down_proj: bfloat16 [5632, 2048], P('mp'), may hold values from -0.078125 to 0.078125
- cotangent: bfloat16 [2, 1024, 4, 2048], P(None, 'mp', 'dp'), may hold values from -6 to 6
Outputs:
- layer_out: bfloat16 [2, 1024, 4, 2048], P(None, 'mp', 'dp')
- grad_tokens: float32 [2, 1024, 4, 2048], P(None, 'mp', 'dp')
- grad_norm_gain: float32 [2048], replicated
- grad_in_proj: float32 [2048, 3, 2048], P(None, None, 'mp')
- grad_short_taps: float32 [3, 3, 2048], P(None, None, 'mp')
- grad_conv_skip: float32 [2048], P('mp')
- grad_filter_residue: float32 [2048, 16], P('mp')
- grad_filter_rate: float32 [2048, 16], P('mp')
- grad_filter_freq: float32 [2048, 16], P('mp')
- grad_out_proj: float32 [2048, 2048], P('mp')
- grad_mlp_gain: float32 [2048], replicated
- grad_gate_proj: float32 [2048, 5632], P(None, 'mp')
- grad_up_proj: float32 [2048, 5632], P(None, 'mp')
- grad_down_proj: float32 [5632, 2048], P('mp')
The draws below stay inside these ranges and needn't reach their ends.
Inputs may be any that keep to these rules, and one draw needn't show every extreme that they name: `lengths`: each sequence holds one document from its first position, at least a quarter of 1024 long; among the sequences of all micro-batches held by one index of dp, one (drawn) is exactly 1024 long.
All inputs are finite; a program needn't handle non-finite values.
Results may differ from the reference program's by a relative error of at most 0.017.
Values may be sent and summed in bfloat16 or wider, within the bound.
No kernel may reach another device: no remote copies, remote signals or barrier semaphores. Data moves between devices by JAX's collectives and lax.ppermute only.
A program may use at most 768 MiB of HBM per device.

```python
import math
import jax
import jax.numpy as jnp
from jax import lax

D = 2048
FF = 5632
POLES = 16
SHORT = 3
LEN = 1024
MB = 2
SEQ_DEV = 1
NSEQ = 4


def draw_lengths(key, part):
    key = jax.random.fold_in(key, 11)
    key_len, key_shift, key_pick = jax.random.split(key, 3)
    raw_lengths = jax.random.randint(key_len, (MB, NSEQ), 1, LEN + 1)
    shifts = jax.random.randint(key_shift, (MB, NSEQ), 0, 2)
    doc_lengths = jnp.maximum(jnp.right_shift(raw_lengths, shifts), LEN // 4)
    chosen = jax.random.randint(key_pick, (NSEQ // SEQ_DEV,), 0, MB * SEQ_DEV)
    micro_ids = jnp.arange(MB)[:, None]
    seq_ids = jnp.arange(NSEQ)[None, :]
    slot_index = micro_ids * SEQ_DEV + seq_ids % SEQ_DEV
    is_full = slot_index == chosen[seq_ids // SEQ_DEV]
    return jnp.where(is_full, LEN, doc_lengths).astype(jnp.int32)


def block_levels(rng, dims, shards, low, top_value):
    def one(dim, blocks):
        steps = jax.random.uniform(jax.random.fold_in(jax.random.fold_in(rng, 6), dim), (blocks,), jnp.float32, low / len(shards), top_value / len(shards))
        return jnp.repeat(jnp.exp(steps), dims[dim] // blocks).reshape((-1,) + (1,) * (len(dims) - dim - 1))

    gain = one(*shards[0])
    for cut in shards[1:]:
        gain = gain * one(*cut)
    return gain


def noise(stream_key, dims, scale, limit, cuts=(), dtype=jnp.bfloat16):
    gain = block_levels(stream_key, dims, cuts, -0.22, 0.18) if cuts else 1.0
    result = jax.random.normal(stream_key, dims, jnp.float32) * scale * gain
    return jnp.minimum(jnp.maximum(result, -limit), limit).astype(dtype)


def setup_inputs(seed: int = 0) -> dict:
    seeds = jax.random.split(jax.random.key(seed), 16)
    tokens = noise(seeds[0], (MB, LEN, NSEQ, D), 1.0, 6.0, ((1, 8), (2, 4)))
    lengths = draw_lengths(jax.random.fold_in(seeds[15], 71), 0)
    norm_gain = jnp.clip(1.0 + 0.18 * jax.random.normal(seeds[2], (D,), jnp.float32), 0.1, 1.9)
    in_proj = noise(seeds[3], (D, SHORT, D), D ** -0.5, 0.125, ((2, 8),))
    short_taps = noise(seeds[4], (SHORT, SHORT, D), 0.6, 3.0, ((2, 8),), jnp.float32)
    conv_skip = jnp.clip(0.5 + 1.0 * jax.random.uniform(seeds[5], (D,), jnp.float32) ** block_levels(seeds[5], (D,), ((0, 8),), -0.2, 0.2), 0.5, 1.5)
    filter_residue = noise(seeds[6], (D, POLES), 0.08, 0.4, ((0, 8),), jnp.float32)
    filter_rate = jnp.clip(jnp.exp(math.log(0.05) - 3.218876 * jax.random.uniform(seeds[7], (D, POLES), jnp.float32) ** block_levels(seeds[7], (D, POLES), ((0, 8),), -0.2, 0.2)), 0.002, 0.05)
    filter_freq = jnp.clip(1.0 * jax.random.uniform(seeds[8], (D, POLES), jnp.float32) ** block_levels(seeds[8], (D, POLES), ((0, 8),), -0.2, 0.2), 0.0, 1.0)
    out_proj = noise(seeds[9], (D, D), D ** -0.5, 0.125, ((0, 8),))
    mlp_gain = jnp.clip(1.0 + 0.18 * jax.random.normal(seeds[10], (D,), jnp.float32), 0.1, 1.9)
    gate_proj = noise(seeds[11], (D, FF), D ** -0.5, 0.125, ((1, 8),))
    up_proj = noise(seeds[12], (D, FF), D ** -0.5, 0.125, ((1, 8),))
    down_proj = noise(seeds[13], (FF, D), FF ** -0.5, 0.078125, ((0, 8),))
    cotangent = noise(seeds[14], (MB, LEN, NSEQ, D), 1.0, 6.0, ((1, 8), (2, 4)))
    return dict(tokens=tokens, lengths=lengths, norm_gain=norm_gain, in_proj=in_proj, short_taps=short_taps, conv_skip=conv_skip, filter_residue=filter_residue, filter_rate=filter_rate, filter_freq=filter_freq, out_proj=out_proj, mlp_gain=mlp_gain, gate_proj=gate_proj, up_proj=up_proj, down_proj=down_proj, cotangent=cotangent)


@jax.custom_vjp
def low(v):
    return lax.optimization_barrier(v.astype(jnp.bfloat16)).astype(jnp.float32)

@jax.custom_vjp
def low_back(v):
    return v

def low_keep(v):
    return (low(v), None)

def low_pass(kept, grad):
    return (grad,)

def back_keep(v):
    return (v, None)

def back_low(kept, grad):
    return (low(grad),)
low.defvjp(low_keep, low_pass)
low_back.defvjp(back_keep, back_low)
epsilon = 1e-06
highest = lax.Precision.HIGHEST

def matmul(left, right):
    return jnp.dot(left, right, precision=highest, preferred_element_type=jnp.float32)

def modal_filter(residue, rate, freq):
    positions = jnp.arange(LEN).astype(jnp.float32)

    def add_pole(running, pole):
        res_col, rate_col, freq_col = pole
        shaped = res_col[:, None] * jnp.exp(-rate_col[:, None] * positions[None, :]) * jnp.cos(freq_col[:, None] * positions[None, :])
        return (running + shaped, None)
    start_val = jnp.zeros((residue.shape[0], LEN), jnp.float32)
    total, unused = lax.scan(add_pole, start_val, (residue.T, rate.T, freq.T))
    return total

def rms_norm(rows_in, gain_vec):
    scale_rows = lax.rsqrt(lax.optimization_barrier(jnp.mean(rows_in * rows_in, axis=-1, keepdims=True)) + epsilon)
    return rows_in * scale_rows * gain_vec

def long_conv(signal, filt_low):
    fft_len = 2 * LEN
    spectrum = jnp.fft.rfft(signal, n=fft_len, axis=0) * jnp.fft.rfft(filt_low.T, n=fft_len, axis=0)
    return jnp.fft.irfft(spectrum, n=fft_len, axis=0)[:LEN]

def hyena_block(hidden_in, valid_rows, weight_set, filt_low):
    norm_gain, in_proj, short_taps, conv_skip, out_proj, mlp_gain, gate_proj, up_proj, down_proj = weight_set
    normed = low(rms_norm(hidden_in, norm_gain))
    projected = low_back(matmul(normed, in_proj.reshape(D, 3 * D))).reshape(LEN, 3, D)
    padded = jnp.pad(projected, ((2, 0), (0, 0), (0, 0)))
    shorted = short_taps[0] * padded[2:] + short_taps[1] * padded[1:-1] + short_taps[2] * padded[:-2]
    query_part = shorted[:, 0]
    key_part = shorted[:, 1]
    value_part = shorted[:, 2]
    mixed = low(key_part * value_part)
    conv_out = low_back(long_conv(mixed, filt_low))
    response = conv_out + conv_skip * mixed
    gated = low(query_part * response)
    branch = low_back(matmul(gated, out_proj))
    second = hidden_in + branch
    mlp_normed = low(rms_norm(second, mlp_gain))
    gate_vals = low_back(matmul(mlp_normed, gate_proj))
    up_vals = low_back(matmul(mlp_normed, up_proj))
    hidden = low(jax.nn.silu(gate_vals) * up_vals)
    mlp_out = low_back(matmul(hidden, down_proj))
    return (second + mlp_out) * valid_rows[:, None]

def reference(tokens, lengths, norm_gain, in_proj, short_taps, conv_skip, filter_residue, filter_rate, filter_freq, out_proj, mlp_gain, gate_proj, up_proj, down_proj, cotangent):
    seq_total = MB * NSEQ
    seq_rows = tokens.astype(jnp.float32).transpose(0, 2, 1, 3).reshape(seq_total, LEN, D)
    cotan_rows = cotangent.astype(jnp.float32).transpose(0, 2, 1, 3).reshape(seq_total, LEN, D)
    valid_all = (jnp.arange(LEN)[None, :] < lengths.reshape(seq_total, 1)).astype(jnp.float32)
    weight_set = (norm_gain.astype(jnp.float32), in_proj.astype(jnp.float32), short_taps.astype(jnp.float32), conv_skip.astype(jnp.float32), out_proj.astype(jnp.float32), mlp_gain.astype(jnp.float32), gate_proj.astype(jnp.float32), up_proj.astype(jnp.float32), down_proj.astype(jnp.float32))
    pole_set = (filter_residue.astype(jnp.float32), filter_rate.astype(jnp.float32), filter_freq.astype(jnp.float32))

    def forward(rows_all, weights_now, poles_now):
        filt_low = low(modal_filter(poles_now[0], poles_now[1], poles_now[2]))

        def per_sequence(item):
            return hyena_block(item[0], item[1], weights_now, filt_low)
        return lax.map(jax.checkpoint(per_sequence), (rows_all, valid_all))
    outputs, pullback = jax.vjp(forward, seq_rows, weight_set, pole_set)
    grad_rows, grad_weights, grad_poles = pullback(cotan_rows)

    def unflat(rows_all):
        return rows_all.reshape(MB, NSEQ, LEN, D).transpose(0, 2, 1, 3)
    return (unflat(outputs).astype(jnp.bfloat16), unflat(grad_rows), grad_weights[0], grad_weights[1], grad_weights[2], grad_weights[3], grad_poles[0], grad_poles[1], grad_poles[2], grad_weights[4], grad_weights[5], grad_weights[6], grad_weights[7], grad_weights[8])
```

```python
from functools import partial

import jax
import jax.numpy as jnp
import numpy as np
from jax import lax
from jax.experimental import pallas as pl
from jax.experimental.pallas import tpu as pltpu
from jax.sharding import PartitionSpec as P

epsilon = 1e-06
bf16 = jnp.bfloat16
f32 = jnp.float32
STEP = 32
VMEM_LIMIT = 52 * 1024 * 1024


def dft_matrix(length):
    freqs = np.arange(length)[:, None]
    times = np.arange(length)[None, :]
    angle = np.pi * (((2 * freqs + 1) * times) % (4 * length)) / (2 * length)
    return np.concatenate([np.cos(angle), -np.sin(angle)], axis=0)


def dot32(left, right):
    return jnp.dot(left, right, preferred_element_type=f32)


def contract_rows(left, right):
    return lax.dot_general(left, right, (((0,), (0,)), ((), ())), preferred_element_type=f32)


def contract_cols(left, right):
    return lax.dot_general(left, right, (((1,), (1,)), ((), ())), preferred_element_type=f32)


def row_scale(rows_in):
    return lax.rsqrt(jnp.mean(rows_in * rows_in, axis=-1, keepdims=True) + epsilon)


def norm_back(grad_y, rows_in, scale, gain):
    weighted = gain * grad_y
    inner = jnp.mean(weighted * rows_in, axis=-1, keepdims=True)
    return scale * weighted - rows_in * (scale * scale * scale) * inner


def filter_kernel(hre_ref, him_ref, lre_ref, lim_ref, res_ref, dft_ref, spec_ref, filt_ref):
    blocks, poles, chans = hre_ref.shape
    step = lre_ref.shape[1]
    residue = res_ref[...]

    def fill(block, carry):
        pre = residue * hre_ref[block]
        pim = residue * him_ref[block]
        total = jnp.zeros((step, chans), f32)
        for pole in range(poles):
            total = total + (
                pre[pole : pole + 1] * lre_ref[pole] - pim[pole : pole + 1] * lim_ref[pole]
            )
        filt_ref[pl.ds(pl.multiple_of(block * step, step), step), :] = total.astype(bf16)
        return carry

    lax.fori_loop(0, blocks, fill, 0)
    spec_ref[...] = dot32(dft_ref[...], filt_ref[...])


def pole_kernel(grad_ref, hre_ref, him_ref, lre_ref, lim_ref, sum_ref, vre_ref, vim_ref, turned):
    blocks, poles, chans = hre_ref.shape
    step = lre_ref.shape[1]
    for late in range(step):
        turned[late] = grad_ref[pl.ds(late, blocks, stride=step), :]
    starts = step * lax.broadcasted_iota(jnp.int32, (blocks, chans), 0).astype(f32)

    for pole in range(poles):
        lre, lim = lre_ref[pole], lim_ref[pole]
        part = turned[step - 1]
        sre = part * lre[step - 1 : step]
        sim = part * lim[step - 1 : step]
        tre, tim = sre, sim
        for late in range(step - 2, -1, -1):
            part = turned[late]
            sre = sre + part * lre[late : late + 1]
            sim = sim + part * lim[late : late + 1]
            if late:
                tre = tre + sre
                tim = tim + sim
        hre = hre_ref[:, pole, :]
        him = him_ref[:, pole, :]
        wre = starts * sre + tre
        wim = starts * sim + tim
        sum_ref[pole : pole + 1, :] = jnp.sum(hre * sre - him * sim, axis=0, keepdims=True)
        vre_ref[pole : pole + 1, :] = jnp.sum(hre * wre - him * wim, axis=0, keepdims=True)
        vim_ref[pole : pole + 1, :] = jnp.sum(hre * wim + him * wre, axis=0, keepdims=True)


def load_padded(me, parts, pad):
    blocks, _, rows, _ = parts[0].shape
    for index, part in enumerate(parts):
        pad[index, 0:8, :] = jnp.zeros((8, pad.shape[2]), f32)
        for block in range(blocks):
            pad[index, 8 + block * rows : 8 + (block + 1) * rows, :] = part[me ^ block, 0].astype(f32)


def short_rows(pad, taps, index, start, count):
    total = taps[index : index + 1] * pad[index, 8 + start : 8 + start + count, :]
    for back in (1, 2):
        tap = taps[3 * back + index : 3 * back + index + 1]
        total = total + tap * pad[index, 8 + start - back : 8 + start - back + count, :]
    return total


def mixer_kernel(
    me_ref, q_ref, k_ref, v_ref, taps_ref, skip_ref, filt_ref, dft_ref, inv_ref,
    gated_ref, resp_ref, spec_ref, pad, mixed, product, conv,
):
    me = me_ref[0]
    blocks, _, rows, chans = q_ref.shape
    length = blocks * rows
    load_padded(me, (q_ref, k_ref, v_ref), pad)
    taps = taps_ref[...]
    skip = skip_ref[...]
    for block in range(blocks):
        start = block * rows
        key = short_rows(pad, taps, 1, start, rows)
        value = short_rows(pad, taps, 2, start, rows)
        mixed[start : start + rows, :] = (key * value).astype(bf16)
    spec_ref[0] = dot32(dft_ref[...], mixed[...])
    for block in range(blocks):
        re = slice(block * rows, (block + 1) * rows)
        im = slice(length + block * rows, length + (block + 1) * rows)
        mre, mim = spec_ref[0, re, :], spec_ref[0, im, :]
        hre, him = filt_ref[re, :], filt_ref[im, :]
        product[re, :] = (mre * hre - mim * him).astype(bf16)
        product[im, :] = (mre * him + mim * hre).astype(bf16)
    conv[...] = dot32(inv_ref[...], product[...])
    for block in range(blocks):
        start = block * rows
        response = conv[start : start + rows, :] + skip * mixed[start : start + rows, :].astype(f32)
        resp_ref[0, start : start + rows, :] = response
        query = short_rows(pad, taps, 0, start, rows)
        gated_ref[me ^ block, 0] = (query * response).astype(bf16)


def mixer_back_kernel(
    me_ref, gg_ref, q_ref, k_ref, v_ref, resp_ref, spec_ref, taps_ref, skip_ref, filt_ref, dft_ref, inv_ref,
    gproj_ref, gtaps_ref, gskip_ref, gfilt_ref, pad, late, response_grad, grad_conv, spectrum, product, lags, conv,
):
    me = me_ref[0]
    sequence = pl.program_id(0)
    blocks, _, rows, chans = q_ref.shape
    length = blocks * rows
    load_padded(me, (q_ref, k_ref, v_ref), pad)
    taps = taps_ref[...]
    skip = skip_ref[...]

    @pl.when(sequence == 0)
    def _():
        gtaps_ref[...] = jnp.zeros_like(gtaps_ref)
        gskip_ref[...] = jnp.zeros_like(gskip_ref)
        lags[...] = jnp.zeros_like(lags)

    late[:, length : length + 8, :] = jnp.zeros((3, 8, chans), f32)
    skip_sum = jnp.zeros((1, chans), f32)
    for block in range(blocks):
        start = block * rows
        at = slice(start, start + rows)
        incoming = gg_ref[me ^ block, 0].astype(f32)
        query = short_rows(pad, taps, 0, start, rows)
        key = short_rows(pad, taps, 1, start, rows)
        value = short_rows(pad, taps, 2, start, rows)
        mixed = (key * value).astype(bf16).astype(f32)
        grad = incoming * query
        response_grad[at, :] = grad
        grad_conv[at, :] = grad.astype(bf16)
        late[0, at, :] = incoming * resp_ref[0, at, :]
        skip_sum = skip_sum + jnp.sum(grad * mixed, axis=0, keepdims=True)
    gskip_ref[...] += skip_sum

    spectrum[...] = dot32(dft_ref[...], grad_conv[...])
    for block in range(blocks):
        re = slice(block * rows, (block + 1) * rows)
        im = slice(length + block * rows, length + (block + 1) * rows)
        gre, gim = spectrum[re, :], spectrum[im, :]
        hre, him = filt_ref[re, :], filt_ref[im, :]
        mre, mim = spec_ref[0, re, :], spec_ref[0, im, :]
        product[re, :] = (gre * hre + gim * him).astype(bf16)
        product[im, :] = (gim * hre - gre * him).astype(bf16)
        lags[re, :] += gre * mre + gim * mim
        lags[im, :] += gim * mre - gre * mim
    conv[...] = dot32(inv_ref[...], product[...])

    for block in range(blocks):
        start = block * rows
        at = slice(start, start + rows)
        key = short_rows(pad, taps, 1, start, rows)
        value = short_rows(pad, taps, 2, start, rows)
        grad_mixed = conv[at, :] + skip * response_grad[at, :]
        late[1, at, :] = grad_mixed * value
        late[2, at, :] = grad_mixed * key

    sums = [jnp.zeros((1, chans), f32) for _ in range(9)]
    for block in range(blocks):
        start = block * rows
        for index in range(3):
            grad = late[index, start : start + rows, :]
            total = taps[index : index + 1] * grad
            for back in (1, 2):
                tap = taps[3 * back + index : 3 * back + index + 1]
                total = total + tap * late[index, start + back : start + back + rows, :]
            gproj_ref[me ^ block, 0, :, index * chans : (index + 1) * chans] = total.astype(bf16)
            for back in range(3):
                shifted = pad[index, 8 + start - back : 8 + start - back + rows, :]
                sums[3 * back + index] = sums[3 * back + index] + jnp.sum(
                    grad * shifted, axis=0, keepdims=True
                )
    for index in range(9):
        gtaps_ref[index : index + 1, :] += sums[index]

    @pl.when(sequence == pl.num_programs(0) - 1)
    def _():
        product[...] = lags[...].astype(bf16)
        gfilt_ref[...] = dot32(inv_ref[...], product[...])


def whole(shape):
    return pl.BlockSpec(shape, lambda *_: (0,) * len(shape), pipeline_mode=pl.Buffered(1))


def params():
    return pltpu.CompilerParams(vmem_limit_bytes=VMEM_LIMIT)


def make_filter(tables, residue_t, dft):
    hre, him, lre, lim = tables
    chans = residue_t.shape[1]
    length = dft.shape[1]
    operands = (hre, him, lre, lim, residue_t, dft)
    return pl.pallas_call(
        filter_kernel,
        grid=(1,),
        in_specs=[whole(op.shape) for op in operands],
        out_specs=whole((2 * length, chans)),
        out_shape=jax.ShapeDtypeStruct((2 * length, chans), f32),
        scratch_shapes=[pltpu.VMEM((length, chans), bf16)],
        compiler_params=params(),
        name="modal_filter",
    )(*operands)


def pole_gradients(grad_filt, tables):
    hre, him, lre, lim = tables
    blocks, poles, chans = hre.shape
    step = lre.shape[1]
    lanes = min(chans, 128)

    def lane_block(*lead):
        return pl.BlockSpec(lead + (lanes,), lambda c: (0,) * len(lead) + (c,))

    operands = (grad_filt, hre, him, lre, lim)
    return pl.pallas_call(
        pole_kernel,
        grid=(chans // lanes,),
        in_specs=[lane_block(*op.shape[:-1]) for op in operands],
        out_specs=[lane_block(poles)] * 3,
        out_shape=[jax.ShapeDtypeStruct((poles, chans), f32)] * 3,
        scratch_shapes=[pltpu.VMEM((step, blocks, lanes), f32)],
        compiler_params=params(),
        name="pole_gradients",
    )(*operands)


def mixer(me, proj, taps9, skip, filt_spec, dft, inverse):
    blocks, seqs, rows, triple = proj.shape
    chans = triple // 3
    length = blocks * rows

    def part(index):
        return pl.BlockSpec((blocks, 1, rows, chans), lambda s, m: (0, s, 0, index))

    return pl.pallas_call(
        mixer_kernel,
        grid_spec=pltpu.PrefetchScalarGridSpec(
            num_scalar_prefetch=1,
            grid=(seqs,),
            in_specs=[part(0), part(1), part(2), whole(taps9.shape), whole(skip.shape),
                      whole(filt_spec.shape), whole(dft.shape), whole(inverse.shape)],
            out_specs=[
                pl.BlockSpec((blocks, 1, rows, chans), lambda s, m: (0, s, 0, 0)),
                pl.BlockSpec((1, length, chans), lambda s, m: (s, 0, 0)),
                pl.BlockSpec((1, 2 * length, chans), lambda s, m: (s, 0, 0)),
            ],
            scratch_shapes=[
                pltpu.VMEM((3, length + 8, chans), f32),
                pltpu.VMEM((length, chans), bf16),
                pltpu.VMEM((2 * length, chans), bf16),
                pltpu.VMEM((length, chans), f32),
            ],
        ),
        out_shape=[
            jax.ShapeDtypeStruct((blocks, seqs, rows, chans), bf16),
            jax.ShapeDtypeStruct((seqs, length, chans), f32),
            jax.ShapeDtypeStruct((seqs, 2 * length, chans), f32),
        ],
        compiler_params=params(),
        name="mixer_forward",
    )(me, proj, proj, proj, taps9, skip, filt_spec, dft, inverse)


def mixer_back(me, grad_gated, proj, response, spec, taps9, skip, filt_spec, dft, inverse):
    blocks, seqs, rows, triple = proj.shape
    chans = triple // 3
    length = blocks * rows

    def part(index):
        return pl.BlockSpec((blocks, 1, rows, chans), lambda s, m: (0, s, 0, index))

    return pl.pallas_call(
        mixer_back_kernel,
        grid_spec=pltpu.PrefetchScalarGridSpec(
            num_scalar_prefetch=1,
            grid=(seqs,),
            in_specs=[part(0), part(0), part(1), part(2),
                      pl.BlockSpec((1, length, chans), lambda s, m: (s, 0, 0)),
                      pl.BlockSpec((1, 2 * length, chans), lambda s, m: (s, 0, 0)),
                      whole(taps9.shape), whole(skip.shape),
                      whole(filt_spec.shape), whole(dft.shape), whole(inverse.shape)],
            out_specs=[
                pl.BlockSpec((blocks, 1, rows, triple), lambda s, m: (0, s, 0, 0)),
                whole(taps9.shape),
                whole(skip.shape),
                whole((length, chans)),
            ],
            scratch_shapes=[
                pltpu.VMEM((3, length + 8, chans), f32),
                pltpu.VMEM((3, length + 8, chans), f32),
                pltpu.VMEM((length, chans), f32),
                pltpu.VMEM((length, chans), bf16),
                pltpu.VMEM((2 * length, chans), f32),
                pltpu.VMEM((2 * length, chans), bf16),
                pltpu.VMEM((2 * length, chans), f32),
                pltpu.VMEM((length, chans), f32),
            ],
        ),
        out_shape=[
            jax.ShapeDtypeStruct((blocks, seqs, rows, triple), bf16),
            jax.ShapeDtypeStruct(taps9.shape, f32),
            jax.ShapeDtypeStruct(skip.shape, f32),
            jax.ShapeDtypeStruct((length, chans), f32),
        ],
        compiler_params=params(),
        name="mixer_backward",
    )(me, grad_gated, proj, proj, proj, response, spec, taps9, skip, filt_spec, dft, inverse)


class Plain:
    def __init__(self, size):
        self.size = size

    def origin(self):
        return jnp.zeros((1,), jnp.int32)

    def gather(self, block):
        return [lax.all_gather(block, "mp", axis=0)]

    def scatter(self, groups):
        (partial_sums,) = groups
        return lax.psum_scatter(partial_sums.astype(bf16), "mp", scatter_dimension=0).astype(f32)


class Square:
    def __init__(self):
        self.size = 8

    def origin(self):
        return lax.axis_index("mp").astype(jnp.int32).reshape(1)

    def swap(self, block, bit):
        return lax.ppermute(block, "mp", [(i, i ^ bit) for i in range(8)])

    def gather(self, block):
        half = block.shape[0] // 2
        low, high = block[:half], block[half:]
        x_low, y_high = self.swap(low, 2), self.swap(high, 4)
        sibling = self.swap(block, 1)
        x_high, y_low = self.swap(high, 2), self.swap(low, 4)
        d_low, d_high = self.swap(x_low, 4), self.swap(y_high, 2)
        x_all = jnp.concatenate([x_low, x_high], axis=0)
        y_all = jnp.concatenate([y_low, y_high], axis=0)
        d_all = jnp.concatenate([d_low, d_high], axis=0)
        near = jnp.stack([block, sibling], axis=0)
        side = jnp.stack([x_all, self.swap(x_all, 1), y_all, self.swap(y_all, 1)], axis=0)
        far = jnp.stack([d_all, self.swap(d_all, 1)], axis=0)
        return [near, side, far]

    def scatter(self, groups):
        near, side, far = groups
        half = near.shape[1] // 2

        def both(mine, other):
            return mine.astype(f32) + self.swap(other, 1).astype(f32)

        far_sum = both(far[0], far[1])
        far_low, far_high = far_sum[:half].astype(bf16), far_sum[half:].astype(bf16)
        from_far_low, from_far_high = self.swap(far_low, 2), self.swap(far_high, 4)
        x_sum = both(side[0], side[1])
        y_sum = both(side[2], side[3])
        own_low_x = self.swap(x_sum[:half].astype(bf16), 2)
        own_high_y = self.swap(y_sum[half:].astype(bf16), 4)
        y_low = (y_sum[:half] + from_far_low.astype(f32)).astype(bf16)
        x_high = (x_sum[half:] + from_far_high.astype(f32)).astype(bf16)
        own_low_y = self.swap(y_low, 4)
        own_high_x = self.swap(x_high, 2)
        own = both(near[0], near[1])
        low = own[:half] + own_low_x.astype(f32) + own_low_y.astype(f32)
        high = own[half:] + own_high_y.astype(f32) + own_high_x.astype(f32)
        return jnp.concatenate([low, high], axis=0)


def local(
    links, tokens, lengths, norm_gain, in_proj, short_taps, conv_skip, filter_residue, filter_rate, filter_freq,
    out_proj, mlp_gain, gate_proj, up_proj, down_proj, cotangent,
):
    micro, rows, per_dev, width = tokens.shape
    seqs = micro * per_dev
    chans = in_proj.shape[2]
    hidden_units = gate_proj.shape[1]
    length = rows * links.size
    in_flat = in_proj.reshape(width, 3 * chans)
    table = dft_matrix(length)
    dft = jnp.asarray(table, bf16)
    inverse = jnp.asarray(table.T / length, bf16)
    me = links.origin()

    def by_sequence(array):
        return array.transpose(0, 2, 1, 3).reshape(seqs, rows, array.shape[3])

    def by_position(array):
        return array.reshape(micro, per_dev, rows, array.shape[2]).transpose(0, 2, 1, 3)

    def flat(array):
        return array.reshape(-1, array.shape[-1])

    def grouped(array, like):
        return array.reshape(like.shape[:-1] + (array.shape[-1],))

    positions = lax.axis_index("mp") * rows + jnp.arange(rows)
    valid = (positions[None, :] < lengths.reshape(seqs)[:, None]).astype(f32)[:, :, None]

    rows_in = by_sequence(tokens).astype(f32)
    scale_in = row_scale(rows_in)
    normed = (rows_in * scale_in * norm_gain).astype(bf16)
    normed_groups = links.gather(normed)
    grad_final = by_sequence(cotangent).astype(f32) * valid
    grad_final_all = flat(jnp.concatenate(links.gather(grad_final.astype(bf16)), axis=0))

    high = (STEP * jnp.arange(length // STEP)).astype(f32)[:, None, None]
    low = jnp.arange(STEP).astype(f32)[None, :, None]
    rate_t, freq_t, residue_t = filter_rate.T, filter_freq.T, filter_residue.T
    decay_high, turn_high = jnp.exp(-rate_t * high), freq_t * high
    decay_low, turn_low = jnp.exp(-rate_t[:, None, :] * low), freq_t[:, None, :] * low
    tables = (
        decay_high * jnp.cos(turn_high),
        decay_high * jnp.sin(turn_high),
        decay_low * jnp.cos(turn_low),
        decay_low * jnp.sin(turn_low),
    )
    filt_spec = make_filter(tables, residue_t, dft)

    proj = jnp.concatenate(
        [grouped(dot32(flat(group), in_flat), group) for group in normed_groups], axis=0
    )
    taps9 = short_taps.reshape(9, chans)
    skip = conv_skip.reshape(1, chans)
    gated, response, spec = mixer(me, proj, taps9, skip, filt_spec, dft, inverse)

    counts = [group.shape[0] for group in normed_groups]
    starts = [sum(counts[:i]) for i in range(len(counts))]

    def product_groups(left, right, dot):
        out = [None] * len(counts)
        for i in reversed(range(len(counts))):
            part = left[starts[i] : starts[i] + counts[i]]
            out[i] = grouped(dot(flat(part), right).astype(bf16), part)
        return out

    second = rows_in + links.scatter(product_groups(gated, out_proj, dot32))
    scale_second = row_scale(second)
    mlp_normed = (second * scale_second * mlp_gain).astype(bf16)
    mlp_groups = links.gather(mlp_normed)
    gate = jnp.concatenate([dot32(flat(group), gate_proj) for group in mlp_groups], axis=0)
    up = jnp.concatenate([dot32(flat(group), up_proj) for group in mlp_groups], axis=0)
    sig = jax.nn.sigmoid(gate)
    silu = gate * sig
    hidden = (silu * up).astype(bf16)

    grad_hidden = contract_cols(grad_final_all, down_proj)
    grad_gate = (grad_hidden * up * sig * (1.0 + gate * (1.0 - sig))).astype(bf16)
    grad_up = (grad_hidden * silu).astype(bf16)
    mlp_all = flat(jnp.concatenate(mlp_groups, axis=0))
    grad_down = contract_rows(hidden, grad_final_all).astype(bf16)
    grad_gate_proj = contract_rows(mlp_all, grad_gate)
    grad_up_proj = contract_rows(mlp_all, grad_up)

    chain = [None]

    def over_dp(*arrays):
        if chain[0] is not None:
            arrays = lax.optimization_barrier((arrays, chain[0]))[0]
        summed = lax.psum(arrays, "dp")
        chain[0] = summed
        return summed

    (sum_down,) = over_dp(grad_down)
    sum_gate, sum_up = over_dp(grad_gate_proj.astype(bf16), grad_up_proj.astype(bf16))

    shape4 = gated.shape[:3]
    grad_gate4 = grad_gate.reshape(shape4 + (hidden_units,))
    grad_up4 = grad_up.reshape(shape4 + (hidden_units,))
    partial_groups = []
    for start, count in zip(starts, counts):
        gate_rows = flat(grad_gate4[start : start + count])
        up_rows = flat(grad_up4[start : start + count])
        both = contract_cols(gate_rows, gate_proj) + contract_cols(up_rows, up_proj)
        partial_groups.append(both.astype(bf16).reshape((count,) + shape4[1:] + (width,)))
    grad_mlp_normed = links.scatter(partial_groups)
    grad_second = grad_final + norm_back(grad_mlp_normed, second, scale_second, mlp_gain)
    gain_two = jnp.sum(grad_mlp_normed * second * scale_second, axis=(0, 1))

    grad_branch_groups = links.gather(grad_second.astype(bf16))
    grad_gated = jnp.concatenate(
        [grouped(contract_cols(flat(group), out_proj), group) for group in grad_branch_groups], axis=0
    )
    mlp_out = links.scatter(product_groups(hidden.reshape(shape4 + (hidden_units,)), down_proj, dot32))
    layer_out = ((second + mlp_out) * valid).astype(bf16)

    grad_branch_all = flat(jnp.concatenate(grad_branch_groups, axis=0))
    grad_out = contract_rows(flat(gated), grad_branch_all)
    (sum_out,) = over_dp(grad_out.astype(bf16))
    grad_proj, grad_taps, grad_skip, grad_filt = mixer_back(
        me, grad_gated, proj, response, spec, taps9, skip, filt_spec, dft, inverse
    )
    grad_normed = links.scatter(product_groups(grad_proj, in_flat, contract_cols))
    normed_all = flat(jnp.concatenate(normed_groups, axis=0))
    grad_in = contract_rows(normed_all, flat(grad_proj))
    pole_sum, pole_re, pole_im = pole_gradients(grad_filt, tables)
    grad_tokens = grad_second + norm_back(grad_normed, rows_in, scale_in, norm_gain)
    gain_one = jnp.sum(grad_normed * rows_in * scale_in, axis=(0, 1))

    small = jnp.concatenate(
        [grad_taps, grad_skip, pole_sum, -residue_t * pole_re, -residue_t * pole_im], axis=0
    )
    sum_in, sum_small = over_dp(grad_in.astype(bf16), small.astype(bf16))
    sum_in, sum_small = sum_in.astype(f32), sum_small.astype(f32)
    gains = lax.psum((gain_one, gain_two), ("dp", "mp"))
    poles = filter_residue.shape[1]
    pole_grads = [
        sum_small[10 + poles * i : 10 + poles * (i + 1)].T for i in range(3)
    ]
    return (
        by_position(layer_out),
        by_position(grad_tokens),
        gains[0],
        sum_in.reshape(width, 3, chans),
        sum_small[:9].reshape(3, 3, chans),
        sum_small[9],
        pole_grads[0],
        pole_grads[1],
        pole_grads[2],
        sum_out.astype(f32),
        gains[1],
        sum_gate.astype(f32),
        sum_up.astype(f32),
        sum_down.astype(f32),
    )


def solution(mesh):
    links = Square() if mesh.shape["mp"] == 8 else Plain(mesh.shape["mp"])
    wide = P(None, "mp", "dp", None)
    chan = P("mp", None)
    return jax.shard_map(
        partial(local, links),
        mesh=mesh,
        in_specs=(
            wide, P(None, "dp"), P(), P(None, None, "mp"), P(None, None, "mp"), P("mp"), chan, chan, chan,
            chan, P(), P(None, "mp"), P(None, "mp"), chan, wide,
        ),
        out_specs=(
            wide, wide, P(), P(None, None, "mp"), P(None, None, "mp"), P("mp"), chan, chan, chan,
            chan, P(), P(None, "mp"), P(None, "mp"), chan,
        ),
        check_vma=False,
    )
```

```python
from functools import partial

import jax
import jax.numpy as jnp
import numpy as np
from jax import lax
from jax.experimental import pallas as pl
from jax.experimental.pallas import tpu as pltpu
from jax.sharding import PartitionSpec as P

epsilon = 1e-06
bf16 = jnp.bfloat16
f32 = jnp.float32
STEP = 32
VMEM_LIMIT = 52 * 1024 * 1024


def dft_matrix(length):
    freqs = np.arange(length)[:, None]
    times = np.arange(length)[None, :]
    angle = np.pi * (((2 * freqs + 1) * times) % (4 * length)) / (2 * length)
    return np.concatenate([np.cos(angle), -np.sin(angle)], axis=0)


def dot32(left, right):
    return jnp.dot(left, right, preferred_element_type=f32)


def contract_rows(left, right):
    return lax.dot_general(left, right, (((0,), (0,)), ((), ())), preferred_element_type=f32)


def contract_cols(left, right):
    return lax.dot_general(left, right, (((1,), (1,)), ((), ())), preferred_element_type=f32)


def row_scale(rows_in):
    return lax.rsqrt(jnp.mean(rows_in * rows_in, axis=-1, keepdims=True) + epsilon)


def norm_back(grad_y, rows_in, scale, gain):
    weighted = gain * grad_y
    inner = jnp.mean(weighted * rows_in, axis=-1, keepdims=True)
    return scale * weighted - rows_in * (scale * scale * scale) * inner


def filter_kernel(hre_ref, him_ref, lre_ref, lim_ref, res_ref, dft_ref, spec_ref, filt_ref):
    blocks, poles, chans = hre_ref.shape
    step = lre_ref.shape[1]
    residue = res_ref[...]

    def fill(block, carry):
        pre = residue * hre_ref[block]
        pim = residue * him_ref[block]
        total = jnp.zeros((step, chans), f32)
        for pole in range(poles):
            total = total + (
                pre[pole : pole + 1] * lre_ref[pole] - pim[pole : pole + 1] * lim_ref[pole]
            )
        filt_ref[pl.ds(pl.multiple_of(block * step, step), step), :] = total.astype(bf16)
        return carry

    lax.fori_loop(0, blocks, fill, 0)
    spec_ref[...] = dot32(dft_ref[...], filt_ref[...])


def pole_kernel(grad_ref, hre_ref, him_ref, lre_ref, lim_ref, sum_ref, vre_ref, vim_ref, turned):
    blocks, poles, chans = hre_ref.shape
    step = lre_ref.shape[1]
    for late in range(step):
        turned[late] = grad_ref[pl.ds(late, blocks, stride=step), :]
    starts = step * lax.broadcasted_iota(jnp.int32, (blocks, chans), 0).astype(f32)

    for pole in range(poles):
        lre, lim = lre_ref[pole], lim_ref[pole]
        part = turned[step - 1]
        sre = part * lre[step - 1 : step]
        sim = part * lim[step - 1 : step]
        tre, tim = sre, sim
        for late in range(step - 2, -1, -1):
            part = turned[late]
            sre = sre + part * lre[late : late + 1]
            sim = sim + part * lim[late : late + 1]
            if late:
                tre = tre + sre
                tim = tim + sim
        hre = hre_ref[:, pole, :]
        him = him_ref[:, pole, :]
        wre = starts * sre + tre
        wim = starts * sim + tim
        sum_ref[pole : pole + 1, :] = jnp.sum(hre * sre - him * sim, axis=0, keepdims=True)
        vre_ref[pole : pole + 1, :] = jnp.sum(hre * wre - him * wim, axis=0, keepdims=True)
        vim_ref[pole : pole + 1, :] = jnp.sum(hre * wim + him * wre, axis=0, keepdims=True)


def load_padded(parts, pad):
    for index, part in enumerate(parts):
        blocks, _, rows, chans = part.shape
        pad[index, 0:8, :] = jnp.zeros((8, chans), f32)
        for block in range(blocks):
            pad[index, 8 + block * rows : 8 + (block + 1) * rows, :] = part[block, 0]


def short_rows(pad, taps, index, start, count):
    total = taps[index : index + 1] * pad[index, 8 + start : 8 + start + count, :]
    for back in (1, 2):
        tap = taps[3 * back + index : 3 * back + index + 1]
        total = total + tap * pad[index, 8 + start - back : 8 + start - back + count, :]
    return total


def mixer_kernel(
    me_ref, q_ref, k_ref, v_ref, taps_ref, skip_ref, filt_ref, dft_ref, inv_ref,
    gated_ref, ordered_ref, resp_ref, spec_ref, pad, mixed, product, conv,
):
    me = me_ref[0]
    blocks, _, rows, chans = q_ref.shape
    length = blocks * rows
    load_padded((q_ref, k_ref, v_ref), pad)
    taps = taps_ref[...]
    skip = skip_ref[...]
    for block in range(blocks):
        start = block * rows
        key = short_rows(pad, taps, 1, start, rows)
        value = short_rows(pad, taps, 2, start, rows)
        mixed[start : start + rows, :] = (key * value).astype(bf16)
    spec_ref[0] = dot32(dft_ref[...], mixed[...])
    for block in range(blocks):
        re = slice(block * rows, (block + 1) * rows)
        im = slice(length + block * rows, length + (block + 1) * rows)
        mre, mim = spec_ref[0, re, :], spec_ref[0, im, :]
        hre, him = filt_ref[re, :], filt_ref[im, :]
        product[re, :] = (mre * hre - mim * him).astype(bf16)
        product[im, :] = (mre * him + mim * hre).astype(bf16)
    conv[...] = dot32(inv_ref[...], product[...])
    for block in range(blocks):
        start = block * rows
        response = conv[start : start + rows, :] + skip * mixed[start : start + rows, :].astype(f32)
        resp_ref[0, start : start + rows, :] = response
        query = short_rows(pad, taps, 0, start, rows)
        gated = (query * response).astype(bf16)
        gated_ref[me ^ block, 0] = gated
        ordered_ref[block, 0] = gated


def mixer_back_kernel(
    gg_ref, q_ref, k_ref, v_ref, resp_ref, spec_ref, taps_ref, skip_ref, filt_ref, dft_ref, inv_ref,
    gproj_ref, gtaps_ref, gskip_ref, gfilt_ref, pad, late, response_grad, grad_conv, spectrum, product, lags, conv,
):
    sequence = pl.program_id(0)
    blocks, _, rows, chans = q_ref.shape
    length = blocks * rows
    load_padded((q_ref, k_ref, v_ref), pad)
    taps = taps_ref[...]
    skip = skip_ref[...]

    @pl.when(sequence == 0)
    def _():
        gtaps_ref[...] = jnp.zeros_like(gtaps_ref)
        gskip_ref[...] = jnp.zeros_like(gskip_ref)
        lags[...] = jnp.zeros_like(lags)

    late[:, length : length + 8, :] = jnp.zeros((3, 8, chans), f32)
    skip_sum = jnp.zeros((1, chans), f32)
    for block in range(blocks):
        start = block * rows
        at = slice(start, start + rows)
        incoming = gg_ref[block, 0].astype(f32)
        query = short_rows(pad, taps, 0, start, rows)
        key = short_rows(pad, taps, 1, start, rows)
        value = short_rows(pad, taps, 2, start, rows)
        mixed = (key * value).astype(bf16).astype(f32)
        grad = incoming * query
        response_grad[at, :] = grad
        grad_conv[at, :] = grad.astype(bf16)
        late[0, at, :] = incoming * resp_ref[0, at, :]
        skip_sum = skip_sum + jnp.sum(grad * mixed, axis=0, keepdims=True)
    gskip_ref[...] += skip_sum

    spectrum[...] = dot32(dft_ref[...], grad_conv[...])
    for block in range(blocks):
        re = slice(block * rows, (block + 1) * rows)
        im = slice(length + block * rows, length + (block + 1) * rows)
        gre, gim = spectrum[re, :], spectrum[im, :]
        hre, him = filt_ref[re, :], filt_ref[im, :]
        mre, mim = spec_ref[0, re, :], spec_ref[0, im, :]
        product[re, :] = (gre * hre + gim * him).astype(bf16)
        product[im, :] = (gim * hre - gre * him).astype(bf16)
        lags[re, :] += gre * mre + gim * mim
        lags[im, :] += gim * mre - gre * mim
    conv[...] = dot32(inv_ref[...], product[...])

    for block in range(blocks):
        start = block * rows
        at = slice(start, start + rows)
        key = short_rows(pad, taps, 1, start, rows)
        value = short_rows(pad, taps, 2, start, rows)
        grad_mixed = conv[at, :] + skip * response_grad[at, :]
        late[1, at, :] = grad_mixed * value
        late[2, at, :] = grad_mixed * key

    sums = [jnp.zeros((1, chans), f32) for _ in range(9)]
    for block in range(blocks):
        start = block * rows
        for index in range(3):
            grad = late[index, start : start + rows, :]
            total = taps[index : index + 1] * grad
            for back in (1, 2):
                tap = taps[3 * back + index : 3 * back + index + 1]
                total = total + tap * late[index, start + back : start + back + rows, :]
            gproj_ref[index, block, 0] = total.astype(bf16)
            for back in range(3):
                shifted = pad[index, 8 + start - back : 8 + start - back + rows, :]
                sums[3 * back + index] = sums[3 * back + index] + jnp.sum(
                    grad * shifted, axis=0, keepdims=True
                )
    for index in range(9):
        gtaps_ref[index : index + 1, :] += sums[index]

    @pl.when(sequence == pl.num_programs(0) - 1)
    def _():
        product[...] = lags[...].astype(bf16)
        gfilt_ref[...] = dot32(inv_ref[...], product[...])


def whole(shape):
    return pl.BlockSpec(shape, lambda *_: (0,) * len(shape), pipeline_mode=pl.Buffered(1))


def cost(flops, nbytes):
    return pl.CostEstimate(flops=flops, bytes_accessed=nbytes, transcendentals=0)


def params():
    return pltpu.CompilerParams(vmem_limit_bytes=VMEM_LIMIT)


def make_filter(tables, residue_t, dft):
    hre, him, lre, lim = tables
    chans = residue_t.shape[1]
    length = dft.shape[1]
    operands = (hre, him, lre, lim, residue_t, dft)
    return pl.pallas_call(
        filter_kernel,
        grid=(1,),
        in_specs=[whole(op.shape) for op in operands],
        out_specs=whole((2 * length, chans)),
        out_shape=jax.ShapeDtypeStruct((2 * length, chans), f32),
        scratch_shapes=[pltpu.VMEM((length, chans), bf16)],
        compiler_params=params(),
        name="modal_filter",
    )(*operands)


def pole_gradients(grad_filt, tables):
    hre, him, lre, lim = tables
    blocks, poles, chans = hre.shape
    step = lre.shape[1]
    lanes = min(chans, 128)

    def lane_block(*lead):
        return pl.BlockSpec(lead + (lanes,), lambda c: (0,) * len(lead) + (c,))

    operands = (grad_filt, hre, him, lre, lim)
    return pl.pallas_call(
        pole_kernel,
        grid=(chans // lanes,),
        in_specs=[lane_block(*op.shape[:-1]) for op in operands],
        out_specs=[lane_block(poles)] * 3,
        out_shape=[jax.ShapeDtypeStruct((poles, chans), f32)] * 3,
        scratch_shapes=[pltpu.VMEM((step, blocks, lanes), f32)],
        compiler_params=params(),
        name="pole_gradients",
    )(*operands)


def mixer(me, proj, taps9, skip, filt_spec, dft, inverse):
    blocks, seqs, rows, triple = proj.shape
    chans = triple // 3
    length = blocks * rows
    fixed = (taps9, skip, filt_spec, dft, inverse)

    def part(index):
        return pl.BlockSpec((blocks, 1, rows, chans), lambda s, m: (0, s, 0, index))

    return pl.pallas_call(
        mixer_kernel,
        grid_spec=pltpu.PrefetchScalarGridSpec(
            num_scalar_prefetch=1,
            grid=(seqs,),
            in_specs=[part(0), part(1), part(2)] + [whole(op.shape) for op in fixed],
            out_specs=[
                part(0),
                part(0),
                pl.BlockSpec((1, length, chans), lambda s, m: (s, 0, 0)),
                pl.BlockSpec((1, 2 * length, chans), lambda s, m: (s, 0, 0)),
            ],
            scratch_shapes=[
                pltpu.VMEM((3, length + 8, chans), f32),
                pltpu.VMEM((length, chans), bf16),
                pltpu.VMEM((2 * length, chans), bf16),
                pltpu.VMEM((length, chans), f32),
            ],
        ),
        out_shape=[
            jax.ShapeDtypeStruct((blocks, seqs, rows, chans), bf16),
            jax.ShapeDtypeStruct((blocks, seqs, rows, chans), bf16),
            jax.ShapeDtypeStruct((seqs, length, chans), f32),
            jax.ShapeDtypeStruct((seqs, 2 * length, chans), f32),
        ],
        compiler_params=params(),
        cost_estimate=cost(1000, 1000),
        name="mixer_forward",
    )(me, proj, proj, proj, *fixed)


def mixer_back(grad_gated, proj, response, spec, taps9, skip, filt_spec, dft, inverse):
    blocks, seqs, rows, triple = proj.shape
    chans = triple // 3
    length = blocks * rows
    fixed = (taps9, skip, filt_spec, dft, inverse)

    def part(index):
        return pl.BlockSpec((blocks, 1, rows, chans), lambda s: (0, s, 0, index))

    return pl.pallas_call(
        mixer_back_kernel,
        grid=(seqs,),
        in_specs=[part(0), part(0), part(1), part(2)]
        + [
            pl.BlockSpec((1, length, chans), lambda s: (s, 0, 0)),
            pl.BlockSpec((1, 2 * length, chans), lambda s: (s, 0, 0)),
        ]
        + [whole(op.shape) for op in fixed],
        out_specs=[
            pl.BlockSpec((3, blocks, 1, rows, chans), lambda s: (0, 0, s, 0, 0)),
            whole(taps9.shape),
            whole(skip.shape),
            whole((length, chans)),
        ],
        scratch_shapes=[
            pltpu.VMEM((3, length + 8, chans), f32),
            pltpu.VMEM((3, length + 8, chans), f32),
            pltpu.VMEM((length, chans), f32),
            pltpu.VMEM((length, chans), bf16),
            pltpu.VMEM((2 * length, chans), f32),
            pltpu.VMEM((2 * length, chans), bf16),
            pltpu.VMEM((2 * length, chans), f32),
            pltpu.VMEM((length, chans), f32),
        ],
        out_shape=[
            jax.ShapeDtypeStruct((3, blocks, seqs, rows, chans), bf16),
            jax.ShapeDtypeStruct(taps9.shape, f32),
            jax.ShapeDtypeStruct(skip.shape, f32),
            jax.ShapeDtypeStruct((length, chans), f32),
        ],
        compiler_params=params(),
        cost_estimate=cost(1000, 1000),
        name="mixer_backward",
    )(grad_gated, proj, proj, proj, response, spec, *fixed)


def arrived(refs, counts, step, use):
    at = 0
    for index, count in enumerate(counts):
        block = refs[at : at + count]
        at += count

        @pl.when(step == index)
        def _(block=block):
            rows = [ref[...].reshape(-1, ref.shape[-1]) for ref in block]
            use(rows[0] if len(rows) == 1 else jnp.concatenate(rows, axis=0))


def project_kernel(counts, given, me_ref, *refs):
    pieces = sum(counts)
    weight_ref = refs[pieces]
    out_ref, rows_ref = refs[pieces + 1 + given :]
    chans = weight_ref.shape[2]

    def use(rows):
        rows_ref[0] = rows
        for part in range(3):
            out_ref[0, :, part * chans : (part + 1) * chans] = dot32(rows, weight_ref[part])

    arrived(refs, counts, pl.program_id(0), use)


def hidden_back_kernel(counts, given, me_ref, *refs):
    pieces = sum(counts)
    weight_ref = refs[pieces]
    out_ref, rows_ref = refs[pieces + 1 + given :]

    def use(rows):
        rows_ref[0] = rows
        out_ref[0] = contract_cols(rows, weight_ref[...])

    arrived(refs, counts, pl.program_id(0), use)


def feed_kernel(counts, given, me_ref, *refs):
    pieces = sum(counts)
    gate_w, up_w, back_ref = refs[pieces : pieces + 3]
    hidden_ref, ggate_ref, gup_ref, rows_ref = refs[pieces + 3 + given :]

    def use(rows):
        rows_ref[0] = rows
        gate = contract_cols(rows, gate_w[...])
        up = contract_cols(rows, up_w[...])
        sig = jax.nn.sigmoid(gate)
        silu = gate * sig
        hidden_ref[0] = (silu * up).astype(bf16)
        back = back_ref[0]
        ggate_ref[0] = (back * up * sig * (1.0 + gate * (1.0 - sig))).astype(bf16)
        gup_ref[0] = (back * silu).astype(bf16)

    arrived(refs, counts, pl.program_id(0), use)


def on_arrival(kernel, me, group, start, total, fixed, per_block, outputs, filled):
    pieces = [piece for block in group for piece in block]
    rows = sum(piece.shape[0] * piece.shape[1] for piece in group[0])

    def at_index(i, m):
        return (m[0] ^ (start + i), 0, 0)

    operands = [me, *pieces, *fixed, *per_block, *filled]
    first = len(operands) - len(filled)
    return pl.pallas_call(
        partial(kernel, [len(block) for block in group], len(filled)),
        grid_spec=pltpu.PrefetchScalarGridSpec(
            num_scalar_prefetch=1,
            grid=(len(group),),
            in_specs=[whole(op.shape) for op in (*pieces, *fixed)]
            + [pl.BlockSpec((1,) + op.shape[1:], at_index) for op in per_block]
            + [pl.BlockSpec(memory_space=pl.ANY)] * len(filled),
            out_specs=[pl.BlockSpec((1, rows, width), at_index) for width, _ in outputs],
        ),
        out_shape=[jax.ShapeDtypeStruct((total, rows, width), dtype) for width, dtype in outputs],
        input_output_aliases={first + i: i for i in range(len(filled))},
        compiler_params=params(),
        cost_estimate=cost(1000, 1000),
        name=kernel.__name__.removesuffix("_kernel"),
    )(*operands)


def sum_products(rights, transposed):
    def kernel(*refs):
        count = len(rights)
        dot = contract_cols if transposed else dot32
        total = dot(refs[0][0], refs[count][...])
        for left, right in zip(refs[1:count], refs[count + 1 : 2 * count]):
            total = total + dot(left[0], right[...])
        refs[2 * count][0] = total.astype(bf16)

    def call(*lefts):
        blocks, rows, depth = lefts[0].shape
        width = rights[0].shape[0 if transposed else 1]
        return pl.pallas_call(
            kernel,
            grid=(blocks,),
            in_specs=[pl.BlockSpec((1, rows, depth), lambda i: (i, 0, 0))] * len(lefts)
            + [whole(right.shape) for right in rights],
            out_specs=pl.BlockSpec((1, rows, width), lambda i: (i, 0, 0)),
            out_shape=jax.ShapeDtypeStruct((blocks, rows, width), bf16),
            compiler_params=params(),
            cost_estimate=cost(1000, 1000),
            name="sum_products",
        )(*lefts, *rights)

    return call


def gather_whole(block):
    return lax.all_gather(block, "mp", axis=0)


def scatter_whole(partial_sums):
    return lax.psum_scatter(partial_sums, "mp", scatter_dimension=0).astype(f32)


def together(*values):
    return lax.optimization_barrier(values)


def together(*values):
    return lax.optimization_barrier(values)


class WholeGather:
    def __init__(self, block):
        blocks = gather_whole(block)
        self.blocks = [(blocks[i],) for i in range(blocks.shape[0])]

    def tie(self, names, *values):
        return values

    def reach(self):
        pass

    def near(self):
        return self.blocks

    def side(self):
        return []

    def far(self):
        return []


class Plain:
    def __init__(self):
        self.parts = []

    def counts(self, size):
        return (size, 0, 0)

    def origin(self):
        return jnp.zeros((1,), jnp.int32)

    def gather(self, block):
        return WholeGather(block)

    def scatter(self, groups, given, compute):
        return scatter_whole(groups[0]), compute(given)

    def sum_mp(self, part):
        return lax.psum(part, "mp")

    def push(self, part):
        self.parts.append(part)

    def hop(self, *values):
        return values

    def sums(self):
        return [lax.psum(part, "dp") for part in self.parts]


def swap(block, bit):
    return lax.ppermute(block, "mp", [(i, i ^ bit) for i in range(8)])


class SquareGather:
    def __init__(self, block):
        cut = block.shape[0] // 2
        low, high = block[:cut], block[cut:]
        x_low, y_high = swap(low, 2), swap(high, 4)
        sibling = swap(block, 1)
        low, high, sibling = together(low, high, sibling)
        x_high, y_low = swap(high, 2), swap(low, 4)
        self.here = {"near": (block, sibling), "lead": (x_low, y_high), "rest": (x_high, y_low)}

    def tie(self, names, *values):
        held, values = together([self.here[name] for name in names], values)
        self.here.update(zip(names, held))
        return values

    def reach(self):
        x_low, y_high = self.here["lead"]
        self.here["far"] = (swap(x_low, 4), swap(y_high, 2))

    def near(self):
        return [(block,) for block in self.here["near"]]

    def side(self):
        (x_low, y_high), (x_high, y_low) = self.here["lead"], self.here["rest"]
        return self.twins((x_low, x_high)) + self.twins((y_low, y_high))

    def far(self):
        return self.twins(self.here["far"])

    def twins(self, halves):
        return [halves, tuple(swap(half, 1) for half in halves)]


class Square:
    def __init__(self):
        self.queue, self.half, self.total, self.done = [], None, None, []

    def counts(self, size):
        return (2, 4, 2)

    def origin(self):
        return lax.axis_index("mp").astype(jnp.int32).reshape(1)

    def gather(self, block):
        return SquareGather(block)

    def scatter(self, groups, given, compute):
        near, side, far = groups
        half = near.shape[1] // 2

        def both(mine, other):
            return mine.astype(f32) + swap(other, 1).astype(f32)

        far_sum = both(far[0], far[1])
        far_low, far_high = far_sum[:half].astype(bf16), far_sum[half:].astype(bf16)
        from_far_low, from_far_high = swap(far_low, 2), swap(far_high, 4)
        x_sum = both(side[0], side[1])
        y_sum = both(side[2], side[3])
        own_low_x = swap(x_sum[:half].astype(bf16), 2)
        own_high_y = swap(y_sum[half:].astype(bf16), 4)
        own = both(near[0], near[1])
        own, x_sum, y_sum, given = together(own, x_sum, y_sum, given)
        beside = compute(given)
        from_far_low, from_far_high, beside = together(from_far_low, from_far_high, beside)
        y_low = (y_sum[:half] + from_far_low.astype(f32)).astype(bf16)
        x_high = (x_sum[half:] + from_far_high.astype(f32)).astype(bf16)
        own_low_y = swap(y_low, 4)
        own_high_x = swap(x_high, 2)
        low = own[:half] + own_low_x.astype(f32) + own_low_y.astype(f32)
        high = own[half:] + own_high_y.astype(f32) + own_high_x.astype(f32)
        return jnp.concatenate([low, high], axis=0), beside

    def sum_mp(self, part):
        for bit in (1, 2, 4):
            part = part + swap(part, bit)
        return part

    def push(self, part):
        self.queue.append((part, lax.ppermute(part, "dp", [(0, 1), (3, 2)])))

    def hop(self, *values):
        part = inward = across = outward = None
        if self.queue:
            part, inward = self.queue.pop(0)
        if self.total is not None:
            outward = lax.ppermute(self.total, "dp", [(1, 0), (2, 3)])
        if self.half is not None:
            across = lax.ppermute(self.half, "dp", [(1, 2), (2, 1)])
        inward, across, outward, values = together(inward, across, outward, values)
        if outward is not None:
            place = lax.axis_index("dp")
            self.done.append(jnp.where((place == 0) | (place == 3), outward, self.total))
        self.total = None if across is None else (self.half.astype(f32) + across.astype(f32)).astype(bf16)
        self.half = None if inward is None else (part.astype(f32) + inward.astype(f32)).astype(bf16)
        return values

    def sums(self):
        while self.queue or self.half is not None or self.total is not None:
            self.hop()
        return self.done


def local(
    links, tokens, lengths, norm_gain, in_proj, short_taps, conv_skip, filter_residue, filter_rate, filter_freq,
    out_proj, mlp_gain, gate_proj, up_proj, down_proj, cotangent,
):
    micro, rows, per_dev, width = tokens.shape
    seqs = micro * per_dev
    chans = in_proj.shape[2]
    hidden_units = gate_proj.shape[1]
    length = rows * lax.axis_size("mp")
    in_parts = in_proj.transpose(1, 0, 2)
    gate_t, up_t = gate_proj.T, up_proj.T
    table = dft_matrix(length)
    dft = jnp.asarray(table, bf16)
    inverse = jnp.asarray(table.T / length, bf16)
    me = links.origin()

    def by_sequence(array):
        return array.transpose(0, 2, 1, 3).reshape(seqs, rows, array.shape[3])

    def by_position(array):
        return array.reshape(micro, per_dev, rows, array.shape[2]).transpose(0, 2, 1, 3)

    def flat(array):
        return array.reshape(-1, array.shape[-1])

    def grouped(array, like):
        return array.reshape(like.shape[:-1] + (array.shape[-1],))

    positions = lax.axis_index("mp") * rows + jnp.arange(rows)
    valid = (positions[None, :] < lengths.reshape(seqs)[:, None]).astype(f32)[:, :, None]

    rows_in = by_sequence(tokens).astype(f32)
    scale_in = row_scale(rows_in)
    normed = (rows_in * scale_in * norm_gain).astype(bf16)
    coming = links.gather(normed)

    high = (STEP * jnp.arange(length // STEP)).astype(f32)[:, None, None]
    low = jnp.arange(STEP).astype(f32)[None, :, None]
    rate_t, freq_t, residue_t = filter_rate.T, filter_freq.T, filter_residue.T
    decay_high, turn_high = jnp.exp(-rate_t * high), freq_t * high
    decay_low, turn_low = jnp.exp(-rate_t[:, None, :] * low), freq_t[:, None, :] * low
    tables = (
        decay_high * jnp.cos(turn_high),
        decay_high * jnp.sin(turn_high),
        decay_low * jnp.cos(turn_low),
        decay_low * jnp.sin(turn_low),
    )
    filt_spec = make_filter(tables, residue_t, dft)
    grad_final = by_sequence(cotangent).astype(f32) * valid
    grad_final_low = grad_final.astype(bf16)
    filt_spec, grad_final_low = coming.tie(["lead"], filt_spec, grad_final_low)
    coming.reach()

    blocks = lax.axis_size("mp")
    counts = links.counts(blocks)
    starts = [sum(counts[:i]) for i in range(len(counts))]

    def arrive(kernel, group, number, fixed, per_block, outputs, filled):
        if not group:
            return filled
        return on_arrival(kernel, me, group, starts[number], blocks, fixed, per_block, outputs, filled)

    def projected(group, number, filled):
        return arrive(project_kernel, group, number, (in_parts,), (), ((3 * chans, f32), (width, bf16)), filled)

    filled = projected(coming.near(), 0, ())
    (filled,) = coming.tie(["lead", "rest"], filled)
    filled = projected(coming.side(), 1, filled)
    filled, grad_final_low = coming.tie(["far"], filled, grad_final_low)
    grad_coming = links.gather(grad_final_low)
    proj, normed_all = projected(coming.far(), 2, filled)
    (proj,) = grad_coming.tie(["lead"], proj)
    grad_coming.reach()
    proj = proj.reshape(blocks, seqs, rows, 3 * chans)
    taps9 = short_taps.reshape(9, chans)
    skip = conv_skip.reshape(1, chans)
    gated, gated_ordered, response, spec = mixer(me, proj, taps9, skip, filt_spec, dft, inverse)
    (gated,) = grad_coming.tie(["lead", "rest"], gated)

    mixed_groups = [None] * len(counts)
    for i in reversed(range(len(counts))):
        if counts[i]:
            part = gated[starts[i] : starts[i] + counts[i]]
            mixed_groups[i] = grouped(dot32(flat(part), out_proj).astype(bf16), part)

    def hidden_backed(group, number, filled):
        return arrive(hidden_back_kernel, group, number, (down_proj,), (), ((hidden_units, f32), (width, bf16)), filled)

    def beside_scatter(held):
        near, side = held
        return hidden_backed(side, 1, hidden_backed(near, 0, ()))

    mixed_sum, filled = links.scatter(mixed_groups, (grad_coming.near(), grad_coming.side()), beside_scatter)
    second = rows_in + mixed_sum
    scale_second = row_scale(second)
    mlp_normed = (second * scale_second * mlp_gain).astype(bf16)
    coming = links.gather(mlp_normed)
    filled, mlp_normed = grad_coming.tie(["far"], filled, mlp_normed) if counts[2] else (filled, mlp_normed)
    grad_hidden, grad_final_all = hidden_backed(grad_coming.far(), 2, filled)
    (grad_hidden,) = coming.tie(["lead"], grad_hidden)
    coming.reach()

    def fed(group, number, filled):
        outputs = ((hidden_units, bf16),) * 3 + ((width, bf16),)
        return arrive(feed_kernel, group, number, (gate_t, up_t), (grad_hidden,), outputs, filled)

    filled = fed(coming.near(), 0, ())
    (filled,) = coming.tie(["lead", "rest"], filled)
    filled = fed(coming.side(), 1, filled)
    if counts[2]:
        (filled,) = coming.tie(["far"], filled)
    hidden, grad_gate, grad_up, mlp_all = fed(coming.far(), 2, filled)

    def weight_gradient(left, right, number=0, count=1):
        left, right = flat(left), flat(right)
        total = left.shape[1]
        left = left[:, number * total // count : (number + 1) * total // count]
        return contract_rows(left, right).astype(bf16)

    def blocked(array):
        return array.reshape(blocks, seqs, rows, array.shape[-1])

    down_one, hidden, grad_gate = together(weight_gradient(hidden, grad_final_all, 0, 2), hidden, grad_gate)
    links.push(down_one)
    down_two = weight_gradient(hidden, grad_final_all, 1, 2)
    mlp_back = blocked(sum_products((gate_t, up_t), False)(grad_gate, grad_up))
    mlp_back, down_two, grad_gate = links.hop(mlp_back, down_two, grad_gate)
    links.push(down_two)
    grad_mlp_normed = scatter_whole(mlp_back)
    links.push(weight_gradient(grad_gate, mlp_all, 0, 2))
    gate_two = weight_gradient(grad_gate, mlp_all, 1, 2)
    gate_two, hidden, grad_up = links.hop(gate_two, hidden, grad_up)
    links.push(gate_two)
    up_one = weight_gradient(grad_up, mlp_all, 0, 2)
    up_one, grad_up, second = links.hop(up_one, grad_up, second)
    links.push(up_one)
    grad_second = grad_final + norm_back(grad_mlp_normed, second, scale_second, mlp_gain)
    grad_branch_all = gather_whole(grad_second.astype(bf16))
    gain_two = jnp.sum(grad_mlp_normed * second * scale_second, axis=(0, 1))
    up_two = weight_gradient(grad_up, mlp_all, 1, 2)
    up_two, gain_two, hidden = links.hop(up_two, gain_two, hidden)
    links.push(up_two)
    mlp_part = blocked(dot32(flat(hidden), down_proj).astype(bf16))
    mlp_part, gated_ordered, out_here = links.hop(mlp_part, gated_ordered, out_proj)

    grad_gated = blocked(contract_cols(flat(grad_branch_all), out_here))
    links.push(weight_gradient(gated_ordered, grad_branch_all))
    grad_gated, mlp_part = links.hop(grad_gated, mlp_part)
    mlp_out = scatter_whole(mlp_part)
    grad_proj, grad_taps, grad_skip, grad_filt = mixer_back(
        grad_gated, proj, response, spec, taps9, skip, filt_spec, dft, inverse
    )
    grad_parts = [part.reshape(blocks, seqs * rows, chans) for part in grad_proj]
    grad_q = weight_gradient(normed_all, grad_parts[0])
    links.push(grad_q)
    grad_parts, gain_two = links.hop(grad_parts, gain_two)
    grad_in_rows = blocked(sum_products(tuple(in_parts), True)(*grad_parts))
    grad_k = weight_gradient(normed_all, grad_parts[1])
    links.push(grad_k)
    grad_v = weight_gradient(normed_all, grad_parts[2])
    grad_in_rows, grad_v, grad_filt, mlp_out = links.hop(grad_in_rows, grad_v, grad_filt, mlp_out)
    grad_normed = scatter_whole(grad_in_rows)

    ones = jnp.ones((8, chans), bf16)
    against = sum(
        contract_cols(ones, (grad.astype(f32) * part.astype(f32)).astype(bf16))[0]
        for grad, part in zip((grad_q, grad_k, grad_v), in_parts)
    )
    gains = links.sum_mp(jnp.stack([against / norm_gain, gain_two], axis=0))
    pole_sum, pole_re, pole_im = pole_gradients(grad_filt, tables)
    poles = filter_residue.shape[1]
    small = jnp.concatenate(
        [grad_taps, grad_skip, pole_sum, -residue_t * pole_re, -residue_t * pole_im, gains.reshape(-1, chans)], axis=0
    )
    small_rows = small.shape[0]
    small = jnp.pad(small.astype(bf16), ((0, -small_rows % 32), (0, 0)))
    links.push(jnp.concatenate([grad_v, small], axis=0))
    (mlp_out,) = links.hop(mlp_out)
    layer_out = ((second + mlp_out) * valid).astype(bf16)
    layer_out, grad_second = links.hop(layer_out, grad_second)
    grad_tokens = grad_second + norm_back(grad_normed, rows_in, scale_in, norm_gain)
    (grad_tokens,) = links.hop(by_position(grad_tokens))

    sums = links.sums()
    sum_small = sums[-1][width:].astype(f32)
    pole_grads = [sum_small[10 + poles * i : 10 + poles * (i + 1)].T for i in range(3)]
    gains = sum_small[10 + 3 * poles : small_rows].reshape(2, width)
    sum_in = jnp.stack([sums[7], sums[8], sums[9][:width]], axis=0).astype(f32)
    return (
        by_position(layer_out),
        grad_tokens,
        gains[0],
        sum_in.transpose(1, 0, 2),
        sum_small[:9].reshape(3, 3, chans),
        sum_small[9],
        pole_grads[0],
        pole_grads[1],
        pole_grads[2],
        sums[6].astype(f32),
        gains[1],
        jnp.concatenate(sums[2:4], axis=0).astype(f32).T,
        jnp.concatenate(sums[4:6], axis=0).astype(f32).T,
        jnp.concatenate(sums[:2], axis=0).astype(f32),
    )


def solution(mesh):
    square = mesh.shape["mp"] == 8 and mesh.shape["dp"] == 4
    links = Square() if square else Plain()
    wide = P(None, "mp", "dp", None)
    chan = P("mp", None)
    return jax.shard_map(
        partial(local, links),
        mesh=mesh,
        in_specs=(
            wide, P(None, "dp"), P(), P(None, None, "mp"), P(None, None, "mp"), P("mp"), chan, chan, chan,
            chan, P(), P(None, "mp"), P(None, "mp"), chan, wide,
        ),
        out_specs=(
            wide, wide, P(), P(None, None, "mp"), P(None, None, "mp"), P("mp"), chan, chan, chan,
            chan, P(), P(None, "mp"), P(None, "mp"), chan,
        ),
        check_vma=False,
    )
```

```python
import math
from functools import partial

import jax
import jax.numpy as jnp
import numpy as np
from jax import lax
from jax.experimental import pallas as pl
from jax.experimental.pallas import tpu as pltpu
from jax.sharding import PartitionSpec as P

epsilon = 1e-06
bf16 = jnp.bfloat16
f32 = jnp.float32
STEP = 32
VMEM_LIMIT = 52 * 1024 * 1024


def dft_matrix(length):
    freqs = np.arange(length)[:, None]
    times = np.arange(length)[None, :]
    angle = np.pi * (((2 * freqs + 1) * times) % (4 * length)) / (2 * length)
    return np.concatenate([np.cos(angle), -np.sin(angle)], axis=0)


def dot32(left, right):
    return jnp.dot(left, right, preferred_element_type=f32)


def contract_rows(left, right):
    return lax.dot_general(left, right, (((0,), (0,)), ((), ())), preferred_element_type=f32)


def contract_cols(left, right):
    return lax.dot_general(left, right, (((1,), (1,)), ((), ())), preferred_element_type=f32)


def row_scale(rows_in):
    return lax.rsqrt(jnp.mean(rows_in * rows_in, axis=-1, keepdims=True) + epsilon)


def norm_back(grad_y, rows_in, scale, gain):
    weighted = gain * grad_y
    inner = jnp.mean(weighted * rows_in, axis=-1, keepdims=True)
    return scale * weighted - rows_in * (scale * scale * scale) * inner


def filter_kernel(hre_ref, him_ref, lre_ref, lim_ref, res_ref, dft_ref, spec_ref, filt_ref):
    blocks, poles, chans = hre_ref.shape
    step = lre_ref.shape[1]
    residue = res_ref[...]

    def fill(block, carry):
        pre = residue * hre_ref[block]
        pim = residue * him_ref[block]
        total = jnp.zeros((step, chans), f32)
        for pole in range(poles):
            total = total + (
                pre[pole : pole + 1] * lre_ref[pole] - pim[pole : pole + 1] * lim_ref[pole]
            )
        filt_ref[pl.ds(pl.multiple_of(block * step, step), step), :] = total.astype(bf16)
        return carry

    lax.fori_loop(0, blocks, fill, 0)
    spec_ref[...] = dot32(dft_ref[...], filt_ref[...])


def pole_kernel(grad_ref, hre_ref, him_ref, lre_ref, lim_ref, sum_ref, vre_ref, vim_ref, turned):
    blocks, poles, chans = hre_ref.shape
    step = lre_ref.shape[1]
    for late in range(step):
        turned[late] = grad_ref[pl.ds(late, blocks, stride=step), :]
    starts = step * lax.broadcasted_iota(jnp.int32, (blocks, chans), 0).astype(f32)

    for pole in range(poles):
        lre, lim = lre_ref[pole], lim_ref[pole]
        part = turned[step - 1]
        sre = part * lre[step - 1 : step]
        sim = part * lim[step - 1 : step]
        tre, tim = sre, sim
        for late in range(step - 2, -1, -1):
            part = turned[late]
            sre = sre + part * lre[late : late + 1]
            sim = sim + part * lim[late : late + 1]
            if late:
                tre = tre + sre
                tim = tim + sim
        hre = hre_ref[:, pole, :]
        him = him_ref[:, pole, :]
        wre = starts * sre + tre
        wim = starts * sim + tim
        sum_ref[pole : pole + 1, :] = jnp.sum(hre * sre - him * sim, axis=0, keepdims=True)
        vre_ref[pole : pole + 1, :] = jnp.sum(hre * wre - him * wim, axis=0, keepdims=True)
        vim_ref[pole : pole + 1, :] = jnp.sum(hre * wim + him * wre, axis=0, keepdims=True)


def load_padded(parts, pad):
    for index, part in enumerate(parts):
        blocks, _, rows, chans = part.shape
        pad[index, 0:8, :] = jnp.zeros((8, chans), f32)
        for block in range(blocks):
            pad[index, 8 + block * rows : 8 + (block + 1) * rows, :] = part[block, 0]


def short_rows(pad, taps, index, start, count):
    total = taps[index : index + 1] * pad[index, 8 + start : 8 + start + count, :]
    for back in (1, 2):
        tap = taps[3 * back + index : 3 * back + index + 1]
        total = total + tap * pad[index, 8 + start - back : 8 + start - back + count, :]
    return total


def mixer_kernel(
    me_ref, q_ref, k_ref, v_ref, taps_ref, skip_ref, filt_ref, dft_ref, inv_ref,
    gated_ref, ordered_ref, resp_ref, spec_ref, pad, mixed, product, conv,
):
    me = me_ref[0]
    blocks, _, rows, chans = q_ref.shape
    length = blocks * rows
    load_padded((q_ref, k_ref, v_ref), pad)
    taps = taps_ref[...]
    skip = skip_ref[...]
    for block in range(blocks):
        start = block * rows
        key = short_rows(pad, taps, 1, start, rows)
        value = short_rows(pad, taps, 2, start, rows)
        mixed[start : start + rows, :] = (key * value).astype(bf16)
    spec_ref[0] = dot32(dft_ref[...], mixed[...])
    for block in range(blocks):
        re = slice(block * rows, (block + 1) * rows)
        im = slice(length + block * rows, length + (block + 1) * rows)
        mre, mim = spec_ref[0, re, :], spec_ref[0, im, :]
        hre, him = filt_ref[re, :], filt_ref[im, :]
        product[re, :] = (mre * hre - mim * him).astype(bf16)
        product[im, :] = (mre * him + mim * hre).astype(bf16)
    conv[...] = dot32(inv_ref[...], product[...])
    for block in range(blocks):
        start = block * rows
        response = conv[start : start + rows, :] + skip * mixed[start : start + rows, :].astype(f32)
        resp_ref[0, start : start + rows, :] = response
        query = short_rows(pad, taps, 0, start, rows)
        gated = (query * response).astype(bf16)
        gated_ref[me ^ block, 0] = gated
        ordered_ref[block, 0] = gated


def mixer_back_kernel(first, last, *refs):
    gg_ref, q_ref, k_ref, v_ref, resp_ref, spec_ref, taps_ref, skip_ref, filt_ref, dft_ref, inv_ref = refs[:11]
    refs = refs[11:]
    if not first:
        taps_before, lags_before = refs[3:5]
        refs = refs[5:]
    gq_ref, gk_ref, gv_ref, gtaps_ref, result_ref, pad, late, response_grad, grad_conv, spectrum, product, conv = refs
    blocks, _, rows, chans = q_ref.shape
    length = blocks * rows
    load_padded((q_ref, k_ref, v_ref), pad)
    taps = taps_ref[...]
    skip = skip_ref[...]

    gtaps_ref[...] = jnp.zeros_like(gtaps_ref) if first else taps_before[...]
    late[:, length : length + 8, :] = jnp.zeros((3, 8, chans), f32)
    skip_sum = jnp.zeros((1, chans), f32)
    for block in range(blocks):
        start = block * rows
        at = slice(start, start + rows)
        incoming = gg_ref[block, 0].astype(f32)
        query = short_rows(pad, taps, 0, start, rows)
        key = short_rows(pad, taps, 1, start, rows)
        value = short_rows(pad, taps, 2, start, rows)
        mixed = (key * value).astype(bf16).astype(f32)
        grad = incoming * query
        response_grad[at, :] = grad
        grad_conv[at, :] = grad.astype(bf16)
        late[0, at, :] = incoming * resp_ref[0, at, :]
        skip_sum = skip_sum + jnp.sum(grad * mixed, axis=0, keepdims=True)
    gtaps_ref[9:10, :] += skip_sum

    spectrum[...] = dot32(dft_ref[...], grad_conv[...])
    for block in range(blocks):
        re = slice(block * rows, (block + 1) * rows)
        im = slice(length + block * rows, length + (block + 1) * rows)
        gre, gim = spectrum[re, :], spectrum[im, :]
        hre, him = filt_ref[re, :], filt_ref[im, :]
        mre, mim = spec_ref[0, re, :], spec_ref[0, im, :]
        product[re, :] = (gre * hre + gim * him).astype(bf16)
        product[im, :] = (gim * hre - gre * him).astype(bf16)
        lag_re = gre * mre + gim * mim
        lag_im = gim * mre - gre * mim
        if not first:
            lag_re = lag_re + lags_before[re, :]
            lag_im = lag_im + lags_before[im, :]
        lags = spectrum if last else result_ref
        lags[re, :] = lag_re
        lags[im, :] = lag_im
    conv[...] = dot32(inv_ref[...], product[...])

    for block in range(blocks):
        start = block * rows
        at = slice(start, start + rows)
        key = short_rows(pad, taps, 1, start, rows)
        value = short_rows(pad, taps, 2, start, rows)
        grad_mixed = conv[at, :] + skip * response_grad[at, :]
        late[1, at, :] = grad_mixed * value
        late[2, at, :] = grad_mixed * key

    sums = [jnp.zeros((1, chans), f32) for _ in range(9)]
    for block in range(blocks):
        start = block * rows
        for index in range(3):
            grad = late[index, start : start + rows, :]
            total = taps[index : index + 1] * grad
            for back in (1, 2):
                tap = taps[3 * back + index : 3 * back + index + 1]
                total = total + tap * late[index, start + back : start + back + rows, :]
            (gq_ref, gk_ref, gv_ref)[index][block, 0] = total.astype(bf16)
            for back in range(3):
                shifted = pad[index, 8 + start - back : 8 + start - back + rows, :]
                sums[3 * back + index] = sums[3 * back + index] + jnp.sum(
                    grad * shifted, axis=0, keepdims=True
                )
    for index in range(9):
        gtaps_ref[index : index + 1, :] += sums[index]

    if last:
        product[...] = spectrum[...].astype(bf16)
        result_ref[...] = dot32(inv_ref[...], product[...])


def whole(shape):
    return pl.BlockSpec(shape, lambda *_: (0,) * len(shape), pipeline_mode=pl.Buffered(1))


def cost(flops, nbytes):
    return pl.CostEstimate(flops=flops, bytes_accessed=nbytes, transcendentals=0)


def params():
    return pltpu.CompilerParams(vmem_limit_bytes=VMEM_LIMIT)


def make_filter(tables, residue_t, dft):
    hre, him, lre, lim = tables
    chans = residue_t.shape[1]
    length = dft.shape[1]
    operands = (hre, him, lre, lim, residue_t, dft)
    return pl.pallas_call(
        filter_kernel,
        grid=(1,),
        in_specs=[whole(op.shape) for op in operands],
        out_specs=whole((2 * length, chans)),
        out_shape=jax.ShapeDtypeStruct((2 * length, chans), f32),
        scratch_shapes=[pltpu.VMEM((length, chans), bf16)],
        compiler_params=params(),
        name="modal_filter",
    )(*operands)


def pole_gradients(grad_filt, tables):
    hre, him, lre, lim = tables
    blocks, poles, chans = hre.shape
    step = lre.shape[1]
    lanes = min(chans, 128)

    def lane_block(*lead):
        return pl.BlockSpec(lead + (lanes,), lambda c: (0,) * len(lead) + (c,))

    operands = (grad_filt, hre, him, lre, lim)
    return pl.pallas_call(
        pole_kernel,
        grid=(chans // lanes,),
        in_specs=[lane_block(*op.shape[:-1]) for op in operands],
        out_specs=[lane_block(poles)] * 3,
        out_shape=[jax.ShapeDtypeStruct((poles, chans), f32)] * 3,
        scratch_shapes=[pltpu.VMEM((step, blocks, lanes), f32)],
        compiler_params=params(),
        name="pole_gradients",
    )(*operands)


def mixer(me, proj, taps9, skip, filt_spec, dft, inverse):
    blocks, seqs, rows, triple = proj.shape
    chans = triple // 3
    length = blocks * rows
    fixed = (taps9, skip, filt_spec, dft, inverse)

    def part(index):
        return pl.BlockSpec((blocks, 1, rows, chans), lambda s, m: (0, s, 0, index))

    return pl.pallas_call(
        mixer_kernel,
        grid_spec=pltpu.PrefetchScalarGridSpec(
            num_scalar_prefetch=1,
            grid=(seqs,),
            in_specs=[part(0), part(1), part(2)] + [whole(op.shape) for op in fixed],
            out_specs=[
                part(0),
                part(0),
                pl.BlockSpec((1, length, chans), lambda s, m: (s, 0, 0)),
                pl.BlockSpec((1, 2 * length, chans), lambda s, m: (s, 0, 0)),
            ],
            scratch_shapes=[
                pltpu.VMEM((3, length + 8, chans), f32),
                pltpu.VMEM((length, chans), bf16),
                pltpu.VMEM((2 * length, chans), bf16),
                pltpu.VMEM((length, chans), f32),
            ],
        ),
        out_shape=[
            jax.ShapeDtypeStruct((blocks, seqs, rows, chans), bf16),
            jax.ShapeDtypeStruct((blocks, seqs, rows, chans), bf16),
            jax.ShapeDtypeStruct((seqs, length, chans), f32),
            jax.ShapeDtypeStruct((seqs, 2 * length, chans), f32),
        ],
        compiler_params=params(),
        cost_estimate=cost(8 * length * length * chans * seqs, 40 * length * chans * seqs),
        name="mixer_forward",
    )(me, proj, proj, proj, *fixed)


def mixer_back(number, before, grad_gated, proj, response, spec, taps9, skip, filt_spec, dft, inverse):
    blocks, seqs, rows, triple = proj.shape
    chans = triple // 3
    length = blocks * rows
    fixed = (taps9, skip, filt_spec, dft, inverse)
    first, last = number == 0, number == seqs - 1
    result = (length, chans) if last else (2 * length, chans)

    def part(index):
        return pl.BlockSpec((blocks, 1, rows, chans), lambda i: (0, number, 0, index))

    return pl.pallas_call(
        partial(mixer_back_kernel, first, last),
        grid=(1,),
        in_specs=[part(0), part(0), part(1), part(2)]
        + [
            pl.BlockSpec((1, length, chans), lambda i: (number, 0, 0)),
            pl.BlockSpec((1, 2 * length, chans), lambda i: (number, 0, 0)),
        ]
        + [whole(op.shape) for op in fixed]
        + ([] if first else [pl.BlockSpec(memory_space=pl.ANY)] * 3 + [whole(op.shape) for op in before[3:]]),
        out_specs=[part(0), part(0), part(0), whole((16, chans)), whole(result)],
        scratch_shapes=[
            pltpu.VMEM((3, length + 8, chans), f32),
            pltpu.VMEM((3, length + 8, chans), f32),
            pltpu.VMEM((length, chans), f32),
            pltpu.VMEM((length, chans), bf16),
            pltpu.VMEM((2 * length, chans), f32),
            pltpu.VMEM((2 * length, chans), bf16),
            pltpu.VMEM((length, chans), f32),
        ],
        out_shape=[jax.ShapeDtypeStruct((blocks, seqs, rows, chans), bf16)] * 3
        + [jax.ShapeDtypeStruct((16, chans), f32), jax.ShapeDtypeStruct(result, f32)],
        input_output_aliases={} if first else {11: 0, 12: 1, 13: 2},
        compiler_params=params(),
        cost_estimate=cost(12 * length * length * chans, 80 * length * chans),
        name="mixer_backward",
    )(grad_gated, proj, proj, proj, response, spec, *fixed, *before)


def arrived(refs, counts, step, use):
    at = 0
    for index, count in enumerate(counts):
        block = refs[at : at + count]
        at += count

        @pl.when(step == index)
        def _(block=block):
            rows = [ref[...].reshape(-1, ref.shape[-1]) for ref in block]
            use(rows[0] if len(rows) == 1 else jnp.concatenate(rows, axis=0))


def project_kernel(counts, given, me_ref, *refs):
    pieces = sum(counts)
    weight_ref = refs[pieces]
    out_ref, rows_ref = refs[pieces + 1 + given :]
    chans = weight_ref.shape[2]

    def use(rows):
        rows_ref[0] = rows
        for part in range(3):
            out_ref[0, :, part * chans : (part + 1) * chans] = dot32(rows, weight_ref[part])

    arrived(refs, counts, pl.program_id(0), use)


def hidden_back_kernel(counts, given, me_ref, *refs):
    pieces = sum(counts)
    weight_ref = refs[pieces]
    out_ref, rows_ref = refs[pieces + 1 + given :]

    def use(rows):
        rows_ref[0] = rows
        out_ref[...] = contract_cols(weight_ref[...], rows)

    arrived(refs, counts, pl.program_id(0), use)


def feed_kernel(counts, given, me_ref, *refs):
    pieces = sum(counts)
    gate_w, up_w, back_ref = refs[pieces : pieces + 3]
    hidden_ref, ggate_ref, gup_ref, rows_ref = refs[pieces + 3 + given :]

    def use(rows):
        rows_ref[0] = rows
        gate = contract_cols(gate_w[...], rows)
        up = contract_cols(up_w[...], rows)
        sig = jax.nn.sigmoid(gate)
        silu = gate * sig
        hidden_ref[...] = (silu * up).astype(bf16)
        back = back_ref[...]
        ggate_ref[...] = (back * up * sig * (1.0 + gate * (1.0 - sig))).astype(bf16)
        gup_ref[...] = (back * silu).astype(bf16)

    arrived(refs, counts, pl.program_id(0), use)


def on_arrival(kernel, me, group, start, total, fixed, per_block, outputs, filled):
    pieces = [piece for block in group for piece in block]
    rows = sum(piece.shape[0] * piece.shape[1] for piece in group[0])

    def at_rows(i, m):
        return (m[0] ^ (start + i), 0, 0)

    def at_cols(i, m):
        return (0, m[0] ^ (start + i))

    def out_spec(width, dtype, turned):
        return pl.BlockSpec((width, rows), at_cols) if turned else pl.BlockSpec((1, rows, width), at_rows)

    def out_type(width, dtype, turned):
        return jax.ShapeDtypeStruct((width, total * rows) if turned else (total, rows, width), dtype)

    work = sum(2 * op.size for op in fixed)
    operands = [me, *pieces, *fixed, *per_block, *filled]
    first = len(operands) - len(filled)
    return pl.pallas_call(
        partial(kernel, [len(block) for block in group], len(filled)),
        grid_spec=pltpu.PrefetchScalarGridSpec(
            num_scalar_prefetch=1,
            grid=(len(group),),
            in_specs=[whole(op.shape) for op in (*pieces, *fixed)]
            + [pl.BlockSpec((op.shape[0], rows), at_cols) for op in per_block]
            + [pl.BlockSpec(memory_space=pl.ANY)] * len(filled),
            out_specs=[out_spec(*output) for output in outputs],
        ),
        out_shape=[out_type(*output) for output in outputs],
        input_output_aliases={first + i: i for i in range(len(filled))},
        compiler_params=params(),
        cost_estimate=cost(len(group) * rows * work, sum(op.size * 2 for op in fixed)),
        name=kernel.__name__.removesuffix("_kernel"),
    )(*operands)


def sum_products(dot, rights, dtype, turned):
    def kernel(*refs):
        count = len(rights)
        lefts = [ref[...] if turned else ref[0] for ref in refs[:count]]
        total = dot(lefts[0], refs[count][...])
        for left, right in zip(lefts[1:], refs[count + 1 : 2 * count]):
            total = total + dot(left, right[...])
        refs[2 * count][0] = total.astype(dtype)

    def call(blocks, *lefts):
        if turned:
            depth, rows = lefts[0].shape[0], lefts[0].shape[1] // blocks
            left_spec = pl.BlockSpec((depth, rows), lambda i: (0, i))
        else:
            _, rows, depth = lefts[0].shape
            left_spec = pl.BlockSpec((1, rows, depth), lambda i: (i, 0, 0))
        width = rights[0].shape[0 if dot is contract_cols else 1]
        return pl.pallas_call(
            kernel,
            grid=(blocks,),
            in_specs=[left_spec] * len(lefts) + [whole(right.shape) for right in rights],
            out_specs=pl.BlockSpec((1, rows, width), lambda i: (i, 0, 0)),
            out_shape=jax.ShapeDtypeStruct((blocks, rows, width), dtype),
            compiler_params=params(),
            cost_estimate=cost(sum(2 * left.size * width for left in lefts), 2 * blocks * rows * width),
            name="sum_products",
        )(*lefts, *rights)

    return call


def outer_kernel(left_ref, right_ref, out_ref):
    out_ref[...] = dot32(left_ref[...], right_ref[...]).astype(bf16)


def outer(left, right, number, count):
    height, depth = left.shape[0] // count, left.shape[1]
    width = right.shape[1]
    tile = math.gcd(width, 512)
    return pl.pallas_call(
        outer_kernel,
        grid=(width // tile,),
        in_specs=[
            pl.BlockSpec((height, depth), lambda j: (number, 0)),
            pl.BlockSpec((depth, tile), lambda j: (0, j)),
        ],
        out_specs=pl.BlockSpec((height, tile), lambda j: (0, j)),
        out_shape=jax.ShapeDtypeStruct((height, width), bf16),
        compiler_params=params(),
        cost_estimate=cost(2 * height * depth * width, 2 * depth * width),
        name="weight_gradient",
    )(left, right)


def gather_whole(block):
    return lax.all_gather(block, "mp", axis=0)


def scatter_whole(partial_sums):
    return lax.psum_scatter(partial_sums, "mp", scatter_dimension=0).astype(f32)


def finish_kernel(end_ref, outward_ref, total_ref, *refs):
    refs[-1][...] = jnp.where(end_ref[0] == 1, outward_ref[...].astype(f32), total_ref[...].astype(f32))


def finish(end, outward, total, start, used, height, filled):
    width = total.shape[1]
    rows = math.gcd(start, used) if start else used
    rows = rows // 2 if rows * width > 512 * 1024 and rows % 32 == 0 else rows
    piece = pl.BlockSpec((rows, width), lambda i, e: (i, 0))
    return pl.pallas_call(
        finish_kernel,
        grid_spec=pltpu.PrefetchScalarGridSpec(
            num_scalar_prefetch=1,
            grid=(used // rows,),
            in_specs=[piece, piece] + [pl.BlockSpec(memory_space=pl.ANY)] * len(filled),
            out_specs=pl.BlockSpec((rows, width), lambda i, e: (start // rows + i, 0)),
        ),
        out_shape=jax.ShapeDtypeStruct((height, width), f32),
        input_output_aliases={3: 0} if filled else {},
        compiler_params=params(),
        cost_estimate=cost(1000, 8 * used * width),
        name="finish",
    )(end, outward, total, *filled)


def add_kernel(left_ref, right_ref, out_ref):
    out_ref[...] = (left_ref[...].astype(f32) + right_ref[...].astype(f32)).astype(bf16)


def add(left, right):
    height, width = left.shape
    rows = height // 2 if height % 32 == 0 and height > 128 else height
    piece = pl.BlockSpec((rows, width), lambda i: (i, 0))
    return pl.pallas_call(
        add_kernel,
        grid=(height // rows,),
        in_specs=[piece, piece],
        out_specs=piece,
        out_shape=jax.ShapeDtypeStruct(left.shape, bf16),
        compiler_params=params(),
        cost_estimate=cost(1000, 1000),
        name="add",
    )(left, right)


def together(*values):
    return lax.optimization_barrier(values)


def together(*values):
    return lax.optimization_barrier(values)


class WholeGather:
    def __init__(self, block):
        blocks = gather_whole(block)
        self.blocks = [(blocks[i],) for i in range(blocks.shape[0])]

    def tie(self, names, *values):
        return values

    def reach(self):
        pass

    def near(self):
        return self.blocks

    def side(self):
        return []

    def far(self):
        return []


class Plain:
    def __init__(self):
        self.parts = []

    def counts(self, size):
        return (size, 0, 0)

    def origin(self):
        return jnp.zeros((1,), jnp.int32)

    def gather(self, block):
        return WholeGather(block)

    def scatter(self, array, product, coming, compute):
        return scatter_whole(product(array)), compute(coming)

    def sum_mp(self, part):
        return lax.psum(part, "mp")

    def push(self, part):
        self.parts.append(part)

    def hop_in(self, *values):
        return values

    def hop_out(self, *values, keep=0):
        return values

    def come(self, *values):
        return values

    def sums_so_far(self):
        return self.sums()

    def sums(self):
        return [lax.psum(part, "dp") for part in self.parts]

    def join(self, sums, total=None, before=None, number=0):
        joined = jnp.concatenate(([] if before is None else [before]) + [part.astype(f32) for part in sums], axis=0)
        return joined

    def plain(self, total):
        return total.astype(f32)


def swap(block, bit):
    return lax.ppermute(block, "mp", [(i, i ^ bit) for i in range(8)])


class SquareGather:
    def __init__(self, block):
        self.here = {"near": (block, swap(block, 1)), "side": (swap(block, 2), swap(block, 4))}

    def tie(self, names, *values):
        held, values = together([self.here[name] for name in names], values)
        self.here.update(zip(names, held))
        return values

    def reach(self):
        x_all, y_all = self.here["side"]
        cut = x_all.shape[0] // 2
        self.here["far"] = (swap(x_all[:cut], 4), swap(y_all[cut:], 2))

    def near(self):
        return [(block,) for block in self.here["near"]]

    def side(self):
        return [(block,) for here in self.here["side"] for block in (here, swap(here, 1))]

    def far(self):
        halves = self.here["far"]
        return [halves, tuple(swap(half, 1) for half in halves)]


class Square:
    def __init__(self):
        self.queue, self.middle, self.sent, self.done = [], [], [], []

    def counts(self, size):
        return (2, 4, 2)

    def origin(self):
        return lax.axis_index("mp").astype(jnp.int32).reshape(1)

    def gather(self, block):
        return SquareGather(block)

    def scatter(self, array, product, coming, compute):
        def both(mine, other):
            return mine.astype(f32) + swap(other, 1).astype(f32)

        far, array = together(product(array[6:8]), array)
        half = far.shape[1] // 2
        far_sum = both(far[0], far[1])
        side, near, far_sum = together(product(array[2:6]), product(array[0:2]), far_sum)
        far_low, far_high = far_sum[:half].astype(bf16), far_sum[half:].astype(bf16)
        from_far_low, from_far_high = swap(far_low, 2), swap(far_high, 4)
        x_sum = both(side[0], side[1])
        y_sum = both(side[2], side[3])
        own_low_x = swap(x_sum[:half].astype(bf16), 2)
        own_high_y = swap(y_sum[half:].astype(bf16), 4)
        own = both(near[0], near[1])
        own, x_sum, y_sum = coming.tie(["near", "side", "far"], own, x_sum, y_sum)
        beside = compute(coming)
        from_far_low, from_far_high, own_low_x, own_high_y, beside = together(
            from_far_low, from_far_high, own_low_x, own_high_y, beside
        )
        y_low = (y_sum[:half] + from_far_low.astype(f32)).astype(bf16)
        x_high = (x_sum[half:] + from_far_high.astype(f32)).astype(bf16)
        own_low_y = swap(y_low, 4)
        own_high_x = swap(x_high, 2)
        low = own[:half] + own_low_x.astype(f32) + own_low_y.astype(f32)
        high = own[half:] + own_high_y.astype(f32) + own_high_x.astype(f32)
        return jnp.concatenate([low, high], axis=0), beside

    def sum_mp(self, part):
        for bit in (1, 2, 4):
            part = part + swap(part, bit)
        return part

    def push(self, part):
        self.queue.append((part, lax.ppermute(part, "dp", [(0, 1), (3, 2)])))

    def hop_in(self, *values):
        part, inward = self.queue.pop(0)
        inward, values = together(inward, values)
        half = add(part, inward)
        self.middle.append((half, lax.ppermute(half, "dp", [(1, 2), (2, 1)])))
        return values

    def hop_out(self, *values, keep=0):
        half, across = self.middle.pop(0)
        ready = len(self.sent) - keep
        outward = [sent for _, sent in self.sent[:ready]]
        across, outward, values = together(across, outward, values)
        self.done += list(zip(outward, [total for total, _ in self.sent[:ready]]))
        total = add(half, across)
        self.sent = self.sent[ready:] + [(total, lax.ppermute(total, "dp", [(1, 0), (2, 3)]))]
        return values

    def come(self, *values):
        (total, outward), self.sent = self.sent[0], self.sent[1:]
        outward, values = together(outward, values)
        self.done.append((outward, total))
        return values

    def sums_so_far(self):
        return self.done

    def sums(self):
        return self.done + [(outward, total) for total, outward in self.sent]

    def join(self, sums, total=None, before=None, number=0):
        place = lax.axis_index("dp")
        end = ((place == 0) | (place == 3)).astype(jnp.int32).reshape(1)
        height = sums[0][1].shape[0]
        filled = () if before is None else (before,)
        for outward, part in sums:
            filled = (finish(end, outward, part, number * height, height, height * (total or len(sums)), filled),)
            number += 1
        return filled[0]

    def plain(self, pair):
        place = lax.axis_index("dp")
        outward, total = pair
        return jnp.where((place == 0) | (place == 3), outward, total).astype(f32)


def local(
    links, tokens, lengths, norm_gain, in_proj, short_taps, conv_skip, filter_residue, filter_rate, filter_freq,
    out_proj, mlp_gain, gate_proj, up_proj, down_proj, cotangent,
):
    micro, rows, per_dev, width = tokens.shape
    seqs = micro * per_dev
    chans = in_proj.shape[2]
    hidden_units = gate_proj.shape[1]
    length = rows * lax.axis_size("mp")
    in_parts = in_proj.transpose(1, 0, 2)
    gate_t, up_t = gate_proj.T, up_proj.T
    table = dft_matrix(length)
    dft = jnp.asarray(table, bf16)
    inverse = jnp.asarray(table.T / length, bf16)
    me = links.origin()

    def by_sequence(array):
        return array.transpose(0, 2, 1, 3).reshape(seqs, rows, array.shape[3])

    def by_position(array):
        return array.reshape(micro, per_dev, rows, array.shape[2]).transpose(0, 2, 1, 3)

    def flat(array):
        return array.reshape(-1, array.shape[-1])

    def grouped(array, like):
        return array.reshape(like.shape[:-1] + (array.shape[-1],))

    positions = lax.axis_index("mp") * rows + jnp.arange(rows)
    valid = (positions[None, :] < lengths.reshape(seqs)[:, None]).astype(f32)[:, :, None]

    rows_in = by_sequence(tokens).astype(f32)
    scale_in = row_scale(rows_in)
    normed = (rows_in * scale_in * norm_gain).astype(bf16)
    coming = links.gather(normed)

    high = (STEP * jnp.arange(length // STEP)).astype(f32)[:, None, None]
    low = jnp.arange(STEP).astype(f32)[None, :, None]
    rate_t, freq_t, residue_t = filter_rate.T, filter_freq.T, filter_residue.T
    decay_high, turn_high = jnp.exp(-rate_t * high), freq_t * high
    decay_low, turn_low = jnp.exp(-rate_t[:, None, :] * low), freq_t[:, None, :] * low
    tables = (
        decay_high * jnp.cos(turn_high),
        decay_high * jnp.sin(turn_high),
        decay_low * jnp.cos(turn_low),
        decay_low * jnp.sin(turn_low),
    )
    filt_spec = make_filter(tables, residue_t, dft)
    grad_final = by_sequence(cotangent).astype(f32) * valid
    grad_final_low = grad_final.astype(bf16)
    blocks = lax.axis_size("mp")
    counts = links.counts(blocks)
    starts = [sum(counts[:i]) for i in range(len(counts))]

    def arrive(kernel, group, number, fixed, per_block, outputs, filled):
        if not group:
            return filled
        return on_arrival(kernel, me, group, starts[number], blocks, fixed, per_block, outputs, filled)

    def projected(group, number, filled):
        return arrive(project_kernel, group, number, (in_parts,), (), ((3 * chans, f32, False), (width, bf16, False)), filled)

    filled = projected(coming.near(), 0, ())
    filled, filt_spec, grad_final_low = coming.tie(["side"], filled, filt_spec, grad_final_low)
    coming.reach()
    filled = projected(coming.side(), 1, filled)
    filled, grad_final_low = coming.tie(["far"], filled, grad_final_low)
    grad_coming = links.gather(grad_final_low)
    proj, normed_all = projected(coming.far(), 2, filled)
    proj = proj.reshape(blocks, seqs, rows, 3 * chans)
    taps9 = short_taps.reshape(9, chans)
    skip = conv_skip.reshape(1, chans)
    gated, gated_ordered, response, spec = mixer(me, proj, taps9, skip, filt_spec, dft, inverse)
    (gated,) = grad_coming.tie(["side"], gated)
    grad_coming.reach()

    def mixed_out(part):
        return grouped(dot32(flat(part), out_proj).astype(bf16), part)

    def hidden_backed(group, number, filled):
        return arrive(hidden_back_kernel, group, number, (down_proj,), (), ((hidden_units, f32, True), (width, bf16, False)), filled)

    def beside_scatter(grad_coming):
        return hidden_backed(grad_coming.side(), 1, hidden_backed(grad_coming.near(), 0, ()))

    mixed_sum, filled = links.scatter(gated, mixed_out, grad_coming, beside_scatter)
    second = rows_in + mixed_sum
    scale_second = row_scale(second)
    mlp_normed = (second * scale_second * mlp_gain).astype(bf16)
    coming = links.gather(mlp_normed)
    grad_hidden, grad_final_all = hidden_backed(grad_coming.far(), 2, filled)

    def fed(group, number, filled):
        outputs = ((hidden_units, bf16, True),) * 3 + ((width, bf16, False),)
        return arrive(feed_kernel, group, number, (gate_t, up_t), (grad_hidden,), outputs, filled)

    (filled,) = coming.tie(["side"], fed(coming.near(), 0, ()))
    coming.reach()
    filled = fed(coming.side(), 1, filled)
    (filled,) = coming.tie(["far"], filled)
    hidden, grad_gate, grad_up, mlp_all = fed(coming.far(), 2, filled)

    def weight_gradient(left, right):
        return contract_rows(flat(left), flat(right)).astype(bf16)

    def blocked(array):
        return array.reshape(blocks, seqs, rows, array.shape[-1])

    grad_final_all, mlp_all = flat(grad_final_all), flat(mlp_all)
    links.push(outer(hidden, grad_final_all, 0, 2))
    down_two, grad_gate, grad_up = together(outer(hidden, grad_final_all, 1, 2), grad_gate, grad_up)
    links.push(down_two)
    mlp_back = blocked(sum_products(contract_rows, (gate_t, up_t), bf16, True)(blocks, grad_gate, grad_up))
    gate_one = outer(grad_gate, mlp_all, 0, 2)
    mlp_back, gate_one, grad_gate = links.hop_in(mlp_back, gate_one, grad_gate)
    links.push(gate_one)
    grad_mlp_normed = scatter_whole(mlp_back)
    gate_two = outer(grad_gate, mlp_all, 1, 2)
    gate_two, grad_up = links.hop_in(gate_two, grad_up)
    links.push(gate_two)
    (grad_up,) = links.hop_out(grad_up)
    up_one = outer(grad_up, mlp_all, 0, 2)
    up_one, grad_up = links.hop_in(up_one, grad_up)
    links.push(up_one)
    grad_up, hidden, second = links.hop_out(grad_up, hidden, second)
    grad_second = grad_final + norm_back(grad_mlp_normed, second, scale_second, mlp_gain)
    gain_two = jnp.sum(grad_mlp_normed * second * scale_second, axis=(0, 1))
    grad_branch_all = gather_whole(grad_second.astype(bf16))
    up_two = outer(grad_up, mlp_all, 1, 2)
    up_two, gain_two, hidden = links.hop_in(up_two, gain_two, hidden)
    links.push(up_two)
    mlp_part = blocked(sum_products(contract_rows, (down_proj,), bf16, True)(blocks, hidden))
    (mlp_part,) = links.hop_out(mlp_part)
    (gated_ordered,) = links.hop_in(gated_ordered)

    grad_gated = blocked(
        sum_products(contract_cols, (out_proj,), f32, False)(blocks, grad_branch_all.reshape(blocks, -1, width))
    )
    grads_out = weight_gradient(gated_ordered, grad_branch_all)
    grads_out, grad_gated, mlp_part = links.hop_out(grads_out, grad_gated, mlp_part)
    links.push(grads_out)
    mlp_out = scatter_whole(mlp_part)
    back = ()
    for number in range(seqs - 1):
        back = mixer_back(number, back, grad_gated, proj, response, spec, taps9, skip, filt_spec, dft, inverse)
    back, grad_gated = links.hop_in(back, grad_gated)
    back, grad_gated = links.hop_out(back, grad_gated)
    *grad_parts, grad_taps, grad_filt = mixer_back(
        seqs - 1, tuple(back), grad_gated, proj, response, spec, taps9, skip, filt_spec, dft, inverse
    )
    grad_parts = [part.reshape(blocks, seqs * rows, chans) for part in grad_parts]
    grad_q = weight_gradient(normed_all, grad_parts[0])
    links.push(grad_q)
    grad_q, grad_parts, grad_filt = links.hop_in(grad_q, grad_parts, grad_filt)
    grad_parts, grad_filt = links.hop_out(grad_parts, grad_filt)
    grad_k = weight_gradient(normed_all, grad_parts[1])
    links.push(grad_k)
    grad_v = weight_gradient(normed_all, grad_parts[2])
    links.push(grad_v)
    grads_in, grad_parts, grad_filt = links.hop_in((grad_q, grad_k, grad_v), grad_parts, grad_filt)
    grad_in_rows = blocked(sum_products(contract_cols, tuple(in_parts), bf16, False)(blocks, *grad_parts))
    grad_in_rows, grads_in, grad_filt = links.hop_in(grad_in_rows, grads_in, grad_filt)
    grad_normed = scatter_whole(grad_in_rows)
    grads_in, grad_filt = links.hop_out(grads_in, grad_filt)

    ones = jnp.ones((8, chans), bf16)
    against = sum(
        contract_cols(ones, (grad.astype(f32) * part.astype(f32)).astype(bf16))[0]
        for grad, part in zip(grads_in, in_parts)
    )
    gains = jnp.stack([against / norm_gain, gain_two], axis=0)
    gains, grad_filt = links.hop_in(gains, grad_filt)
    gains, grad_filt = links.hop_out(gains, grad_filt, keep=1)
    pole_sum, pole_re, pole_im = pole_gradients(grad_filt, tables)
    gains, pole_sum = links.hop_out(links.sum_mp(gains), pole_sum, keep=1)
    poles = filter_residue.shape[1]
    small = [grad_taps, pole_sum, -residue_t * pole_re, -residue_t * pole_im, gains.reshape(-1, chans)]
    small = [jnp.pad(rows_of, ((0, -rows_of.shape[0] % 8), (0, 0))) for rows_of in small]
    bounds = np.cumsum([0] + [rows_of.shape[0] for rows_of in small])
    small = jnp.pad(jnp.concatenate(small, axis=0), ((0, -int(bounds[-1]) % 16), (0, 0))).astype(bf16)
    links.push(small)
    sum_down = links.join(links.sums_so_far()[:2])
    sum_down, grad_second = links.hop_out(sum_down, grad_second, keep=1)
    sum_gate = links.join(links.sums_so_far()[2:4])
    sum_gate, grad_second = links.hop_in(sum_gate, grad_second)
    sum_up, sum_out = links.join(links.sums_so_far()[4:6]), links.join(links.sums_so_far()[6:7])
    sum_up, sum_out, mlp_out = links.come(sum_up, sum_out, mlp_out)
    sum_in = links.join(links.sums_so_far()[7:9], 3)
    layer_out = ((second + mlp_out) * valid).astype(bf16)
    grad_tokens = by_position(grad_second + norm_back(grad_normed, rows_in, scale_in, norm_gain))
    sum_in, layer_out, grad_tokens = links.hop_out(sum_in, layer_out, grad_tokens, keep=1)

    sums = links.sums()
    sum_in = links.join(sums[9:10], 3, sum_in, 2).reshape(3, width, chans)
    sum_small = links.plain(sums[10])
    small = [sum_small[low:high] for low, high in zip(bounds[:-1], bounds[1:])]
    gains = small[4][: 2 * width // chans].reshape(2, width)
    return (
        by_position(layer_out),
        grad_tokens,
        gains[0],
        sum_in.transpose(1, 0, 2),
        small[0][:9].reshape(3, 3, chans),
        small[0][9],
        small[1][:poles].T,
        small[2][:poles].T,
        small[3][:poles].T,
        sum_out,
        gains[1],
        sum_gate.T,
        sum_up.T,
        sum_down,
    )


def solution(mesh):
    square = mesh.shape["mp"] == 8 and mesh.shape["dp"] == 4
    links = Square() if square else Plain()
    wide = P(None, "mp", "dp", None)
    chan = P("mp", None)
    return jax.shard_map(
        partial(local, links),
        mesh=mesh,
        in_specs=(
            wide, P(None, "dp"), P(), P(None, None, "mp"), P(None, None, "mp"), P("mp"), chan, chan, chan,
            chan, P(), P(None, "mp"), P(None, "mp"), chan, wide,
        ),
        out_specs=(
            wide, wide, P(), P(None, None, "mp"), P(None, None, "mp"), P("mp"), chan, chan, chan,
            chan, P(), P(None, "mp"), P(None, "mp"), chan,
        ),
        check_vma=False,
    )
```

```python
import math
from functools import partial

import jax
import jax.numpy as jnp
import numpy as np
from jax import lax
from jax.experimental import pallas as pl
from jax.experimental.pallas import tpu as pltpu
from jax.sharding import PartitionSpec as P

epsilon = 1e-06
bf16 = jnp.bfloat16
f32 = jnp.float32
STEP = 32
VMEM_LIMIT = 52 * 1024 * 1024


def dft_matrix(length):
    freqs = np.arange(length)[:, None]
    times = np.arange(length)[None, :]
    angle = np.pi * (((2 * freqs + 1) * times) % (4 * length)) / (2 * length)
    return np.concatenate([np.cos(angle), -np.sin(angle)], axis=0)


def dot32(left, right):
    return jnp.dot(left, right, preferred_element_type=f32)


def contract_rows(left, right):
    return lax.dot_general(left, right, (((0,), (0,)), ((), ())), preferred_element_type=f32)


def contract_cols(left, right):
    return lax.dot_general(left, right, (((1,), (1,)), ((), ())), preferred_element_type=f32)


def row_scale(rows_in):
    return lax.rsqrt(jnp.mean(rows_in * rows_in, axis=-1, keepdims=True) + epsilon)


def norm_back(grad_y, rows_in, scale, gain):
    weighted = gain * grad_y
    inner = jnp.mean(weighted * rows_in, axis=-1, keepdims=True)
    return scale * weighted - rows_in * (scale * scale * scale) * inner


def filter_kernel(hre_ref, him_ref, lre_ref, lim_ref, res_ref, dft_ref, spec_ref, filt_ref):
    blocks, poles, chans = hre_ref.shape
    step = lre_ref.shape[1]
    residue = res_ref[...]

    def fill(block, carry):
        pre = residue * hre_ref[block]
        pim = residue * him_ref[block]
        total = jnp.zeros((step, chans), f32)
        for pole in range(poles):
            total = total + (
                pre[pole : pole + 1] * lre_ref[pole] - pim[pole : pole + 1] * lim_ref[pole]
            )
        filt_ref[pl.ds(pl.multiple_of(block * step, step), step), :] = total.astype(bf16)
        return carry

    lax.fori_loop(0, blocks, fill, 0)
    spec_ref[...] = dot32(dft_ref[...], filt_ref[...])


def pole_kernel(grad_ref, hre_ref, him_ref, lre_ref, lim_ref, sum_ref, vre_ref, vim_ref, turned):
    blocks, poles, chans = hre_ref.shape
    step = lre_ref.shape[1]
    for late in range(step):
        turned[late] = grad_ref[pl.ds(late, blocks, stride=step), :]
    starts = step * lax.broadcasted_iota(jnp.int32, (blocks, chans), 0).astype(f32)

    for pole in range(poles):
        lre, lim = lre_ref[pole], lim_ref[pole]
        part = turned[step - 1]
        sre = part * lre[step - 1 : step]
        sim = part * lim[step - 1 : step]
        tre, tim = sre, sim
        for late in range(step - 2, -1, -1):
            part = turned[late]
            sre = sre + part * lre[late : late + 1]
            sim = sim + part * lim[late : late + 1]
            if late:
                tre = tre + sre
                tim = tim + sim
        hre = hre_ref[:, pole, :]
        him = him_ref[:, pole, :]
        wre = starts * sre + tre
        wim = starts * sim + tim
        sum_ref[pole : pole + 1, :] = jnp.sum(hre * sre - him * sim, axis=0, keepdims=True)
        vre_ref[pole : pole + 1, :] = jnp.sum(hre * wre - him * wim, axis=0, keepdims=True)
        vim_ref[pole : pole + 1, :] = jnp.sum(hre * wim + him * wre, axis=0, keepdims=True)


def load_padded(parts, pad):
    for index, part in enumerate(parts):
        blocks, _, rows, chans = part.shape
        pad[index, 0:8, :] = jnp.zeros((8, chans), f32)
        for block in range(blocks):
            pad[index, 8 + block * rows : 8 + (block + 1) * rows, :] = part[block, 0]


def short_rows(pad, taps, index, start, count):
    total = taps[index : index + 1] * pad[index, 8 + start : 8 + start + count, :]
    for back in (1, 2):
        tap = taps[3 * back + index : 3 * back + index + 1]
        total = total + tap * pad[index, 8 + start - back : 8 + start - back + count, :]
    return total


def mixer_kernel(
    me_ref, q_ref, k_ref, v_ref, taps_ref, skip_ref, filt_ref, dft_ref, inv_ref,
    gated_ref, ordered_ref, resp_ref, spec_ref, pad, mixed, product, conv,
):
    me = me_ref[0]
    blocks, _, rows, chans = q_ref.shape
    length = blocks * rows
    load_padded((q_ref, k_ref, v_ref), pad)
    taps = taps_ref[...]
    skip = skip_ref[...]
    for block in range(blocks):
        start = block * rows
        key = short_rows(pad, taps, 1, start, rows)
        value = short_rows(pad, taps, 2, start, rows)
        mixed[start : start + rows, :] = (key * value).astype(bf16)
    spec_ref[0] = dot32(dft_ref[...], mixed[...])
    for block in range(blocks):
        re = slice(block * rows, (block + 1) * rows)
        im = slice(length + block * rows, length + (block + 1) * rows)
        mre, mim = spec_ref[0, re, :], spec_ref[0, im, :]
        hre, him = filt_ref[re, :], filt_ref[im, :]
        product[re, :] = (mre * hre - mim * him).astype(bf16)
        product[im, :] = (mre * him + mim * hre).astype(bf16)
    conv[...] = dot32(inv_ref[...], product[...])
    for block in range(blocks):
        start = block * rows
        response = conv[start : start + rows, :] + skip * mixed[start : start + rows, :].astype(f32)
        resp_ref[0, start : start + rows, :] = response
        query = short_rows(pad, taps, 0, start, rows)
        gated = (query * response).astype(bf16)
        gated_ref[me ^ block, 0] = gated
        ordered_ref[block, 0] = gated


def mixer_back_kernel(first, last, *refs):
    gg_ref, q_ref, k_ref, v_ref, resp_ref, spec_ref, taps_ref, skip_ref, filt_ref, dft_ref, inv_ref = refs[:11]
    refs = refs[11:]
    if not first:
        taps_before, lags_before = refs[1:3]
        refs = refs[3:]
    gproj_ref, gtaps_ref, result_ref, pad, late, response_grad, grad_conv, spectrum, product, conv = refs
    blocks, _, rows, chans = q_ref.shape
    length = blocks * rows
    load_padded((q_ref, k_ref, v_ref), pad)
    taps = taps_ref[...]
    skip = skip_ref[...]

    gtaps_ref[...] = jnp.zeros_like(gtaps_ref) if first else taps_before[...]
    late[:, length : length + 8, :] = jnp.zeros((3, 8, chans), f32)
    skip_sum = jnp.zeros((1, chans), f32)
    for block in range(blocks):
        start = block * rows
        at = slice(start, start + rows)
        incoming = gg_ref[block, 0].astype(f32)
        query = short_rows(pad, taps, 0, start, rows)
        key = short_rows(pad, taps, 1, start, rows)
        value = short_rows(pad, taps, 2, start, rows)
        mixed = (key * value).astype(bf16).astype(f32)
        grad = incoming * query
        response_grad[at, :] = grad
        grad_conv[at, :] = grad.astype(bf16)
        late[0, at, :] = incoming * resp_ref[0, at, :]
        skip_sum = skip_sum + jnp.sum(grad * mixed, axis=0, keepdims=True)
    gtaps_ref[9:10, :] += skip_sum

    spectrum[...] = dot32(dft_ref[...], grad_conv[...])
    for block in range(blocks):
        re = slice(block * rows, (block + 1) * rows)
        im = slice(length + block * rows, length + (block + 1) * rows)
        gre, gim = spectrum[re, :], spectrum[im, :]
        hre, him = filt_ref[re, :], filt_ref[im, :]
        mre, mim = spec_ref[0, re, :], spec_ref[0, im, :]
        product[re, :] = (gre * hre + gim * him).astype(bf16)
        product[im, :] = (gim * hre - gre * him).astype(bf16)
        lag_re = gre * mre + gim * mim
        lag_im = gim * mre - gre * mim
        if not first:
            lag_re = lag_re + lags_before[re, :]
            lag_im = lag_im + lags_before[im, :]
        lags = spectrum if last else result_ref
        lags[re, :] = lag_re
        lags[im, :] = lag_im
    conv[...] = dot32(inv_ref[...], product[...])

    for block in range(blocks):
        start = block * rows
        at = slice(start, start + rows)
        key = short_rows(pad, taps, 1, start, rows)
        value = short_rows(pad, taps, 2, start, rows)
        grad_mixed = conv[at, :] + skip * response_grad[at, :]
        late[1, at, :] = grad_mixed * value
        late[2, at, :] = grad_mixed * key

    sums = [jnp.zeros((1, chans), f32) for _ in range(9)]
    for block in range(blocks):
        start = block * rows
        for index in range(3):
            grad = late[index, start : start + rows, :]
            total = taps[index : index + 1] * grad
            for back in (1, 2):
                tap = taps[3 * back + index : 3 * back + index + 1]
                total = total + tap * late[index, start + back : start + back + rows, :]
            gproj_ref[block, 0, :, index * chans : (index + 1) * chans] = total.astype(bf16)
            for back in range(3):
                shifted = pad[index, 8 + start - back : 8 + start - back + rows, :]
                sums[3 * back + index] = sums[3 * back + index] + jnp.sum(
                    grad * shifted, axis=0, keepdims=True
                )
    for index in range(9):
        gtaps_ref[index : index + 1, :] += sums[index]

    if last:
        product[...] = spectrum[...].astype(bf16)
        result_ref[...] = dot32(inv_ref[...], product[...])


def whole(shape):
    return pl.BlockSpec(shape, lambda *_: (0,) * len(shape), pipeline_mode=pl.Buffered(1))


def cost(flops, nbytes):
    return pl.CostEstimate(flops=flops, bytes_accessed=nbytes, transcendentals=0)


def params():
    return pltpu.CompilerParams(vmem_limit_bytes=VMEM_LIMIT)


def make_filter(tables, residue_t, dft):
    hre, him, lre, lim = tables
    chans = residue_t.shape[1]
    length = dft.shape[1]
    operands = (hre, him, lre, lim, residue_t, dft)
    return pl.pallas_call(
        filter_kernel,
        grid=(1,),
        in_specs=[whole(op.shape) for op in operands],
        out_specs=whole((2 * length, chans)),
        out_shape=jax.ShapeDtypeStruct((2 * length, chans), f32),
        scratch_shapes=[pltpu.VMEM((length, chans), bf16)],
        compiler_params=params(),
        name="modal_filter",
    )(*operands)


def pole_gradients(grad_filt, tables):
    hre, him, lre, lim = tables
    blocks, poles, chans = hre.shape
    step = lre.shape[1]
    lanes = min(chans, 128)

    def lane_block(*lead):
        return pl.BlockSpec(lead + (lanes,), lambda c: (0,) * len(lead) + (c,))

    operands = (grad_filt, hre, him, lre, lim)
    return pl.pallas_call(
        pole_kernel,
        grid=(chans // lanes,),
        in_specs=[lane_block(*op.shape[:-1]) for op in operands],
        out_specs=[lane_block(poles)] * 3,
        out_shape=[jax.ShapeDtypeStruct((poles, chans), f32)] * 3,
        scratch_shapes=[pltpu.VMEM((step, blocks, lanes), f32)],
        compiler_params=params(),
        name="pole_gradients",
    )(*operands)


def mixer(me, proj, taps9, skip, filt_spec, dft, inverse):
    blocks, seqs, rows, triple = proj.shape
    chans = triple // 3
    length = blocks * rows
    fixed = (taps9, skip, filt_spec, dft, inverse)

    def part(index):
        return pl.BlockSpec((blocks, 1, rows, chans), lambda s, m: (0, s, 0, index))

    return pl.pallas_call(
        mixer_kernel,
        grid_spec=pltpu.PrefetchScalarGridSpec(
            num_scalar_prefetch=1,
            grid=(seqs,),
            in_specs=[part(0), part(1), part(2)] + [whole(op.shape) for op in fixed],
            out_specs=[
                part(0),
                part(0),
                pl.BlockSpec((1, length, chans), lambda s, m: (s, 0, 0)),
                pl.BlockSpec((1, 2 * length, chans), lambda s, m: (s, 0, 0)),
            ],
            scratch_shapes=[
                pltpu.VMEM((3, length + 8, chans), f32),
                pltpu.VMEM((length, chans), bf16),
                pltpu.VMEM((2 * length, chans), bf16),
                pltpu.VMEM((length, chans), f32),
            ],
        ),
        out_shape=[
            jax.ShapeDtypeStruct((blocks, seqs, rows, chans), bf16),
            jax.ShapeDtypeStruct((blocks, seqs, rows, chans), bf16),
            jax.ShapeDtypeStruct((seqs, length, chans), f32),
            jax.ShapeDtypeStruct((seqs, 2 * length, chans), f32),
        ],
        compiler_params=params(),
        cost_estimate=cost(8 * length * length * chans * seqs, 40 * length * chans * seqs),
        name="mixer_forward",
    )(me, proj, proj, proj, *fixed)


def mixer_back(number, before, grad_gated, proj, response, spec, taps9, skip, filt_spec, dft, inverse):
    blocks, seqs, rows, triple = proj.shape
    chans = triple // 3
    length = blocks * rows
    fixed = (taps9, skip, filt_spec, dft, inverse)
    first, last = number == 0, number == seqs - 1
    result = (length, chans) if last else (2 * length, chans)

    def part(index):
        return pl.BlockSpec((blocks, 1, rows, chans), lambda i: (0, number, 0, index))

    return pl.pallas_call(
        partial(mixer_back_kernel, first, last),
        grid=(1,),
        in_specs=[part(0), part(0), part(1), part(2)]
        + [
            pl.BlockSpec((1, length, chans), lambda i: (number, 0, 0)),
            pl.BlockSpec((1, 2 * length, chans), lambda i: (number, 0, 0)),
        ]
        + [whole(op.shape) for op in fixed]
        + ([] if first else [pl.BlockSpec(memory_space=pl.ANY)] + [whole(op.shape) for op in before[1:]]),
        out_specs=[
            pl.BlockSpec((blocks, 1, rows, triple), lambda i: (0, number, 0, 0)),
            whole((16, chans)),
            whole(result),
        ],
        scratch_shapes=[
            pltpu.VMEM((3, length + 8, chans), f32),
            pltpu.VMEM((3, length + 8, chans), f32),
            pltpu.VMEM((length, chans), f32),
            pltpu.VMEM((length, chans), bf16),
            pltpu.VMEM((2 * length, chans), f32),
            pltpu.VMEM((2 * length, chans), bf16),
            pltpu.VMEM((length, chans), f32),
        ],
        out_shape=[
            jax.ShapeDtypeStruct((blocks, seqs, rows, triple), bf16),
            jax.ShapeDtypeStruct((16, chans), f32),
            jax.ShapeDtypeStruct(result, f32),
        ],
        input_output_aliases={} if first else {11: 0},
        compiler_params=params(),
        cost_estimate=cost(12 * length * length * chans, 80 * length * chans),
        name="mixer_backward",
    )(grad_gated, proj, proj, proj, response, spec, *fixed, *before)


def arrived(refs, counts, step, use):
    at = 0
    for index, count in enumerate(counts):
        block = refs[at : at + count]
        at += count

        @pl.when(step == index)
        def _(block=block):
            rows = [ref[...].reshape(-1, ref.shape[-1]) for ref in block]
            use(rows[0] if len(rows) == 1 else jnp.concatenate(rows, axis=0))


def project_kernel(counts, given, me_ref, *refs):
    pieces = sum(counts)
    weight_ref = refs[pieces]
    out_ref, rows_ref = refs[pieces + 1 + given :]
    chans = weight_ref.shape[2]

    def use(rows):
        rows_ref[0] = rows
        for part in range(3):
            out_ref[0, :, part * chans : (part + 1) * chans] = dot32(rows, weight_ref[part])

    arrived(refs, counts, pl.program_id(0), use)


def hidden_back_kernel(counts, given, me_ref, *refs):
    pieces = sum(counts)
    weight_ref = refs[pieces]
    out_ref, rows_ref = refs[pieces + 1 + given :]

    def use(rows):
        rows_ref[0] = rows
        out_ref[...] = contract_cols(weight_ref[...], rows)

    arrived(refs, counts, pl.program_id(0), use)


def feed_kernel(counts, given, me_ref, *refs):
    pieces = sum(counts)
    gate_w, up_w, back_ref = refs[pieces : pieces + 3]
    hidden_ref, ggate_ref, gup_ref, rows_ref = refs[pieces + 3 + given :]

    def use(rows):
        rows_ref[0] = rows
        gate = contract_cols(gate_w[...], rows)
        up = contract_cols(up_w[...], rows)
        sig = jax.nn.sigmoid(gate)
        silu = gate * sig
        hidden_ref[...] = (silu * up).astype(bf16)
        back = back_ref[...]
        ggate_ref[...] = (back * up * sig * (1.0 + gate * (1.0 - sig))).astype(bf16)
        gup_ref[...] = (back * silu).astype(bf16)

    arrived(refs, counts, pl.program_id(0), use)


def on_arrival(kernel, me, group, start, total, fixed, per_block, outputs, filled):
    pieces = [piece for block in group for piece in block]
    rows = sum(piece.shape[0] * piece.shape[1] for piece in group[0])

    def at_rows(i, m):
        return (m[0] ^ (start + i), 0, 0)

    def at_cols(i, m):
        return (0, m[0] ^ (start + i))

    def out_spec(width, dtype, turned):
        return pl.BlockSpec((width, rows), at_cols) if turned else pl.BlockSpec((1, rows, width), at_rows)

    def out_type(width, dtype, turned):
        return jax.ShapeDtypeStruct((width, total * rows) if turned else (total, rows, width), dtype)

    work = sum(2 * op.size for op in fixed)
    operands = [me, *pieces, *fixed, *per_block, *filled]
    first = len(operands) - len(filled)
    return pl.pallas_call(
        partial(kernel, [len(block) for block in group], len(filled)),
        grid_spec=pltpu.PrefetchScalarGridSpec(
            num_scalar_prefetch=1,
            grid=(len(group),),
            in_specs=[whole(op.shape) for op in (*pieces, *fixed)]
            + [pl.BlockSpec((op.shape[0], rows), at_cols) for op in per_block]
            + [pl.BlockSpec(memory_space=pl.ANY)] * len(filled),
            out_specs=[out_spec(*output) for output in outputs],
        ),
        out_shape=[out_type(*output) for output in outputs],
        input_output_aliases={first + i: i for i in range(len(filled))},
        compiler_params=params(),
        cost_estimate=cost(len(group) * rows * work, sum(op.size * 2 for op in fixed)),
        name=kernel.__name__.removesuffix("_kernel"),
    )(*operands)


def sum_products(dot, rights, dtype, turned):
    def kernel(*refs):
        count = len(rights)
        lefts = [ref[...] if turned else ref[0] for ref in refs[:count]]
        total = dot(lefts[0], refs[count][...])
        for left, right in zip(lefts[1:], refs[count + 1 : 2 * count]):
            total = total + dot(left, right[...])
        refs[2 * count][0] = total.astype(dtype)

    def call(blocks, *lefts):
        if turned:
            depth, rows = lefts[0].shape[0], lefts[0].shape[1] // blocks
            left_spec = pl.BlockSpec((depth, rows), lambda i: (0, i))
        else:
            _, rows, depth = lefts[0].shape
            left_spec = pl.BlockSpec((1, rows, depth), lambda i: (i, 0, 0))
        width = rights[0].shape[0 if dot is contract_cols else 1]
        return pl.pallas_call(
            kernel,
            grid=(blocks,),
            in_specs=[left_spec] * len(lefts) + [whole(right.shape) for right in rights],
            out_specs=pl.BlockSpec((1, rows, width), lambda i: (i, 0, 0)),
            out_shape=jax.ShapeDtypeStruct((blocks, rows, width), dtype),
            compiler_params=params(),
            cost_estimate=cost(sum(2 * left.size * width for left in lefts), 2 * blocks * rows * width),
            name="sum_products",
        )(*lefts, *rights)

    return call


def token_grad_kernel(grad_ref, rows_ref, second_ref, gain_ref, out_ref):
    rows_in = rows_ref[0].astype(f32)
    scale = row_scale(rows_in)
    total = second_ref[0] + norm_back(grad_ref[0].astype(f32), rows_in, scale, gain_ref[...])
    out_ref[0, :, 0, :] = total


def token_grad(grad_normed, rows_in, grad_second, gain):
    seqs, rows, width = grad_normed.shape
    part = pl.BlockSpec((1, rows, width), lambda i: (i, 0, 0))
    return pl.pallas_call(
        token_grad_kernel,
        grid=(seqs,),
        in_specs=[part, part, part, whole((1, width))],
        out_specs=pl.BlockSpec((1, rows, 1, width), lambda i: (i, 0, 0, 0)),
        out_shape=jax.ShapeDtypeStruct((seqs, rows, 1, width), f32),
        compiler_params=params(),
        cost_estimate=cost(1000, 1000),
        name="token_grad",
    )(grad_normed, rows_in, grad_second, gain.reshape(1, width))


def outer_kernel(left_ref, right_ref, out_ref):
    out_ref[...] = dot32(left_ref[...], right_ref[...]).astype(bf16)


def outer(left, right, number, count):
    height, depth = left.shape[0] // count, left.shape[1]
    width = right.shape[1]
    tile = math.gcd(width, 512)
    return pl.pallas_call(
        outer_kernel,
        grid=(width // tile,),
        in_specs=[
            pl.BlockSpec((height, depth), lambda j: (number, 0)),
            pl.BlockSpec((depth, tile), lambda j: (0, j)),
        ],
        out_specs=pl.BlockSpec((height, tile), lambda j: (0, j)),
        out_shape=jax.ShapeDtypeStruct((height, width), bf16),
        compiler_params=params(),
        cost_estimate=cost(2 * height * depth * width, 2 * depth * width),
        name="weight_gradient",
    )(left, right)


def gather_whole(block):
    return lax.all_gather(block, "mp", axis=0)


def scatter_whole(partial_sums):
    return lax.psum_scatter(partial_sums, "mp", scatter_dimension=0).astype(f32)


def finish_kernel(end_ref, *refs):
    out_ref = refs[-1]
    count = len(refs) // 2
    for number in range(count):

        @pl.when(pl.program_id(0) == number)
        def _(number=number):
            outward, total = refs[2 * number][...].astype(f32), refs[2 * number + 1][...].astype(f32)
            out_ref[...] = jnp.where(end_ref[0] == 1, outward, total)


def finish(end, pairs):
    height, width = pairs[0][1].shape
    operands = [array for pair in pairs for array in pair]
    return pl.pallas_call(
        finish_kernel,
        grid_spec=pltpu.PrefetchScalarGridSpec(
            num_scalar_prefetch=1,
            grid=(len(pairs),),
            in_specs=[whole(op.shape) for op in operands],
            out_specs=pl.BlockSpec((height, width), lambda i, e: (i, 0)),
        ),
        out_shape=jax.ShapeDtypeStruct((height * len(pairs), width), f32),
        compiler_params=params(),
        cost_estimate=cost(1000, 1000),
        name="finish",
    )(end, *operands)


def add_kernel(left_ref, right_ref, out_ref):
    out_ref[...] = (left_ref[...].astype(f32) + right_ref[...].astype(f32)).astype(bf16)


def add(left, right):
    height, width = left.shape
    rows = height // 2 if height % 32 == 0 and height > 128 else height
    piece = pl.BlockSpec((rows, width), lambda i: (i, 0))
    return pl.pallas_call(
        add_kernel,
        grid=(height // rows,),
        in_specs=[piece, piece],
        out_specs=piece,
        out_shape=jax.ShapeDtypeStruct(left.shape, bf16),
        compiler_params=params(),
        cost_estimate=cost(1000, 1000),
        name="add",
    )(left, right)


def merge_kernel(end_ref, part_ref, left_ref, right_ref, out_ref):
    total = (left_ref[...].astype(f32) + right_ref[...].astype(f32)).astype(bf16)
    out_ref[...] = jnp.where(end_ref[0] == 1, part_ref[...].astype(f32), total.astype(f32)).astype(bf16)


def merge(end, part, left, right):
    piece = pl.BlockSpec(left.shape, lambda i, e: (0, 0))
    return pl.pallas_call(
        merge_kernel,
        grid_spec=pltpu.PrefetchScalarGridSpec(
            num_scalar_prefetch=1, grid=(1,), in_specs=[piece] * 3, out_specs=piece
        ),
        out_shape=jax.ShapeDtypeStruct(left.shape, bf16),
        compiler_params=params(),
        cost_estimate=cost(1000, 1000),
        name="merge",
    )(end, part, left, right)


def together(*values):
    return lax.optimization_barrier(values)


def together(*values):
    return lax.optimization_barrier(values)


class WholeGather:
    def __init__(self, block):
        self.here = gather_whole(block)

    def tie(self, names, *values):
        return values

    def reach(self):
        pass

    def near(self):
        return [(self.here[i],) for i in range(self.here.shape[0])]

    def side(self):
        return []

    def far(self):
        return []


class Plain:
    def __init__(self):
        self.parts = []

    def counts(self, size):
        return (size, 0, 0)

    def origin(self):
        return jnp.zeros((1,), jnp.int32)

    def gather(self, block):
        return WholeGather(block)

    def scatter(self, array, product, coming):
        return scatter_whole(product(array))

    def sum_mp(self, part):
        return lax.psum(part, "mp")

    def hop(self, *values, part=None, last=False):
        if part is not None:
            self.parts.append(lax.psum(part, "dp"))
        return values

    def sums(self):
        return self.parts

    def join(self, first, last):
        return jnp.concatenate([part.astype(f32) for part in self.parts[first:last]], axis=0)

    def inward(self, part):
        return lax.psum(part, "dp")

    def across(self, part, came):
        return came, came

    def outward(self, half, came):
        return came, came

    def settled(self, total, came):
        return came.astype(f32)


def swap(block, bit):
    return lax.ppermute(block, "mp", [(i, i ^ bit) for i in range(8)])


class SquareGather:
    def __init__(self, block):
        self.here = {"near": (block, swap(block, 1)), "side": (swap(block, 2), swap(block, 4))}

    def tie(self, names, *values):
        held, values = together([self.here[name] for name in names], values)
        self.here.update(zip(names, held))
        return values

    def reach(self):
        x_all, y_all = self.here["side"]
        cut = x_all.shape[0] // 2
        self.here["far"] = (swap(x_all[:cut], 4), swap(y_all[cut:], 2))

    def near(self):
        return [(block,) for block in self.here["near"]]

    def side(self):
        return [(block,) for here in self.here["side"] for block in (here, swap(here, 1))]

    def far(self):
        halves = self.here["far"]
        return [halves, tuple(swap(half, 1) for half in halves)]


class Lane:
    def __init__(self):
        self.queue, self.flight, self.done = [], {}, []
        self.part = self.half = self.total = None

    def advance(self, end):
        flight = self.flight
        if "out" in flight:
            self.done.append((flight["out"], self.total))
        half = add(self.part, flight["in"]) if "in" in flight else None
        self.part = self.queue.pop(0) if self.queue else None
        started = {}
        if "across" in flight and self.part is not None and self.part.shape == self.half.shape:
            self.total = merge(end, self.part, self.half, flight["across"])
            started["in"] = started["out"] = lax.ppermute(self.total, "dp", [(0, 1), (3, 2), (1, 0), (2, 3)])
        else:
            if self.part is not None:
                started["in"] = lax.ppermute(self.part, "dp", [(0, 1), (3, 2)])
            if "across" in flight:
                self.total = add(self.half, flight["across"])
                started["out"] = lax.ppermute(self.total, "dp", [(1, 0), (2, 3)])
        if half is not None:
            started["across"] = lax.ppermute(half, "dp", [(1, 2), (2, 1)])
        self.half, self.flight = half, started


class Square:
    def __init__(self):
        self.lanes, self.turn = (Lane(), Lane()), 0

    def counts(self, size):
        return (2, 4, 2)

    def origin(self):
        return lax.axis_index("mp").astype(jnp.int32).reshape(1)

    def gather(self, block):
        return SquareGather(block)

    def scatter(self, array, product, coming):
        def both(mine, other):
            return mine.astype(f32) + swap(other, 1).astype(f32)

        far, array = together(product(array[6:8]), array)
        half = far.shape[1] // 2
        far_sum = both(far[0], far[1])
        far_low, far_high = far_sum[:half].astype(bf16), far_sum[half:].astype(bf16)
        side, near, far_low, far_high = together(product(array[2:6]), product(array[0:2]), far_low, far_high)
        from_far_low, from_far_high = swap(far_low, 2), swap(far_high, 4)
        x_sum = both(side[0], side[1])
        y_sum = both(side[2], side[3])
        x_sum, y_sum = coming.tie(["far"], x_sum, y_sum)
        own_low_x = swap(x_sum[:half].astype(bf16), 2)
        own_high_y = swap(y_sum[half:].astype(bf16), 4)
        own = both(near[0], near[1])
        y_low = (y_sum[:half] + from_far_low.astype(f32)).astype(bf16)
        x_high = (x_sum[half:] + from_far_high.astype(f32)).astype(bf16)
        own_low_y = swap(y_low, 4)
        own_high_x = swap(x_high, 2)
        low = own[:half] + own_low_x.astype(f32) + own_low_y.astype(f32)
        high = own[half:] + own_high_y.astype(f32) + own_high_x.astype(f32)
        return jnp.concatenate([low, high], axis=0)

    def sum_mp(self, part):
        for bit in (1, 2, 4):
            part = part + swap(part, bit)
        return part

    def end(self):
        place = lax.axis_index("dp")
        return ((place == 0) | (place == 3)).astype(jnp.int32).reshape(1)

    def hop(self, *values, part=None, last=False):
        lane = self.lanes[self.turn]
        self.turn = 1 - self.turn
        if last:
            done = [each.done for each in self.lanes]
            lane.flight, done, values = together(lane.flight, done, values)
            for each, sums in zip(self.lanes, done):
                each.done = list(sums)
        else:
            lane.flight, part, values = together(lane.flight, part, values)
        if part is not None:
            cut = part.shape[0] // 2
            for each, half in zip(self.lanes, (part[:cut], part[cut:])):
                each.queue.append(half)
        lane.advance(self.end())
        return values

    def join(self, first, last):
        return finish(self.end(), [lane.done[number] for number in range(first, last) for lane in self.lanes])


    def inward(self, part):
        return lax.ppermute(part, "dp", [(0, 1), (3, 2)])

    def across(self, part, came):
        half = add(part, came)
        return half, lax.ppermute(half, "dp", [(1, 2), (2, 1)])

    def outward(self, half, came):
        total = add(half, came)
        return total, lax.ppermute(total, "dp", [(1, 0), (2, 3)])

    def settled(self, total, came):
        return jnp.where(self.end()[0] == 1, came, total).astype(f32)


def local(
    links, tokens, lengths, norm_gain, in_proj, short_taps, conv_skip, filter_residue, filter_rate, filter_freq,
    out_proj, mlp_gain, gate_proj, up_proj, down_proj, cotangent,
):
    micro, rows, per_dev, width = tokens.shape
    seqs = micro * per_dev
    chans = in_proj.shape[2]
    hidden_units = gate_proj.shape[1]
    length = rows * lax.axis_size("mp")
    in_parts = in_proj.transpose(1, 0, 2)
    in_flat = in_proj.reshape(width, 3 * chans)
    gate_t, up_t = gate_proj.T, up_proj.T
    table = dft_matrix(length)
    dft = jnp.asarray(table, bf16)
    inverse = jnp.asarray(table.T / length, bf16)
    me = links.origin()

    def by_sequence(array):
        return array.transpose(0, 2, 1, 3).reshape(seqs, rows, array.shape[3])

    def by_position(array):
        return array.reshape(micro, per_dev, rows, array.shape[2]).transpose(0, 2, 1, 3)

    def flat(array):
        return array.reshape(-1, array.shape[-1])

    def grouped(array, like):
        return array.reshape(like.shape[:-1] + (array.shape[-1],))

    positions = lax.axis_index("mp") * rows + jnp.arange(rows)
    valid = (positions[None, :] < lengths.reshape(seqs)[:, None]).astype(f32)[:, :, None]

    rows_in = by_sequence(tokens).astype(f32)
    scale_in = row_scale(rows_in)
    normed = (rows_in * scale_in * norm_gain).astype(bf16)
    coming = links.gather(normed)

    high = (STEP * jnp.arange(length // STEP)).astype(f32)[:, None, None]
    low = jnp.arange(STEP).astype(f32)[None, :, None]
    rate_t, freq_t, residue_t = filter_rate.T, filter_freq.T, filter_residue.T
    decay_high, turn_high = jnp.exp(-rate_t * high), freq_t * high
    decay_low, turn_low = jnp.exp(-rate_t[:, None, :] * low), freq_t[:, None, :] * low
    tables = (
        decay_high * jnp.cos(turn_high),
        decay_high * jnp.sin(turn_high),
        decay_low * jnp.cos(turn_low),
        decay_low * jnp.sin(turn_low),
    )
    filt_spec = make_filter(tables, residue_t, dft)
    grad_final = by_sequence(cotangent).astype(f32) * valid
    grad_final_low = grad_final.astype(bf16)
    blocks = lax.axis_size("mp")
    counts = links.counts(blocks)
    starts = [sum(counts[:i]) for i in range(len(counts))]

    def arrive(kernel, group, number, fixed, per_block, outputs, filled):
        if not group:
            return filled
        return on_arrival(kernel, me, group, starts[number], blocks, fixed, per_block, outputs, filled)

    def projected(group, number, filled):
        return arrive(project_kernel, group, number, (in_parts,), (), ((3 * chans, f32, False), (width, bf16, False)), filled)

    filled = projected(coming.near(), 0, ())
    filled, filt_spec, grad_final_low, in_flat = coming.tie(["side"], filled, filt_spec, grad_final_low, in_flat)
    coming.reach()
    filled = projected(coming.side(), 1, filled)
    filled, grad_final_low = coming.tie(["far"], filled, grad_final_low)
    grad_coming = links.gather(grad_final_low)
    proj, normed_all = projected(coming.far(), 2, filled)
    proj = proj.reshape(blocks, seqs, rows, 3 * chans)
    taps9 = short_taps.reshape(9, chans)
    skip = conv_skip.reshape(1, chans)
    gated, gated_ordered, response, spec = mixer(me, proj, taps9, skip, filt_spec, dft, inverse)
    (gated,) = grad_coming.tie(["side"], gated)
    grad_coming.reach()

    def mixed_out(part):
        return grouped(dot32(flat(part), out_proj).astype(bf16), part)

    def hidden_backed(group, number, filled):
        return arrive(hidden_back_kernel, group, number, (down_proj,), (), ((hidden_units, f32, True), (width, bf16, False)), filled)

    second = rows_in + links.scatter(gated, mixed_out, grad_coming)
    scale_second = row_scale(second)
    mlp_normed = (second * scale_second * mlp_gain).astype(bf16)
    mlp_normed, grad_coming.here = together(mlp_normed, grad_coming.here)
    coming = links.gather(mlp_normed)
    filled = hidden_backed(grad_coming.near(), 0, ())
    filled = hidden_backed(grad_coming.side(), 1, filled)
    grad_hidden, grad_final_all = hidden_backed(grad_coming.far(), 2, filled)
    (grad_hidden,) = coming.tie(["side"], grad_hidden)

    def fed(group, number, filled):
        outputs = ((hidden_units, bf16, True),) * 3 + ((width, bf16, False),)
        return arrive(feed_kernel, group, number, (gate_t, up_t), (grad_hidden,), outputs, filled)

    coming.reach()
    filled = fed(coming.near(), 0, ())
    filled = fed(coming.side(), 1, filled)
    (filled,) = coming.tie(["far"], filled)
    hidden, grad_gate, grad_up, mlp_all = fed(coming.far(), 2, filled)

    def weight_gradient(left, right):
        return contract_rows(flat(left), flat(right)).astype(bf16)

    def blocked(array):
        return array.reshape(blocks, seqs, rows, array.shape[-1])

    grad_final_all, mlp_all = flat(grad_final_all), flat(mlp_all)
    links.hop(part=outer(hidden, grad_final_all, 0, 2))
    links.hop()
    grad_gate, grad_up, hidden = links.hop(
        grad_gate, grad_up, hidden, part=outer(hidden, grad_final_all, 1, 2)
    )
    mlp_back = blocked(sum_products(contract_rows, (gate_t, up_t), bf16, True)(blocks, grad_gate, grad_up))
    mlp_back, grad_gate = links.hop(mlp_back, grad_gate)
    grad_mlp_normed = scatter_whole(mlp_back)
    grad_gate, grad_up = links.hop(grad_gate, grad_up, part=outer(grad_gate, mlp_all, 0, 2))
    gate_two, grad_up = links.hop(outer(grad_gate, mlp_all, 1, 2), grad_up)
    up_one, grad_up = links.hop(outer(grad_up, mlp_all, 0, 2), grad_up, part=gate_two)
    up_two, second = links.hop(outer(grad_up, mlp_all, 1, 2), second)
    second, hidden = links.hop(second, hidden, part=up_one)
    grad_second = grad_final + norm_back(grad_mlp_normed, second, scale_second, mlp_gain)
    gain_two = jnp.sum(grad_mlp_normed * second * scale_second, axis=(0, 1))
    grad_branch_all = gather_whole(grad_second.astype(bf16))
    mlp_part = blocked(sum_products(contract_rows, (down_proj,), bf16, True)(blocks, hidden))
    mlp_part, gain_two = links.hop(mlp_part, gain_two)
    mlp_part, gated_ordered = links.hop(mlp_part, gated_ordered, part=up_two)
    mlp_part, gated_ordered = links.hop(mlp_part, gated_ordered)

    grad_gated = blocked(
        sum_products(contract_cols, (out_proj,), f32, False)(blocks, grad_branch_all.reshape(blocks, -1, width))
    )
    grad_out = weight_gradient(gated_ordered, grad_branch_all)
    grad_gated, mlp_part = links.hop(grad_gated, mlp_part, part=grad_out)
    mlp_out = scatter_whole(mlp_part)
    back = ()
    for number in range(seqs - 1):
        back = mixer_back(number, back, grad_gated, proj, response, spec, taps9, skip, filt_spec, dft, inverse)
    back, grad_gated = links.hop(back, grad_gated)
    grad_proj, grad_taps, grad_filt = mixer_back(
        seqs - 1, tuple(back), grad_gated, proj, response, spec, taps9, skip, filt_spec, dft, inverse
    )
    grad_in = weight_gradient(normed_all, grad_proj)
    grads_in = [grad_in[:, part * chans : (part + 1) * chans] for part in range(3)]
    grads_in, grad_proj, grad_filt = links.hop(grads_in, grad_proj, grad_filt, part=grads_in[0])
    grad_in_rows = blocked(contract_cols(flat(grad_proj), in_flat).astype(bf16).reshape(blocks, -1, width))
    grad_in_rows, grads_in = links.hop(grad_in_rows, grads_in)
    grads_in, grad_filt = links.hop(grads_in, grad_filt, part=grads_in[1])
    grad_normed = scatter_whole(grad_in_rows)

    ones = jnp.ones((8, chans), bf16)
    against = sum(
        contract_cols(ones, (grad.astype(f32) * part.astype(f32)).astype(bf16))[0]
        for grad, part in zip(grads_in, in_parts)
    )
    gains = jnp.stack([against / norm_gain, gain_two], axis=0)
    gains, grad_filt = links.hop(gains, grad_filt)
    pole_sum, pole_re, pole_im = pole_gradients(grad_filt, tables)
    gains, pole_sum = links.hop(links.sum_mp(gains), pole_sum, part=grads_in[2])
    poles = filter_residue.shape[1]
    small = [grad_taps, pole_sum, -residue_t * pole_re, -residue_t * pole_im, gains.reshape(-1, chans)]
    small = [jnp.pad(rows_of, ((0, -rows_of.shape[0] % 8), (0, 0))) for rows_of in small]
    bounds = np.cumsum([0] + [rows_of.shape[0] for rows_of in small])
    small = jnp.pad(jnp.concatenate(small, axis=0), ((0, -int(bounds[-1]) % 32), (0, 0))).astype(bf16)
    (small,) = links.hop(small)
    came = links.inward(small)
    links.hop()
    (came,) = links.hop(came)
    half, came = links.across(small, came)
    grad_second, mlp_out = links.hop(grad_second, mlp_out)
    layer_out = ((second + mlp_out) * valid).astype(bf16)
    half, came, layer_out, grad_second = links.hop(half, came, layer_out, grad_second, last=True)
    total, came = links.outward(half, came)
    if per_dev == 1:
        grad_tokens = token_grad(grad_normed, by_sequence(tokens), grad_second, norm_gain)
    else:
        grad_tokens = by_position(grad_second + norm_back(grad_normed, rows_in, scale_in, norm_gain))
    sum_down, sum_gate, sum_up, sum_out = (links.join(*at) for at in ((0, 2), (2, 4), (4, 6), (6, 7)))
    grad_tokens, total = links.hop(grad_tokens, total)
    came, sum_down, sum_gate, sum_up, sum_out = links.hop(came, sum_down, sum_gate, sum_up, sum_out)
    sum_small = links.settled(total, came)
    sum_in = links.join(7, 10).reshape(3, width, chans)
    small = [sum_small[low:high] for low, high in zip(bounds[:-1], bounds[1:])]
    gains = small[4][: 2 * width // chans].reshape(2, width)
    return (
        by_position(layer_out),
        grad_tokens,
        gains[0],
        sum_in.transpose(1, 0, 2),
        small[0][:9].reshape(3, 3, chans),
        small[0][9],
        small[1][:poles].T,
        small[2][:poles].T,
        small[3][:poles].T,
        sum_out,
        gains[1],
        sum_gate.T,
        sum_up.T,
        sum_down,
    )


def solution(mesh):
    square = mesh.shape["mp"] == 8 and mesh.shape["dp"] == 4
    links = Square() if square else Plain()
    wide = P(None, "mp", "dp", None)
    chan = P("mp", None)
    return jax.shard_map(
        partial(local, links),
        mesh=mesh,
        in_specs=(
            wide, P(None, "dp"), P(), P(None, None, "mp"), P(None, None, "mp"), P("mp"), chan, chan, chan,
            chan, P(), P(None, "mp"), P(None, "mp"), chan, wide,
        ),
        out_specs=(
            wide, wide, P(), P(None, None, "mp"), P(None, None, "mp"), P("mp"), chan, chan, chan,
            chan, P(), P(None, "mp"), P(None, "mp"), chan,
        ),
        check_vma=False,
    )
```

```python
import math
from functools import partial

import jax
import jax.numpy as jnp
import numpy as np
from jax import lax
from jax.experimental import pallas as pl
from jax.experimental.pallas import tpu as pltpu
from jax.sharding import PartitionSpec as P

epsilon = 1e-06
bf16 = jnp.bfloat16
f32 = jnp.float32
STEP = 32
VMEM_LIMIT = 52 * 1024 * 1024
SMALL_LIMIT = 30 * 1024 * 1024


def dft_matrix(length):
    freqs = np.arange(length)[:, None]
    times = np.arange(length)[None, :]
    angle = np.pi * (((2 * freqs + 1) * times) % (4 * length)) / (2 * length)
    return np.concatenate([np.cos(angle), -np.sin(angle)], axis=0)


def dot32(left, right):
    return jnp.dot(left, right, preferred_element_type=f32)


def contract_rows(left, right):
    return lax.dot_general(left, right, (((0,), (0,)), ((), ())), preferred_element_type=f32)


def contract_cols(left, right):
    return lax.dot_general(left, right, (((1,), (1,)), ((), ())), preferred_element_type=f32)


def row_scale(rows_in):
    return lax.rsqrt(jnp.mean(rows_in * rows_in, axis=-1, keepdims=True) + epsilon)


def norm_back(grad_y, rows_in, scale, gain):
    weighted = gain * grad_y
    inner = jnp.mean(weighted * rows_in, axis=-1, keepdims=True)
    return scale * weighted - rows_in * (scale * scale * scale) * inner


def filter_kernel(hre_ref, him_ref, lre_ref, lim_ref, res_ref, dft_ref, spec_ref, filt_ref):
    blocks, poles, chans = hre_ref.shape
    step = lre_ref.shape[1]
    residue = res_ref[...]

    def fill(block, carry):
        pre = residue * hre_ref[block]
        pim = residue * him_ref[block]
        total = jnp.zeros((step, chans), f32)
        for pole in range(poles):
            total = total + (
                pre[pole : pole + 1] * lre_ref[pole] - pim[pole : pole + 1] * lim_ref[pole]
            )
        filt_ref[pl.ds(pl.multiple_of(block * step, step), step), :] = total.astype(bf16)
        return carry

    lax.fori_loop(0, blocks, fill, 0)
    spec_ref[...] = dot32(dft_ref[...], filt_ref[...])


def pole_kernel(grad_ref, hre_ref, him_ref, lre_ref, lim_ref, sum_ref, vre_ref, vim_ref, turned):
    blocks, poles, chans = hre_ref.shape
    step = lre_ref.shape[1]
    for late in range(step):
        turned[late] = grad_ref[pl.ds(late, blocks, stride=step), :]
    starts = step * lax.broadcasted_iota(jnp.int32, (blocks, chans), 0).astype(f32)

    for pole in range(poles):
        lre, lim = lre_ref[pole], lim_ref[pole]
        part = turned[step - 1]
        sre = part * lre[step - 1 : step]
        sim = part * lim[step - 1 : step]
        tre, tim = sre, sim
        for late in range(step - 2, -1, -1):
            part = turned[late]
            sre = sre + part * lre[late : late + 1]
            sim = sim + part * lim[late : late + 1]
            if late:
                tre = tre + sre
                tim = tim + sim
        hre = hre_ref[:, pole, :]
        him = him_ref[:, pole, :]
        wre = starts * sre + tre
        wim = starts * sim + tim
        sum_ref[pole : pole + 1, :] = jnp.sum(hre * sre - him * sim, axis=0, keepdims=True)
        vre_ref[pole : pole + 1, :] = jnp.sum(hre * wre - him * wim, axis=0, keepdims=True)
        vim_ref[pole : pole + 1, :] = jnp.sum(hre * wim + him * wre, axis=0, keepdims=True)


def load_padded(parts, pad):
    for index, part in enumerate(parts):
        blocks, _, rows, chans = part.shape
        pad[index, 0:8, :] = jnp.zeros((8, chans), f32)
        for block in range(blocks):
            pad[index, 8 + block * rows : 8 + (block + 1) * rows, :] = part[block, 0]


def short_rows(pad, taps, index, start, count):
    total = taps[index : index + 1] * pad[index, 8 + start : 8 + start + count, :]
    for back in (1, 2):
        tap = taps[3 * back + index : 3 * back + index + 1]
        total = total + tap * pad[index, 8 + start - back : 8 + start - back + count, :]
    return total


def mixer_kernel(
    me_ref, q_ref, k_ref, v_ref, taps_ref, skip_ref, filt_ref, dft_ref, inv_ref,
    gated_ref, ordered_ref, resp_ref, spec_ref, pad, mixed, product, conv,
):
    me = me_ref[0]
    blocks, _, rows, chans = q_ref.shape
    length = blocks * rows
    load_padded((q_ref, k_ref, v_ref), pad)
    taps = taps_ref[...]
    skip = skip_ref[...]
    for block in range(blocks):
        start = block * rows
        key = short_rows(pad, taps, 1, start, rows)
        value = short_rows(pad, taps, 2, start, rows)
        mixed[start : start + rows, :] = (key * value).astype(bf16)
    spec_ref[0] = dot32(dft_ref[...], mixed[...])
    for block in range(blocks):
        re = slice(block * rows, (block + 1) * rows)
        im = slice(length + block * rows, length + (block + 1) * rows)
        mre, mim = spec_ref[0, re, :], spec_ref[0, im, :]
        hre, him = filt_ref[re, :], filt_ref[im, :]
        product[re, :] = (mre * hre - mim * him).astype(bf16)
        product[im, :] = (mre * him + mim * hre).astype(bf16)
    conv[...] = dot32(inv_ref[...], product[...])
    for block in range(blocks):
        start = block * rows
        response = conv[start : start + rows, :] + skip * mixed[start : start + rows, :].astype(f32)
        resp_ref[0, start : start + rows, :] = response
        query = short_rows(pad, taps, 0, start, rows)
        gated = (query * response).astype(bf16)
        gated_ref[me ^ block, 0] = gated
        ordered_ref[block, 0] = gated


def mixer_back_kernel(first, last, *refs):
    gg_ref, q_ref, k_ref, v_ref, resp_ref, spec_ref, taps_ref, skip_ref, filt_ref, dft_ref, inv_ref = refs[:11]
    refs = refs[11:]
    if not first:
        taps_before, lags_before = refs[1:3]
        refs = refs[3:]
    gproj_ref, gtaps_ref, result_ref, pad, late, response_grad, grad_conv, spectrum, product, conv = refs
    blocks, _, rows, chans = q_ref.shape
    length = blocks * rows
    load_padded((q_ref, k_ref, v_ref), pad)
    taps = taps_ref[...]
    skip = skip_ref[...]

    gtaps_ref[...] = jnp.zeros_like(gtaps_ref) if first else taps_before[...]
    late[:, length : length + 8, :] = jnp.zeros((3, 8, chans), f32)
    skip_sum = jnp.zeros((1, chans), f32)
    for block in range(blocks):
        start = block * rows
        at = slice(start, start + rows)
        incoming = gg_ref[block, 0].astype(f32)
        query = short_rows(pad, taps, 0, start, rows)
        key = short_rows(pad, taps, 1, start, rows)
        value = short_rows(pad, taps, 2, start, rows)
        mixed = (key * value).astype(bf16).astype(f32)
        grad = incoming * query
        response_grad[at, :] = grad
        grad_conv[at, :] = grad.astype(bf16)
        late[0, at, :] = incoming * resp_ref[0, at, :]
        skip_sum = skip_sum + jnp.sum(grad * mixed, axis=0, keepdims=True)
    gtaps_ref[9:10, :] += skip_sum

    spectrum[...] = dot32(dft_ref[...], grad_conv[...])
    for block in range(blocks):
        re = slice(block * rows, (block + 1) * rows)
        im = slice(length + block * rows, length + (block + 1) * rows)
        gre, gim = spectrum[re, :], spectrum[im, :]
        hre, him = filt_ref[re, :], filt_ref[im, :]
        mre, mim = spec_ref[0, re, :], spec_ref[0, im, :]
        product[re, :] = (gre * hre + gim * him).astype(bf16)
        product[im, :] = (gim * hre - gre * him).astype(bf16)
        lag_re = gre * mre + gim * mim
        lag_im = gim * mre - gre * mim
        if not first:
            lag_re = lag_re + lags_before[re, :]
            lag_im = lag_im + lags_before[im, :]
        lags = spectrum if last else result_ref
        lags[re, :] = lag_re
        lags[im, :] = lag_im
    conv[...] = dot32(inv_ref[...], product[...])

    for block in range(blocks):
        start = block * rows
        at = slice(start, start + rows)
        key = short_rows(pad, taps, 1, start, rows)
        value = short_rows(pad, taps, 2, start, rows)
        grad_mixed = conv[at, :] + skip * response_grad[at, :]
        late[1, at, :] = grad_mixed * value
        late[2, at, :] = grad_mixed * key

    sums = [jnp.zeros((1, chans), f32) for _ in range(9)]
    for block in range(blocks):
        start = block * rows
        for index in range(3):
            grad = late[index, start : start + rows, :]
            total = taps[index : index + 1] * grad
            for back in (1, 2):
                tap = taps[3 * back + index : 3 * back + index + 1]
                total = total + tap * late[index, start + back : start + back + rows, :]
            gproj_ref[block, 0, :, index * chans : (index + 1) * chans] = total.astype(bf16)
            for back in range(3):
                shifted = pad[index, 8 + start - back : 8 + start - back + rows, :]
                sums[3 * back + index] = sums[3 * back + index] + jnp.sum(
                    grad * shifted, axis=0, keepdims=True
                )
    for index in range(9):
        gtaps_ref[index : index + 1, :] += sums[index]

    if last:
        product[...] = spectrum[...].astype(bf16)
        result_ref[...] = dot32(inv_ref[...], product[...])


def whole(shape):
    return pl.BlockSpec(shape, lambda *_: (0,) * len(shape), pipeline_mode=pl.Buffered(1))


def cost(flops, nbytes):
    return pl.CostEstimate(flops=flops, bytes_accessed=nbytes, transcendentals=0)


def params(limit=VMEM_LIMIT):
    return pltpu.CompilerParams(vmem_limit_bytes=limit)


def make_filter(tables, residue_t, dft):
    hre, him, lre, lim = tables
    chans = residue_t.shape[1]
    length = dft.shape[1]
    operands = (hre, him, lre, lim, residue_t, dft)
    return pl.pallas_call(
        filter_kernel,
        grid=(1,),
        in_specs=[whole(op.shape) for op in operands],
        out_specs=whole((2 * length, chans)),
        out_shape=jax.ShapeDtypeStruct((2 * length, chans), f32),
        scratch_shapes=[pltpu.VMEM((length, chans), bf16)],
        compiler_params=params(),
        name="modal_filter",
    )(*operands)


def pole_gradients(grad_filt, tables):
    hre, him, lre, lim = tables
    blocks, poles, chans = hre.shape
    step = lre.shape[1]
    lanes = min(chans, 128)

    def lane_block(*lead):
        return pl.BlockSpec(lead + (lanes,), lambda c: (0,) * len(lead) + (c,))

    operands = (grad_filt, hre, him, lre, lim)
    return pl.pallas_call(
        pole_kernel,
        grid=(chans // lanes,),
        in_specs=[lane_block(*op.shape[:-1]) for op in operands],
        out_specs=[lane_block(poles)] * 3,
        out_shape=[jax.ShapeDtypeStruct((poles, chans), f32)] * 3,
        scratch_shapes=[pltpu.VMEM((step, blocks, lanes), f32)],
        compiler_params=params(),
        name="pole_gradients",
    )(*operands)


def mixer(me, proj, taps9, skip, filt_spec, dft, inverse):
    blocks, seqs, rows, triple = proj.shape
    chans = triple // 3
    length = blocks * rows
    fixed = (taps9, skip, filt_spec, dft, inverse)

    def part(index):
        return pl.BlockSpec((blocks, 1, rows, chans), lambda s, m: (0, s, 0, index))

    return pl.pallas_call(
        mixer_kernel,
        grid_spec=pltpu.PrefetchScalarGridSpec(
            num_scalar_prefetch=1,
            grid=(seqs,),
            in_specs=[part(0), part(1), part(2)] + [whole(op.shape) for op in fixed],
            out_specs=[
                part(0),
                part(0),
                pl.BlockSpec((1, length, chans), lambda s, m: (s, 0, 0)),
                pl.BlockSpec((1, 2 * length, chans), lambda s, m: (s, 0, 0)),
            ],
            scratch_shapes=[
                pltpu.VMEM((3, length + 8, chans), f32),
                pltpu.VMEM((length, chans), bf16),
                pltpu.VMEM((2 * length, chans), bf16),
                pltpu.VMEM((length, chans), f32),
            ],
        ),
        out_shape=[
            jax.ShapeDtypeStruct((blocks, seqs, rows, chans), bf16),
            jax.ShapeDtypeStruct((blocks, seqs, rows, chans), bf16),
            jax.ShapeDtypeStruct((seqs, length, chans), f32),
            jax.ShapeDtypeStruct((seqs, 2 * length, chans), f32),
        ],
        compiler_params=params(),
        cost_estimate=cost(8 * length * length * chans * seqs, 40 * length * chans * seqs),
        name="mixer_forward",
    )(me, proj, proj, proj, *fixed)


def mixer_back(number, before, grad_gated, proj, response, spec, taps9, skip, filt_spec, dft, inverse):
    blocks, seqs, rows, triple = proj.shape
    chans = triple // 3
    length = blocks * rows
    fixed = (taps9, skip, filt_spec, dft, inverse)
    first, last = number == 0, number == seqs - 1
    result = (length, chans) if last else (2 * length, chans)

    def part(index):
        return pl.BlockSpec((blocks, 1, rows, chans), lambda i: (0, number, 0, index))

    return pl.pallas_call(
        partial(mixer_back_kernel, first, last),
        grid=(1,),
        in_specs=[part(0), part(0), part(1), part(2)]
        + [
            pl.BlockSpec((1, length, chans), lambda i: (number, 0, 0)),
            pl.BlockSpec((1, 2 * length, chans), lambda i: (number, 0, 0)),
        ]
        + [whole(op.shape) for op in fixed]
        + ([] if first else [pl.BlockSpec(memory_space=pl.ANY)] + [whole(op.shape) for op in before[1:]]),
        out_specs=[
            pl.BlockSpec((blocks, 1, rows, triple), lambda i: (0, number, 0, 0)),
            whole((16, chans)),
            whole(result),
        ],
        scratch_shapes=[
            pltpu.VMEM((3, length + 8, chans), f32),
            pltpu.VMEM((3, length + 8, chans), f32),
            pltpu.VMEM((length, chans), f32),
            pltpu.VMEM((length, chans), bf16),
            pltpu.VMEM((2 * length, chans), f32),
            pltpu.VMEM((2 * length, chans), bf16),
            pltpu.VMEM((length, chans), f32),
        ],
        out_shape=[
            jax.ShapeDtypeStruct((blocks, seqs, rows, triple), bf16),
            jax.ShapeDtypeStruct((16, chans), f32),
            jax.ShapeDtypeStruct(result, f32),
        ],
        input_output_aliases={} if first else {11: 0},
        compiler_params=params(),
        cost_estimate=cost(12 * length * length * chans, 80 * length * chans),
        name="mixer_backward",
    )(grad_gated, proj, proj, proj, response, spec, *fixed, *before)


def arrived(refs, counts, step, use):
    at = 0
    for index, count in enumerate(counts):
        block = refs[at : at + count]
        at += count

        @pl.when(step == index)
        def _(block=block):
            rows = [ref[...].reshape(-1, ref.shape[-1]) for ref in block]
            use(rows[0] if len(rows) == 1 else jnp.concatenate(rows, axis=0))


def project_kernel(counts, given, me_ref, *refs):
    pieces = sum(counts)
    weight_ref = refs[pieces]
    out_ref, rows_ref = refs[pieces + 1 + given :]
    chans = weight_ref.shape[2]

    def use(rows):
        rows_ref[0] = rows
        for part in range(3):
            out_ref[0, :, part * chans : (part + 1) * chans] = dot32(rows, weight_ref[part])

    arrived(refs, counts, pl.program_id(0), use)


def hidden_back_kernel(counts, given, me_ref, *refs):
    pieces = sum(counts)
    weight_ref = refs[pieces]
    out_ref, rows_ref = refs[pieces + 1 + given :]

    def use(rows):
        rows_ref[0] = rows
        out_ref[...] = contract_cols(weight_ref[...], rows)

    arrived(refs, counts, pl.program_id(0), use)


def feed_kernel(counts, given, me_ref, *refs):
    pieces = sum(counts)
    gate_w, up_w, back_ref = refs[pieces : pieces + 3]
    hidden_ref, ggate_ref, gup_ref, rows_ref = refs[pieces + 3 + given :]

    def use(rows):
        rows_ref[0] = rows
        gate = contract_cols(gate_w[...], rows)
        up = contract_cols(up_w[...], rows)
        sig = jax.nn.sigmoid(gate)
        silu = gate * sig
        hidden_ref[...] = (silu * up).astype(bf16)
        back = back_ref[...]
        ggate_ref[...] = (back * up * sig * (1.0 + gate * (1.0 - sig))).astype(bf16)
        gup_ref[...] = (back * silu).astype(bf16)

    arrived(refs, counts, pl.program_id(0), use)


def on_arrival(kernel, me, group, start, total, fixed, per_block, outputs, filled):
    pieces = [piece for block in group for piece in block]
    rows = sum(piece.shape[0] * piece.shape[1] for piece in group[0])

    def at_rows(i, m):
        return (m[0] ^ (start + i), 0, 0)

    def at_cols(i, m):
        return (0, m[0] ^ (start + i))

    def out_spec(width, dtype, turned):
        return pl.BlockSpec((width, rows), at_cols) if turned else pl.BlockSpec((1, rows, width), at_rows)

    def out_type(width, dtype, turned):
        return jax.ShapeDtypeStruct((width, total * rows) if turned else (total, rows, width), dtype)

    work = sum(2 * op.size for op in fixed)
    operands = [me, *pieces, *fixed, *per_block, *filled]
    first = len(operands) - len(filled)
    return pl.pallas_call(
        partial(kernel, [len(block) for block in group], len(filled)),
        grid_spec=pltpu.PrefetchScalarGridSpec(
            num_scalar_prefetch=1,
            grid=(len(group),),
            in_specs=[whole(op.shape) for op in (*pieces, *fixed)]
            + [pl.BlockSpec((op.shape[0], rows), at_cols) for op in per_block]
            + [pl.BlockSpec(memory_space=pl.ANY)] * len(filled),
            out_specs=[out_spec(*output) for output in outputs],
        ),
        out_shape=[out_type(*output) for output in outputs],
        input_output_aliases={first + i: i for i in range(len(filled))},
        compiler_params=params(VMEM_LIMIT if kernel is project_kernel else SMALL_LIMIT),
        cost_estimate=cost(len(group) * rows * work, sum(op.size * 2 for op in fixed)),
        name=kernel.__name__.removesuffix("_kernel"),
    )(*operands)


def sum_products(dot, rights, dtype, turned):
    def kernel(*refs):
        count = len(rights)
        lefts = [ref[...] if turned else ref[0] for ref in refs[:count]]
        total = dot(lefts[0], refs[count][...])
        for left, right in zip(lefts[1:], refs[count + 1 : 2 * count]):
            total = total + dot(left, right[...])
        refs[2 * count][0] = total.astype(dtype)

    def call(blocks, *lefts):
        if turned:
            depth, rows = lefts[0].shape[0], lefts[0].shape[1] // blocks
            left_spec = pl.BlockSpec((depth, rows), lambda i: (0, i))
        else:
            _, rows, depth = lefts[0].shape
            left_spec = pl.BlockSpec((1, rows, depth), lambda i: (i, 0, 0))
        width = rights[0].shape[0 if dot is contract_cols else 1]
        return pl.pallas_call(
            kernel,
            grid=(blocks,),
            in_specs=[left_spec] * len(lefts) + [whole(right.shape) for right in rights],
            out_specs=pl.BlockSpec((1, rows, width), lambda i: (i, 0, 0)),
            out_shape=jax.ShapeDtypeStruct((blocks, rows, width), dtype),
            compiler_params=params(SMALL_LIMIT),
            cost_estimate=cost(sum(2 * left.size * width for left in lefts), 2 * blocks * rows * width),
            name="sum_products",
        )(*lefts, *rights)

    return call


def token_grad_kernel(grad_ref, rows_ref, second_ref, gain_ref, out_ref):
    rows_in = rows_ref[0].astype(f32)
    scale = row_scale(rows_in)
    total = second_ref[0] + norm_back(grad_ref[0].astype(f32), rows_in, scale, gain_ref[...])
    out_ref[0, :, 0, :] = total


def token_grad(grad_normed, rows_in, grad_second, gain):
    seqs, rows, width = grad_normed.shape
    part = pl.BlockSpec((1, rows, width), lambda i: (i, 0, 0))
    return pl.pallas_call(
        token_grad_kernel,
        grid=(seqs,),
        in_specs=[part, part, part, whole((1, width))],
        out_specs=pl.BlockSpec((1, rows, 1, width), lambda i: (i, 0, 0, 0)),
        out_shape=jax.ShapeDtypeStruct((seqs, rows, 1, width), f32),
        compiler_params=params(SMALL_LIMIT),
        cost_estimate=cost(1000, 1000),
        name="token_grad",
    )(grad_normed, rows_in, grad_second, gain.reshape(1, width))


def outer_kernel(left_ref, right_ref, out_ref):
    out_ref[...] = dot32(left_ref[...], right_ref[...]).astype(bf16)


def outer(left, right, number, count):
    height, depth = left.shape[0] // count, left.shape[1]
    width = right.shape[1]
    tile = math.gcd(width, 512)
    return pl.pallas_call(
        outer_kernel,
        grid=(width // tile,),
        in_specs=[
            pl.BlockSpec((height, depth), lambda j: (number, 0)),
            pl.BlockSpec((depth, tile), lambda j: (0, j)),
        ],
        out_specs=pl.BlockSpec((height, tile), lambda j: (0, j)),
        out_shape=jax.ShapeDtypeStruct((height, width), bf16),
        compiler_params=params(SMALL_LIMIT),
        cost_estimate=cost(2 * height * depth * width, 2 * depth * width),
        name="weight_gradient",
    )(left, right)


def gather_whole(block):
    return lax.all_gather(block, "mp", axis=0)


def scatter_whole(partial_sums):
    return lax.psum_scatter(partial_sums, "mp", scatter_dimension=0).astype(f32)


def finish_kernel(end_ref, *refs):
    out_ref = refs[-1]
    count = len(refs) // 2
    for number in range(count):

        @pl.when(pl.program_id(0) == number)
        def _(number=number):
            outward, total = refs[2 * number][...].astype(f32), refs[2 * number + 1][...].astype(f32)
            out_ref[...] = jnp.where(end_ref[0] == 1, outward, total)


def finish(end, pairs):
    height, width = pairs[0][1].shape
    operands = [array for pair in pairs for array in pair]
    return pl.pallas_call(
        finish_kernel,
        grid_spec=pltpu.PrefetchScalarGridSpec(
            num_scalar_prefetch=1,
            grid=(len(pairs),),
            in_specs=[whole(op.shape) for op in operands],
            out_specs=pl.BlockSpec((height, width), lambda i, e: (i, 0)),
        ),
        out_shape=jax.ShapeDtypeStruct((height * len(pairs), width), f32),
        compiler_params=params(SMALL_LIMIT),
        cost_estimate=cost(1000, 1000),
        name="finish",
    )(end, *operands)


def add_kernel(left_ref, right_ref, out_ref):
    out_ref[...] = (left_ref[...].astype(f32) + right_ref[...].astype(f32)).astype(bf16)


def add(left, right):
    height, width = left.shape
    rows = height // 2 if height % 32 == 0 and height > 128 else height
    piece = pl.BlockSpec((rows, width), lambda i: (i, 0))
    return pl.pallas_call(
        add_kernel,
        grid=(height // rows,),
        in_specs=[piece, piece],
        out_specs=piece,
        out_shape=jax.ShapeDtypeStruct(left.shape, bf16),
        compiler_params=params(SMALL_LIMIT),
        cost_estimate=cost(1000, 1000),
        name="add",
    )(left, right)


def merge_kernel(end_ref, part_ref, left_ref, right_ref, out_ref):
    total = (left_ref[...].astype(f32) + right_ref[...].astype(f32)).astype(bf16)
    out_ref[...] = jnp.where(end_ref[0] == 1, part_ref[...].astype(f32), total.astype(f32)).astype(bf16)


def merge(end, part, left, right):
    piece = pl.BlockSpec(left.shape, lambda i, e: (0, 0))
    return pl.pallas_call(
        merge_kernel,
        grid_spec=pltpu.PrefetchScalarGridSpec(
            num_scalar_prefetch=1, grid=(1,), in_specs=[piece] * 3, out_specs=piece
        ),
        out_shape=jax.ShapeDtypeStruct(left.shape, bf16),
        compiler_params=params(SMALL_LIMIT),
        cost_estimate=cost(1000, 1000),
        name="merge",
    )(end, part, left, right)


def together(*values):
    return lax.optimization_barrier(values)


def together(*values):
    return lax.optimization_barrier(values)


class WholeGather:
    def __init__(self, block):
        self.here = gather_whole(block)

    def tie(self, names, *values):
        return values

    def reach(self):
        pass

    def near(self):
        return [(self.here[i],) for i in range(self.here.shape[0])]

    def side(self):
        return []

    def far(self):
        return []


class Plain:
    def __init__(self):
        self.parts = []

    def counts(self, size):
        return (size, 0, 0)

    def origin(self):
        return jnp.zeros((1,), jnp.int32)

    def gather(self, block):
        return WholeGather(block)

    def scatter(self, array, product, coming, compute):
        return scatter_whole(product(array)), compute()

    def sum_mp(self, part):
        return lax.psum(part, "mp")

    def hop(self, *values, part=None, last=False):
        if part is not None:
            self.parts.append(lax.psum(part, "dp"))
        return values

    def sums(self):
        return self.parts

    def join(self, first, last):
        return jnp.concatenate([part.astype(f32) for part in self.parts[first:last]], axis=0)

    def inward(self, part):
        return lax.psum(part, "dp")

    def across(self, part, came):
        return came, came

    def outward(self, half, came):
        return came, came

    def settled(self, total, came):
        return came.astype(f32)


def swap(block, bit):
    return lax.ppermute(block, "mp", [(i, i ^ bit) for i in range(8)])


class SquareGather:
    def __init__(self, block):
        self.here = {"near": (block, swap(block, 1)), "side": (swap(block, 2), swap(block, 4))}

    def tie(self, names, *values):
        held, values = together([self.here[name] for name in names], values)
        self.here.update(zip(names, held))
        return values

    def reach(self):
        x_all, y_all = self.here["side"]
        cut = x_all.shape[0] // 2
        self.here["far"] = (swap(x_all[:cut], 4), swap(y_all[cut:], 2))

    def near(self):
        return [(block,) for block in self.here["near"]]

    def side(self):
        return [(block,) for here in self.here["side"] for block in (here, swap(here, 1))]

    def far(self):
        halves = self.here["far"]
        return [halves, tuple(swap(half, 1) for half in halves)]


class Lane:
    def __init__(self):
        self.queue, self.flight, self.done = [], {}, []
        self.part = self.half = self.total = None

    def advance(self, end):
        flight = self.flight
        if "out" in flight:
            self.done.append((flight["out"], self.total))
        half = add(self.part, flight["in"]) if "in" in flight else None
        self.part = self.queue.pop(0) if self.queue else None
        started = {}
        if "across" in flight and self.part is not None and self.part.shape == self.half.shape:
            self.total = merge(end, self.part, self.half, flight["across"])
            started["in"] = started["out"] = lax.ppermute(self.total, "dp", [(0, 1), (3, 2), (1, 0), (2, 3)])
        else:
            if self.part is not None:
                started["in"] = lax.ppermute(self.part, "dp", [(0, 1), (3, 2)])
            if "across" in flight:
                self.total = add(self.half, flight["across"])
                started["out"] = lax.ppermute(self.total, "dp", [(1, 0), (2, 3)])
        if half is not None:
            started["across"] = lax.ppermute(half, "dp", [(1, 2), (2, 1)])
        self.half, self.flight = half, started


class Square:
    def __init__(self):
        self.lanes, self.turn = (Lane(), Lane()), 0

    def counts(self, size):
        return (2, 4, 2)

    def origin(self):
        return lax.axis_index("mp").astype(jnp.int32).reshape(1)

    def gather(self, block):
        return SquareGather(block)

    def scatter(self, array, product, coming, compute):
        def both(mine, other):
            return mine.astype(f32) + swap(other, 1).astype(f32)

        far, array = together(product(array[6:8]), array)
        half = far.shape[1] // 2
        far_sum = both(far[0], far[1])
        far_low, far_high = far_sum[:half].astype(bf16), far_sum[half:].astype(bf16)
        side, near, far_low, far_high = together(product(array[2:6]), product(array[0:2]), far_low, far_high)
        from_far_low, from_far_high = swap(far_low, 2), swap(far_high, 4)
        x_sum = both(side[0], side[1])
        y_sum = both(side[2], side[3])
        own = both(near[0], near[1])
        own, x_sum, y_sum = coming.tie(["near", "side"], own, x_sum, y_sum)
        own_low_x = swap(x_sum[:half].astype(bf16), 2)
        own_high_y = swap(y_sum[half:].astype(bf16), 4)
        beside = compute()
        from_far_low, from_far_high, own_low_x, own_high_y, beside = together(
            from_far_low, from_far_high, own_low_x, own_high_y, beside
        )
        y_low = (y_sum[:half] + from_far_low.astype(f32)).astype(bf16)
        x_high = (x_sum[half:] + from_far_high.astype(f32)).astype(bf16)
        own_low_y = swap(y_low, 4)
        own_high_x = swap(x_high, 2)
        low = own[:half] + own_low_x.astype(f32) + own_low_y.astype(f32)
        high = own[half:] + own_high_y.astype(f32) + own_high_x.astype(f32)
        return jnp.concatenate([low, high], axis=0), beside

    def sum_mp(self, part):
        for bit in (1, 2, 4):
            part = part + swap(part, bit)
        return part

    def end(self):
        place = lax.axis_index("dp")
        return ((place == 0) | (place == 3)).astype(jnp.int32).reshape(1)

    def hop(self, *values, part=None, last=False):
        lane = self.lanes[self.turn]
        self.turn = 1 - self.turn
        if last:
            done = [each.done for each in self.lanes]
            lane.flight, done, values = together(lane.flight, done, values)
            for each, sums in zip(self.lanes, done):
                each.done = list(sums)
        else:
            lane.flight, part, values = together(lane.flight, part, values)
        if part is not None:
            cut = part.shape[0] // 2
            for each, half in zip(self.lanes, (part[:cut], part[cut:])):
                each.queue.append(half)
        lane.advance(self.end())
        return values

    def join(self, first, last):
        return finish(self.end(), [lane.done[number] for number in range(first, last) for lane in self.lanes])


    def inward(self, part):
        return lax.ppermute(part, "dp", [(0, 1), (3, 2)])

    def across(self, part, came):
        half = add(part, came)
        return half, lax.ppermute(half, "dp", [(1, 2), (2, 1)])

    def outward(self, half, came):
        total = add(half, came)
        return total, lax.ppermute(total, "dp", [(1, 0), (2, 3)])

    def settled(self, total, came):
        return jnp.where(self.end()[0] == 1, came, total).astype(f32)


def local(
    links, tokens, lengths, norm_gain, in_proj, short_taps, conv_skip, filter_residue, filter_rate, filter_freq,
    out_proj, mlp_gain, gate_proj, up_proj, down_proj, cotangent,
):
    micro, rows, per_dev, width = tokens.shape
    seqs = micro * per_dev
    chans = in_proj.shape[2]
    hidden_units = gate_proj.shape[1]
    length = rows * lax.axis_size("mp")
    in_parts = in_proj.transpose(1, 0, 2)
    in_flat = in_proj.reshape(width, 3 * chans)
    gate_t, up_t = gate_proj.T, up_proj.T
    table = dft_matrix(length)
    dft = jnp.asarray(table, bf16)
    inverse = jnp.asarray(table.T / length, bf16)
    me = links.origin()

    def by_sequence(array):
        return array.transpose(0, 2, 1, 3).reshape(seqs, rows, array.shape[3])

    def by_position(array):
        return array.reshape(micro, per_dev, rows, array.shape[2]).transpose(0, 2, 1, 3)

    def flat(array):
        return array.reshape(-1, array.shape[-1])

    def grouped(array, like):
        return array.reshape(like.shape[:-1] + (array.shape[-1],))

    positions = lax.axis_index("mp") * rows + jnp.arange(rows)
    valid = (positions[None, :] < lengths.reshape(seqs)[:, None]).astype(f32)[:, :, None]

    rows_in = by_sequence(tokens).astype(f32)
    scale_in = row_scale(rows_in)
    normed = (rows_in * scale_in * norm_gain).astype(bf16)
    coming = links.gather(normed)

    high = (STEP * jnp.arange(length // STEP)).astype(f32)[:, None, None]
    low = jnp.arange(STEP).astype(f32)[None, :, None]
    rate_t, freq_t, residue_t = filter_rate.T, filter_freq.T, filter_residue.T
    decay_high, turn_high = jnp.exp(-rate_t * high), freq_t * high
    decay_low, turn_low = jnp.exp(-rate_t[:, None, :] * low), freq_t[:, None, :] * low
    tables = (
        decay_high * jnp.cos(turn_high),
        decay_high * jnp.sin(turn_high),
        decay_low * jnp.cos(turn_low),
        decay_low * jnp.sin(turn_low),
    )
    filt_spec = make_filter(tables, residue_t, dft)
    grad_final = by_sequence(cotangent).astype(f32) * valid
    grad_final_low = grad_final.astype(bf16)
    blocks = lax.axis_size("mp")
    counts = links.counts(blocks)
    starts = [sum(counts[:i]) for i in range(len(counts))]

    def arrive(kernel, group, number, fixed, per_block, outputs, filled):
        if not group:
            return filled
        return on_arrival(kernel, me, group, starts[number], blocks, fixed, per_block, outputs, filled)

    def projected(group, number, filled):
        return arrive(project_kernel, group, number, (in_parts,), (), ((3 * chans, f32, False), (width, bf16, False)), filled)

    filled = projected(coming.near(), 0, ())
    filled, filt_spec, grad_final_low, in_flat = coming.tie(["side"], filled, filt_spec, grad_final_low, in_flat)
    coming.reach()
    filled = projected(coming.side(), 1, filled)
    filled, grad_final_low = coming.tie(["far"], filled, grad_final_low)
    grad_coming = links.gather(grad_final_low)
    proj, normed_all = projected(coming.far(), 2, filled)
    proj = proj.reshape(blocks, seqs, rows, 3 * chans)
    taps9 = short_taps.reshape(9, chans)
    skip = conv_skip.reshape(1, chans)
    gated, gated_ordered, response, spec = mixer(me, proj, taps9, skip, filt_spec, dft, inverse)
    (gated,) = grad_coming.tie(["side"], gated)
    grad_coming.reach()

    def mixed_out(part):
        return grouped(dot32(flat(part), out_proj).astype(bf16), part)

    def hidden_backed(group, number, filled):
        return arrive(hidden_back_kernel, group, number, (down_proj,), (), ((hidden_units, f32, True), (width, bf16, False)), filled)

    def beside_scatter():
        return hidden_backed(grad_coming.side(), 1, hidden_backed(grad_coming.near(), 0, ()))

    mixed_sum, filled = links.scatter(gated, mixed_out, grad_coming, beside_scatter)
    second = rows_in + mixed_sum
    scale_second = row_scale(second)
    mlp_normed = (second * scale_second * mlp_gain).astype(bf16)
    coming = links.gather(mlp_normed)
    grad_hidden, grad_final_all = hidden_backed(grad_coming.far(), 2, filled)

    def fed(group, number, filled):
        outputs = ((hidden_units, bf16, True),) * 3 + ((width, bf16, False),)
        return arrive(feed_kernel, group, number, (gate_t, up_t), (grad_hidden,), outputs, filled)

    (filled,) = coming.tie(["side"], fed(coming.near(), 0, ()))
    coming.reach()
    filled = fed(coming.side(), 1, filled)
    (filled,) = coming.tie(["far"], filled)
    hidden, grad_gate, grad_up, mlp_all = fed(coming.far(), 2, filled)

    def weight_gradient(left, right):
        return contract_rows(flat(left), flat(right)).astype(bf16)

    def blocked(array):
        return array.reshape(blocks, seqs, rows, array.shape[-1])

    grad_final_all, mlp_all = flat(grad_final_all), flat(mlp_all)
    links.hop(part=outer(hidden, grad_final_all, 0, 2))
    links.hop()
    grad_gate, grad_up, hidden = links.hop(
        grad_gate, grad_up, hidden, part=outer(hidden, grad_final_all, 1, 2)
    )
    mlp_back = blocked(sum_products(contract_rows, (gate_t, up_t), bf16, True)(blocks, grad_gate, grad_up))
    mlp_back, grad_gate = links.hop(mlp_back, grad_gate)
    grad_mlp_normed = scatter_whole(mlp_back)
    grad_gate, grad_up = links.hop(grad_gate, grad_up, part=outer(grad_gate, mlp_all, 0, 2))
    gate_two, grad_up = links.hop(outer(grad_gate, mlp_all, 1, 2), grad_up)
    up_one, grad_up = links.hop(outer(grad_up, mlp_all, 0, 2), grad_up, part=gate_two)
    up_two, second = links.hop(outer(grad_up, mlp_all, 1, 2), second)
    second, hidden = links.hop(second, hidden, part=up_one)
    grad_second = grad_final + norm_back(grad_mlp_normed, second, scale_second, mlp_gain)
    gain_two = jnp.sum(grad_mlp_normed * second * scale_second, axis=(0, 1))
    grad_branch_all = gather_whole(grad_second.astype(bf16))
    mlp_part = blocked(sum_products(contract_rows, (down_proj,), bf16, True)(blocks, hidden))
    mlp_part, gain_two = links.hop(mlp_part, gain_two)
    mlp_part, gated_ordered = links.hop(mlp_part, gated_ordered, part=up_two)
    mlp_part, gated_ordered = links.hop(mlp_part, gated_ordered)

    grad_gated = blocked(
        sum_products(contract_cols, (out_proj,), f32, False)(blocks, grad_branch_all.reshape(blocks, -1, width))
    )
    grad_out = weight_gradient(gated_ordered, grad_branch_all)
    grad_gated, mlp_part = links.hop(grad_gated, mlp_part, part=grad_out)
    mlp_out = scatter_whole(mlp_part)
    back = ()
    for number in range(seqs - 1):
        back = mixer_back(number, back, grad_gated, proj, response, spec, taps9, skip, filt_spec, dft, inverse)
    back, grad_gated = links.hop(back, grad_gated)
    grad_proj, grad_taps, grad_filt = mixer_back(
        seqs - 1, tuple(back), grad_gated, proj, response, spec, taps9, skip, filt_spec, dft, inverse
    )
    grad_in = weight_gradient(normed_all, grad_proj)
    grads_in = [grad_in[:, part * chans : (part + 1) * chans] for part in range(3)]
    grads_in, grad_proj, grad_filt = links.hop(grads_in, grad_proj, grad_filt, part=grads_in[0])
    grad_in_rows = blocked(contract_cols(flat(grad_proj), in_flat).astype(bf16).reshape(blocks, -1, width))
    grad_in_rows, grads_in = links.hop(grad_in_rows, grads_in)
    grads_in, grad_filt = links.hop(grads_in, grad_filt, part=grads_in[1])
    grad_normed = scatter_whole(grad_in_rows)

    ones = jnp.ones((8, chans), bf16)
    against = sum(
        contract_cols(ones, (grad.astype(f32) * part.astype(f32)).astype(bf16))[0]
        for grad, part in zip(grads_in, in_parts)
    )
    gains = jnp.stack([against / norm_gain, gain_two], axis=0)
    gains, grad_filt = links.hop(gains, grad_filt)
    pole_sum, pole_re, pole_im = pole_gradients(grad_filt, tables)
    gains, pole_sum = links.hop(links.sum_mp(gains), pole_sum, part=grads_in[2])
    poles = filter_residue.shape[1]
    small = [grad_taps, pole_sum, -residue_t * pole_re, -residue_t * pole_im, gains.reshape(-1, chans)]
    small = [jnp.pad(rows_of, ((0, -rows_of.shape[0] % 8), (0, 0))) for rows_of in small]
    bounds = np.cumsum([0] + [rows_of.shape[0] for rows_of in small])
    small = jnp.pad(jnp.concatenate(small, axis=0), ((0, -int(bounds[-1]) % 32), (0, 0))).astype(bf16)
    (small,) = links.hop(small)
    came = links.inward(small)
    links.hop()
    (came,) = links.hop(came)
    half, came = links.across(small, came)
    grad_second, mlp_out = links.hop(grad_second, mlp_out)
    layer_out = ((second + mlp_out) * valid).astype(bf16)
    half, came, layer_out, grad_second = links.hop(half, came, layer_out, grad_second, last=True)
    total, came = links.outward(half, came)
    if per_dev == 1:
        grad_tokens = token_grad(grad_normed, by_sequence(tokens), grad_second, norm_gain)
    else:
        grad_tokens = by_position(grad_second + norm_back(grad_normed, rows_in, scale_in, norm_gain))
    sum_down, sum_gate, sum_up, sum_out = (links.join(*at) for at in ((0, 2), (2, 4), (4, 6), (6, 7)))
    grad_tokens, total = links.hop(grad_tokens, total)
    came, sum_down, sum_gate, sum_up, sum_out = links.hop(came, sum_down, sum_gate, sum_up, sum_out)
    sum_small = links.settled(total, came)
    sum_in = links.join(7, 10).reshape(3, width, chans)
    small = [sum_small[low:high] for low, high in zip(bounds[:-1], bounds[1:])]
    gains = small[4][: 2 * width // chans].reshape(2, width)
    return (
        by_position(layer_out),
        grad_tokens,
        gains[0],
        sum_in.transpose(1, 0, 2),
        small[0][:9].reshape(3, 3, chans),
        small[0][9],
        small[1][:poles].T,
        small[2][:poles].T,
        small[3][:poles].T,
        sum_out,
        gains[1],
        sum_gate.T,
        sum_up.T,
        sum_down,
    )


def solution(mesh):
    square = mesh.shape["mp"] == 8 and mesh.shape["dp"] == 4
    links = Square() if square else Plain()
    wide = P(None, "mp", "dp", None)
    chan = P("mp", None)
    return jax.shard_map(
        partial(local, links),
        mesh=mesh,
        in_specs=(
            wide, P(None, "dp"), P(), P(None, None, "mp"), P(None, None, "mp"), P("mp"), chan, chan, chan,
            chan, P(), P(None, "mp"), P(None, "mp"), chan, wide,
        ),
        out_specs=(
            wide, wide, P(), P(None, None, "mp"), P(None, None, "mp"), P("mp"), chan, chan, chan,
            chan, P(), P(None, "mp"), P(None, "mp"), chan,
        ),
        check_vma=False,
    )
```

```python
import math
from functools import partial

import jax
import jax.numpy as jnp
import numpy as np
from jax import lax
from jax.experimental import pallas as pl
from jax.experimental.pallas import tpu as pltpu
from jax.sharding import PartitionSpec as P

epsilon = 1e-06
bf16 = jnp.bfloat16
f32 = jnp.float32
STEP = 32
VMEM_LIMIT = 52 * 1024 * 1024
SMALL_LIMIT = 30 * 1024 * 1024


def dft_matrix(length):
    freqs = np.arange(length)[:, None]
    times = np.arange(length)[None, :]
    angle = np.pi * (((2 * freqs + 1) * times) % (4 * length)) / (2 * length)
    return np.concatenate([np.cos(angle), -np.sin(angle)], axis=0)


def dot32(left, right):
    return jnp.dot(left, right, preferred_element_type=f32)


def contract_rows(left, right):
    return lax.dot_general(left, right, (((0,), (0,)), ((), ())), preferred_element_type=f32)


def contract_cols(left, right):
    return lax.dot_general(left, right, (((1,), (1,)), ((), ())), preferred_element_type=f32)


def row_scale(rows_in):
    return lax.rsqrt(jnp.mean(rows_in * rows_in, axis=-1, keepdims=True) + epsilon)


def norm_back(grad_y, rows_in, scale, gain):
    weighted = gain * grad_y
    inner = jnp.mean(weighted * rows_in, axis=-1, keepdims=True)
    return scale * weighted - rows_in * (scale * scale * scale) * inner


def filter_kernel(hre_ref, him_ref, lre_ref, lim_ref, res_ref, dft_ref, spec_ref, filt_ref):
    blocks, poles, chans = hre_ref.shape
    step = lre_ref.shape[1]
    residue = res_ref[...]

    def fill(block, carry):
        pre = residue * hre_ref[block]
        pim = residue * him_ref[block]
        total = jnp.zeros((step, chans), f32)
        for pole in range(poles):
            total = total + (
                pre[pole : pole + 1] * lre_ref[pole] - pim[pole : pole + 1] * lim_ref[pole]
            )
        filt_ref[pl.ds(pl.multiple_of(block * step, step), step), :] = total.astype(bf16)
        return carry

    lax.fori_loop(0, blocks, fill, 0)
    spec_ref[...] = dot32(dft_ref[...], filt_ref[...])


def pole_kernel(grad_ref, hre_ref, him_ref, lre_ref, lim_ref, sum_ref, vre_ref, vim_ref, turned):
    blocks, poles, chans = hre_ref.shape
    step = lre_ref.shape[1]
    for late in range(step):
        turned[late] = grad_ref[pl.ds(late, blocks, stride=step), :]
    starts = step * lax.broadcasted_iota(jnp.int32, (blocks, chans), 0).astype(f32)

    for pole in range(poles):
        lre, lim = lre_ref[pole], lim_ref[pole]
        part = turned[step - 1]
        sre = part * lre[step - 1 : step]
        sim = part * lim[step - 1 : step]
        tre, tim = sre, sim
        for late in range(step - 2, -1, -1):
            part = turned[late]
            sre = sre + part * lre[late : late + 1]
            sim = sim + part * lim[late : late + 1]
            if late:
                tre = tre + sre
                tim = tim + sim
        hre = hre_ref[:, pole, :]
        him = him_ref[:, pole, :]
        wre = starts * sre + tre
        wim = starts * sim + tim
        sum_ref[pole : pole + 1, :] = jnp.sum(hre * sre - him * sim, axis=0, keepdims=True)
        vre_ref[pole : pole + 1, :] = jnp.sum(hre * wre - him * wim, axis=0, keepdims=True)
        vim_ref[pole : pole + 1, :] = jnp.sum(hre * wim + him * wre, axis=0, keepdims=True)


def load_padded(parts, pad):
    for index, part in enumerate(parts):
        blocks, _, rows, chans = part.shape
        pad[index, 0:8, :] = jnp.zeros((8, chans), f32)
        for block in range(blocks):
            pad[index, 8 + block * rows : 8 + (block + 1) * rows, :] = part[block, 0]


def short_rows(pad, taps, index, start, count):
    total = taps[index : index + 1] * pad[index, 8 + start : 8 + start + count, :]
    for back in (1, 2):
        tap = taps[3 * back + index : 3 * back + index + 1]
        total = total + tap * pad[index, 8 + start - back : 8 + start - back + count, :]
    return total


def mixer_kernel(
    me_ref, q_ref, k_ref, v_ref, taps_ref, skip_ref, filt_ref, dft_ref, inv_ref,
    gated_ref, ordered_ref, resp_ref, spec_ref, pad, mixed, product, conv,
):
    me = me_ref[0]
    blocks, _, rows, chans = q_ref.shape
    length = blocks * rows
    load_padded((q_ref, k_ref, v_ref), pad)
    taps = taps_ref[...]
    skip = skip_ref[...]
    for block in range(blocks):
        start = block * rows
        key = short_rows(pad, taps, 1, start, rows)
        value = short_rows(pad, taps, 2, start, rows)
        mixed[start : start + rows, :] = (key * value).astype(bf16)
    spec_ref[0] = dot32(dft_ref[...], mixed[...])
    for block in range(blocks):
        re = slice(block * rows, (block + 1) * rows)
        im = slice(length + block * rows, length + (block + 1) * rows)
        mre, mim = spec_ref[0, re, :], spec_ref[0, im, :]
        hre, him = filt_ref[re, :], filt_ref[im, :]
        product[re, :] = (mre * hre - mim * him).astype(bf16)
        product[im, :] = (mre * him + mim * hre).astype(bf16)
    conv[...] = dot32(inv_ref[...], product[...])
    for block in range(blocks):
        start = block * rows
        response = conv[start : start + rows, :] + skip * mixed[start : start + rows, :].astype(f32)
        resp_ref[0, start : start + rows, :] = response
        query = short_rows(pad, taps, 0, start, rows)
        gated = (query * response).astype(bf16)
        gated_ref[me ^ block, 0] = gated
        ordered_ref[block, 0] = gated


def mixer_back_kernel(first, last, *refs):
    gg_ref, q_ref, k_ref, v_ref, resp_ref, spec_ref, taps_ref, skip_ref, filt_ref, dft_ref, inv_ref = refs[:11]
    refs = refs[11:]
    if not first:
        taps_before, lags_before = refs[1:3]
        refs = refs[3:]
    gproj_ref, gtaps_ref, result_ref, pad, late, response_grad, grad_conv, spectrum, product, conv = refs
    blocks, _, rows, chans = q_ref.shape
    length = blocks * rows
    load_padded((q_ref, k_ref, v_ref), pad)
    taps = taps_ref[...]
    skip = skip_ref[...]

    gtaps_ref[...] = jnp.zeros_like(gtaps_ref) if first else taps_before[...]
    late[:, length : length + 8, :] = jnp.zeros((3, 8, chans), f32)
    skip_sum = jnp.zeros((1, chans), f32)
    for block in range(blocks):
        start = block * rows
        at = slice(start, start + rows)
        incoming = gg_ref[block, 0].astype(f32)
        query = short_rows(pad, taps, 0, start, rows)
        key = short_rows(pad, taps, 1, start, rows)
        value = short_rows(pad, taps, 2, start, rows)
        mixed = (key * value).astype(bf16).astype(f32)
        grad = incoming * query
        response_grad[at, :] = grad
        grad_conv[at, :] = grad.astype(bf16)
        late[0, at, :] = incoming * resp_ref[0, at, :]
        skip_sum = skip_sum + jnp.sum(grad * mixed, axis=0, keepdims=True)
    gtaps_ref[9:10, :] += skip_sum

    spectrum[...] = dot32(dft_ref[...], grad_conv[...])
    for block in range(blocks):
        re = slice(block * rows, (block + 1) * rows)
        im = slice(length + block * rows, length + (block + 1) * rows)
        gre, gim = spectrum[re, :], spectrum[im, :]
        hre, him = filt_ref[re, :], filt_ref[im, :]
        mre, mim = spec_ref[0, re, :], spec_ref[0, im, :]
        product[re, :] = (gre * hre + gim * him).astype(bf16)
        product[im, :] = (gim * hre - gre * him).astype(bf16)
        lag_re = gre * mre + gim * mim
        lag_im = gim * mre - gre * mim
        if not first:
            lag_re = lag_re + lags_before[re, :]
            lag_im = lag_im + lags_before[im, :]
        lags = spectrum if last else result_ref
        lags[re, :] = lag_re
        lags[im, :] = lag_im
    conv[...] = dot32(inv_ref[...], product[...])

    for block in range(blocks):
        start = block * rows
        at = slice(start, start + rows)
        key = short_rows(pad, taps, 1, start, rows)
        value = short_rows(pad, taps, 2, start, rows)
        grad_mixed = conv[at, :] + skip * response_grad[at, :]
        late[1, at, :] = grad_mixed * value
        late[2, at, :] = grad_mixed * key

    sums = [jnp.zeros((1, chans), f32) for _ in range(9)]
    for block in range(blocks):
        start = block * rows
        for index in range(3):
            grad = late[index, start : start + rows, :]
            total = taps[index : index + 1] * grad
            for back in (1, 2):
                tap = taps[3 * back + index : 3 * back + index + 1]
                total = total + tap * late[index, start + back : start + back + rows, :]
            gproj_ref[block, 0, :, index * chans : (index + 1) * chans] = total.astype(bf16)
            for back in range(3):
                shifted = pad[index, 8 + start - back : 8 + start - back + rows, :]
                sums[3 * back + index] = sums[3 * back + index] + jnp.sum(
                    grad * shifted, axis=0, keepdims=True
                )
    for index in range(9):
        gtaps_ref[index : index + 1, :] += sums[index]

    if last:
        product[...] = spectrum[...].astype(bf16)
        result_ref[...] = dot32(inv_ref[...], product[...])


def whole(shape):
    return pl.BlockSpec(shape, lambda *_: (0,) * len(shape), pipeline_mode=pl.Buffered(1))


def cost(flops, nbytes):
    return pl.CostEstimate(flops=flops, bytes_accessed=nbytes, transcendentals=0)


def params(limit=VMEM_LIMIT):
    return pltpu.CompilerParams(vmem_limit_bytes=limit)


def make_filter(tables, residue_t, dft):
    hre, him, lre, lim = tables
    chans = residue_t.shape[1]
    length = dft.shape[1]
    operands = (hre, him, lre, lim, residue_t, dft)
    return pl.pallas_call(
        filter_kernel,
        grid=(1,),
        in_specs=[whole(op.shape) for op in operands],
        out_specs=whole((2 * length, chans)),
        out_shape=jax.ShapeDtypeStruct((2 * length, chans), f32),
        scratch_shapes=[pltpu.VMEM((length, chans), bf16)],
        compiler_params=params(),
        name="modal_filter",
    )(*operands)


def pole_gradients(grad_filt, tables):
    hre, him, lre, lim = tables
    blocks, poles, chans = hre.shape
    step = lre.shape[1]
    lanes = min(chans, 128)

    def lane_block(*lead):
        return pl.BlockSpec(lead + (lanes,), lambda c: (0,) * len(lead) + (c,))

    operands = (grad_filt, hre, him, lre, lim)
    return pl.pallas_call(
        pole_kernel,
        grid=(chans // lanes,),
        in_specs=[lane_block(*op.shape[:-1]) for op in operands],
        out_specs=[lane_block(poles)] * 3,
        out_shape=[jax.ShapeDtypeStruct((poles, chans), f32)] * 3,
        scratch_shapes=[pltpu.VMEM((step, blocks, lanes), f32)],
        compiler_params=params(),
        name="pole_gradients",
    )(*operands)


def mixer(me, proj, taps9, skip, filt_spec, dft, inverse):
    blocks, seqs, rows, triple = proj.shape
    chans = triple // 3
    length = blocks * rows
    fixed = (taps9, skip, filt_spec, dft, inverse)

    def part(index):
        return pl.BlockSpec((blocks, 1, rows, chans), lambda s, m: (0, s, 0, index))

    return pl.pallas_call(
        mixer_kernel,
        grid_spec=pltpu.PrefetchScalarGridSpec(
            num_scalar_prefetch=1,
            grid=(seqs,),
            in_specs=[part(0), part(1), part(2)] + [whole(op.shape) for op in fixed],
            out_specs=[
                part(0),
                part(0),
                pl.BlockSpec((1, length, chans), lambda s, m: (s, 0, 0)),
                pl.BlockSpec((1, 2 * length, chans), lambda s, m: (s, 0, 0)),
            ],
            scratch_shapes=[
                pltpu.VMEM((3, length + 8, chans), f32),
                pltpu.VMEM((length, chans), bf16),
                pltpu.VMEM((2 * length, chans), bf16),
                pltpu.VMEM((length, chans), f32),
            ],
        ),
        out_shape=[
            jax.ShapeDtypeStruct((blocks, seqs, rows, chans), bf16),
            jax.ShapeDtypeStruct((blocks, seqs, rows, chans), bf16),
            jax.ShapeDtypeStruct((seqs, length, chans), f32),
            jax.ShapeDtypeStruct((seqs, 2 * length, chans), f32),
        ],
        compiler_params=params(),
        cost_estimate=cost(8 * length * length * chans * seqs, 40 * length * chans * seqs),
        name="mixer_forward",
    )(me, proj, proj, proj, *fixed)


def mixer_back(number, before, grad_gated, proj, response, spec, taps9, skip, filt_spec, dft, inverse):
    blocks, seqs, rows, triple = proj.shape
    chans = triple // 3
    length = blocks * rows
    fixed = (taps9, skip, filt_spec, dft, inverse)
    first, last = number == 0, number == seqs - 1
    result = (length, chans) if last else (2 * length, chans)

    def part(index):
        return pl.BlockSpec((blocks, 1, rows, chans), lambda i: (0, number, 0, index))

    return pl.pallas_call(
        partial(mixer_back_kernel, first, last),
        grid=(1,),
        in_specs=[part(0), part(0), part(1), part(2)]
        + [
            pl.BlockSpec((1, length, chans), lambda i: (number, 0, 0)),
            pl.BlockSpec((1, 2 * length, chans), lambda i: (number, 0, 0)),
        ]
        + [whole(op.shape) for op in fixed]
        + ([] if first else [pl.BlockSpec(memory_space=pl.ANY)] + [whole(op.shape) for op in before[1:]]),
        out_specs=[
            pl.BlockSpec((blocks, 1, rows, triple), lambda i: (0, number, 0, 0)),
            whole((16, chans)),
            whole(result),
        ],
        scratch_shapes=[
            pltpu.VMEM((3, length + 8, chans), f32),
            pltpu.VMEM((3, length + 8, chans), f32),
            pltpu.VMEM((length, chans), f32),
            pltpu.VMEM((length, chans), bf16),
            pltpu.VMEM((2 * length, chans), f32),
            pltpu.VMEM((2 * length, chans), bf16),
            pltpu.VMEM((length, chans), f32),
        ],
        out_shape=[
            jax.ShapeDtypeStruct((blocks, seqs, rows, triple), bf16),
            jax.ShapeDtypeStruct((16, chans), f32),
            jax.ShapeDtypeStruct(result, f32),
        ],
        input_output_aliases={} if first else {11: 0},
        compiler_params=params(),
        cost_estimate=cost(12 * length * length * chans, 80 * length * chans),
        name="mixer_backward",
    )(grad_gated, proj, proj, proj, response, spec, *fixed, *before)


def arrived(refs, counts, step, use):
    at = 0
    for index, count in enumerate(counts):
        block = refs[at : at + count]
        at += count

        @pl.when(step == index)
        def _(block=block):
            rows = [ref[...].reshape(-1, ref.shape[-1]) for ref in block]
            use(rows[0] if len(rows) == 1 else jnp.concatenate(rows, axis=0))


def project_kernel(counts, given, me_ref, *refs):
    pieces = sum(counts)
    weight_ref = refs[pieces]
    out_ref, rows_ref = refs[pieces + 1 + given :]
    chans = weight_ref.shape[2]

    def use(rows):
        rows_ref[0] = rows
        for part in range(3):
            out_ref[0, :, part * chans : (part + 1) * chans] = dot32(rows, weight_ref[part])

    arrived(refs, counts, pl.program_id(0), use)


def hidden_back_kernel(counts, given, me_ref, *refs):
    pieces = sum(counts)
    weight_ref = refs[pieces]
    out_ref, rows_ref = refs[pieces + 1 + given :]

    def use(rows):
        rows_ref[0] = rows
        out_ref[...] = contract_cols(weight_ref[...], rows)

    arrived(refs, counts, pl.program_id(0), use)


def feed_kernel(counts, given, me_ref, *refs):
    pieces = sum(counts)
    gate_w, up_w, back_ref = refs[pieces : pieces + 3]
    hidden_ref, ggate_ref, gup_ref, rows_ref = refs[pieces + 3 + given :]

    def use(rows):
        rows_ref[0] = rows
        gate = contract_cols(gate_w[...], rows)
        up = contract_cols(up_w[...], rows)
        sig = jax.nn.sigmoid(gate)
        silu = gate * sig
        hidden_ref[...] = (silu * up).astype(bf16)
        back = back_ref[...]
        ggate_ref[...] = (back * up * sig * (1.0 + gate * (1.0 - sig))).astype(bf16)
        gup_ref[...] = (back * silu).astype(bf16)

    arrived(refs, counts, pl.program_id(0), use)


def on_arrival(kernel, me, group, start, total, fixed, per_block, outputs, filled):
    pieces = [piece for block in group for piece in block]
    rows = sum(piece.shape[0] * piece.shape[1] for piece in group[0])

    def at_rows(i, m):
        return (m[0] ^ (start + i), 0, 0)

    def at_cols(i, m):
        return (0, m[0] ^ (start + i))

    def out_spec(width, dtype, turned):
        return pl.BlockSpec((width, rows), at_cols) if turned else pl.BlockSpec((1, rows, width), at_rows)

    def out_type(width, dtype, turned):
        return jax.ShapeDtypeStruct((width, total * rows) if turned else (total, rows, width), dtype)

    work = sum(2 * op.size for op in fixed)
    operands = [me, *pieces, *fixed, *per_block, *filled]
    first = len(operands) - len(filled)
    return pl.pallas_call(
        partial(kernel, [len(block) for block in group], len(filled)),
        grid_spec=pltpu.PrefetchScalarGridSpec(
            num_scalar_prefetch=1,
            grid=(len(group),),
            in_specs=[whole(op.shape) for op in (*pieces, *fixed)]
            + [pl.BlockSpec((op.shape[0], rows), at_cols) for op in per_block]
            + [pl.BlockSpec(memory_space=pl.ANY)] * len(filled),
            out_specs=[out_spec(*output) for output in outputs],
        ),
        out_shape=[out_type(*output) for output in outputs],
        input_output_aliases={first + i: i for i in range(len(filled))},
        compiler_params=params(VMEM_LIMIT if kernel is project_kernel else SMALL_LIMIT),
        cost_estimate=cost(len(group) * rows * work, sum(op.size * 2 for op in fixed)),
        name=kernel.__name__.removesuffix("_kernel"),
    )(*operands)


def sum_products(dot, rights, dtype, turned):
    def kernel(*refs):
        count = len(rights)
        lefts = [ref[...] if turned else ref[0] for ref in refs[:count]]
        total = dot(lefts[0], refs[count][...])
        for left, right in zip(lefts[1:], refs[count + 1 : 2 * count]):
            total = total + dot(left, right[...])
        refs[2 * count][0] = total.astype(dtype)

    def call(blocks, *lefts):
        if turned:
            depth, rows = lefts[0].shape[0], lefts[0].shape[1] // blocks
            left_spec = pl.BlockSpec((depth, rows), lambda i: (0, i))
        else:
            _, rows, depth = lefts[0].shape
            left_spec = pl.BlockSpec((1, rows, depth), lambda i: (i, 0, 0))
        width = rights[0].shape[0 if dot is contract_cols else 1]
        return pl.pallas_call(
            kernel,
            grid=(blocks,),
            in_specs=[left_spec] * len(lefts) + [whole(right.shape) for right in rights],
            out_specs=pl.BlockSpec((1, rows, width), lambda i: (i, 0, 0)),
            out_shape=jax.ShapeDtypeStruct((blocks, rows, width), dtype),
            compiler_params=params(SMALL_LIMIT),
            cost_estimate=cost(sum(2 * left.size * width for left in lefts), 2 * blocks * rows * width),
            name="sum_products",
        )(*lefts, *rights)

    return call


def token_grad_kernel(grad_ref, rows_ref, second_ref, gain_ref, out_ref):
    rows_in = rows_ref[0].astype(f32)
    scale = row_scale(rows_in)
    total = second_ref[0] + norm_back(grad_ref[0].astype(f32), rows_in, scale, gain_ref[...])
    out_ref[0, :, 0, :] = total


def token_grad(grad_normed, rows_in, grad_second, gain):
    seqs, rows, width = grad_normed.shape
    part = pl.BlockSpec((1, rows, width), lambda i: (i, 0, 0))
    return pl.pallas_call(
        token_grad_kernel,
        grid=(seqs,),
        in_specs=[part, part, part, whole((1, width))],
        out_specs=pl.BlockSpec((1, rows, 1, width), lambda i: (i, 0, 0, 0)),
        out_shape=jax.ShapeDtypeStruct((seqs, rows, 1, width), f32),
        compiler_params=params(SMALL_LIMIT),
        cost_estimate=cost(1000, 1000),
        name="token_grad",
    )(grad_normed, rows_in, grad_second, gain.reshape(1, width))


def outer_kernel(left_ref, right_ref, out_ref):
    out_ref[...] = dot32(left_ref[...], right_ref[...]).astype(bf16)


def outer(left, right, number, count):
    height, depth = left.shape[0] // count, left.shape[1]
    width = right.shape[1]
    tile = math.gcd(width, 512)
    return pl.pallas_call(
        outer_kernel,
        grid=(width // tile,),
        in_specs=[
            pl.BlockSpec((height, depth), lambda j: (number, 0)),
            pl.BlockSpec((depth, tile), lambda j: (0, j)),
        ],
        out_specs=pl.BlockSpec((height, tile), lambda j: (0, j)),
        out_shape=jax.ShapeDtypeStruct((height, width), bf16),
        compiler_params=params(),
        cost_estimate=cost(2 * height * depth * width, 2 * depth * width),
        name="weight_gradient",
    )(left, right)


def gather_whole(block):
    return lax.all_gather(block, "mp", axis=0)


def scatter_whole(partial_sums):
    return lax.psum_scatter(partial_sums, "mp", scatter_dimension=0).astype(f32)


def finish_kernel(end_ref, *refs):
    out_ref = refs[-1]
    count = len(refs) // 2
    for number in range(count):

        @pl.when(pl.program_id(0) == number)
        def _(number=number):
            outward, total = refs[2 * number][...].astype(f32), refs[2 * number + 1][...].astype(f32)
            out_ref[...] = jnp.where(end_ref[0] == 1, outward, total)


def finish(end, pairs):
    height, width = pairs[0][1].shape
    operands = [array for pair in pairs for array in pair]
    return pl.pallas_call(
        finish_kernel,
        grid_spec=pltpu.PrefetchScalarGridSpec(
            num_scalar_prefetch=1,
            grid=(len(pairs),),
            in_specs=[whole(op.shape) for op in operands],
            out_specs=pl.BlockSpec((height, width), lambda i, e: (i, 0)),
        ),
        out_shape=jax.ShapeDtypeStruct((height * len(pairs), width), f32),
        compiler_params=params(SMALL_LIMIT),
        cost_estimate=cost(1000, 1000),
        name="finish",
    )(end, *operands)


def add_kernel(left_ref, right_ref, out_ref):
    out_ref[...] = (left_ref[...].astype(f32) + right_ref[...].astype(f32)).astype(bf16)


def add(left, right):
    height, width = left.shape
    rows = height // 2 if height % 32 == 0 and height > 128 else height
    piece = pl.BlockSpec((rows, width), lambda i: (i, 0))
    return pl.pallas_call(
        add_kernel,
        grid=(height // rows,),
        in_specs=[piece, piece],
        out_specs=piece,
        out_shape=jax.ShapeDtypeStruct(left.shape, bf16),
        compiler_params=params(SMALL_LIMIT),
        cost_estimate=cost(1000, 1000),
        name="add",
    )(left, right)


def merge_kernel(end_ref, part_ref, left_ref, right_ref, out_ref):
    total = (left_ref[...].astype(f32) + right_ref[...].astype(f32)).astype(bf16)
    out_ref[...] = jnp.where(end_ref[0] == 1, part_ref[...].astype(f32), total.astype(f32)).astype(bf16)


def merge(end, part, left, right):
    piece = pl.BlockSpec(left.shape, lambda i, e: (0, 0))
    return pl.pallas_call(
        merge_kernel,
        grid_spec=pltpu.PrefetchScalarGridSpec(
            num_scalar_prefetch=1, grid=(1,), in_specs=[piece] * 3, out_specs=piece
        ),
        out_shape=jax.ShapeDtypeStruct(left.shape, bf16),
        compiler_params=params(SMALL_LIMIT),
        cost_estimate=cost(1000, 1000),
        name="merge",
    )(end, part, left, right)


def together(*values):
    return lax.optimization_barrier(values)


def together(*values):
    return lax.optimization_barrier(values)


class WholeGather:
    def __init__(self, block):
        self.here = gather_whole(block)

    def tie(self, names, *values):
        return values

    def reach(self):
        pass

    def near(self):
        return [(self.here[i],) for i in range(self.here.shape[0])]

    def side(self):
        return []

    def far(self):
        return []


class Plain:
    def __init__(self):
        self.parts = []

    def counts(self, size):
        return (size, 0, 0)

    def origin(self):
        return jnp.zeros((1,), jnp.int32)

    def gather(self, block):
        return WholeGather(block)

    def scatter(self, array, product, coming, compute):
        return scatter_whole(product(array)), compute()

    def sum_mp(self, part):
        return lax.psum(part, "mp")

    def hop(self, *values, part=None, last=False):
        if part is not None:
            self.parts.append(lax.psum(part, "dp"))
        return values

    def sums(self):
        return self.parts

    def join(self, first, last):
        return jnp.concatenate([part.astype(f32) for part in self.parts[first:last]], axis=0)

    def inward(self, part):
        return lax.psum(part, "dp")

    def across(self, part, came):
        return came, came

    def outward(self, half, came):
        return came, came

    def settled(self, total, came):
        return came.astype(f32)


def swap(block, bit):
    return lax.ppermute(block, "mp", [(i, i ^ bit) for i in range(8)])


class SquareGather:
    def __init__(self, block):
        self.here = {"near": (block, swap(block, 1)), "side": (swap(block, 2), swap(block, 4))}

    def tie(self, names, *values):
        held, values = together([self.here[name] for name in names], values)
        self.here.update(zip(names, held))
        return values

    def reach(self):
        x_all, y_all = self.here["side"]
        cut = x_all.shape[0] // 2
        self.here["far"] = (swap(x_all[:cut], 4), swap(y_all[cut:], 2))

    def near(self):
        return [(block,) for block in self.here["near"]]

    def side(self):
        return [(block,) for here in self.here["side"] for block in (here, swap(here, 1))]

    def far(self):
        halves = self.here["far"]
        return [halves, tuple(swap(half, 1) for half in halves)]


class Lane:
    def __init__(self):
        self.queue, self.flight, self.done = [], {}, []
        self.part = self.half = self.total = None

    def advance(self, end):
        flight = self.flight
        if "out" in flight:
            self.done.append((flight["out"], self.total))
        half = add(self.part, flight["in"]) if "in" in flight else None
        self.part = self.queue.pop(0) if self.queue else None
        started = {}
        if "across" in flight and self.part is not None and self.part.shape == self.half.shape:
            self.total = merge(end, self.part, self.half, flight["across"])
            started["in"] = started["out"] = lax.ppermute(self.total, "dp", [(0, 1), (3, 2), (1, 0), (2, 3)])
        else:
            if self.part is not None:
                started["in"] = lax.ppermute(self.part, "dp", [(0, 1), (3, 2)])
            if "across" in flight:
                self.total = add(self.half, flight["across"])
                started["out"] = lax.ppermute(self.total, "dp", [(1, 0), (2, 3)])
        if half is not None:
            started["across"] = lax.ppermute(half, "dp", [(1, 2), (2, 1)])
        self.half, self.flight = half, started


class Square:
    def __init__(self):
        self.lanes, self.turn = (Lane(), Lane()), 0

    def counts(self, size):
        return (2, 4, 2)

    def origin(self):
        return lax.axis_index("mp").astype(jnp.int32).reshape(1)

    def gather(self, block):
        return SquareGather(block)

    def scatter(self, array, product, coming, compute):
        def both(mine, other):
            return mine.astype(f32) + swap(other, 1).astype(f32)

        far, array = together(product(array[6:8]), array)
        half = far.shape[1] // 2
        far_sum = both(far[0], far[1])
        far_low, far_high = far_sum[:half].astype(bf16), far_sum[half:].astype(bf16)
        side, near, far_low, far_high = together(product(array[2:6]), product(array[0:2]), far_low, far_high)
        from_far_low, from_far_high = swap(far_low, 2), swap(far_high, 4)
        x_sum = both(side[0], side[1])
        y_sum = both(side[2], side[3])
        own = both(near[0], near[1])
        own, x_sum, y_sum = coming.tie(["near", "side"], own, x_sum, y_sum)
        own_low_x = swap(x_sum[:half].astype(bf16), 2)
        own_high_y = swap(y_sum[half:].astype(bf16), 4)
        beside = compute()
        from_far_low, from_far_high, own_low_x, own_high_y, beside = together(
            from_far_low, from_far_high, own_low_x, own_high_y, beside
        )
        y_low = (y_sum[:half] + from_far_low.astype(f32)).astype(bf16)
        x_high = (x_sum[half:] + from_far_high.astype(f32)).astype(bf16)
        own_low_y = swap(y_low, 4)
        own_high_x = swap(x_high, 2)
        low = own[:half] + own_low_x.astype(f32) + own_low_y.astype(f32)
        high = own[half:] + own_high_y.astype(f32) + own_high_x.astype(f32)
        return jnp.concatenate([low, high], axis=0), beside

    def sum_mp(self, part):
        for bit in (1, 2, 4):
            part = part + swap(part, bit)
        return part

    def end(self):
        place = lax.axis_index("dp")
        return ((place == 0) | (place == 3)).astype(jnp.int32).reshape(1)

    def hop(self, *values, part=None, last=False):
        lane = self.lanes[self.turn]
        self.turn = 1 - self.turn
        if last:
            done = [each.done for each in self.lanes]
            lane.flight, done, values = together(lane.flight, done, values)
            for each, sums in zip(self.lanes, done):
                each.done = list(sums)
        else:
            lane.flight, part, values = together(lane.flight, part, values)
        if part is not None:
            cut = part.shape[0] // 2
            for each, half in zip(self.lanes, (part[:cut], part[cut:])):
                each.queue.append(half)
        lane.advance(self.end())
        return values

    def join(self, first, last):
        return finish(self.end(), [lane.done[number] for number in range(first, last) for lane in self.lanes])


    def inward(self, part):
        return lax.ppermute(part, "dp", [(0, 1), (3, 2)])

    def across(self, part, came):
        half = add(part, came)
        return half, lax.ppermute(half, "dp", [(1, 2), (2, 1)])

    def outward(self, half, came):
        total = add(half, came)
        return total, lax.ppermute(total, "dp", [(1, 0), (2, 3)])

    def settled(self, total, came):
        return jnp.where(self.end()[0] == 1, came, total).astype(f32)


def local(
    links, tokens, lengths, norm_gain, in_proj, short_taps, conv_skip, filter_residue, filter_rate, filter_freq,
    out_proj, mlp_gain, gate_proj, up_proj, down_proj, cotangent,
):
    micro, rows, per_dev, width = tokens.shape
    seqs = micro * per_dev
    chans = in_proj.shape[2]
    hidden_units = gate_proj.shape[1]
    length = rows * lax.axis_size("mp")
    in_parts = in_proj.transpose(1, 0, 2)
    in_flat = in_proj.reshape(width, 3 * chans)
    gate_t, up_t = gate_proj.T, up_proj.T
    table = dft_matrix(length)
    dft = jnp.asarray(table, bf16)
    inverse = jnp.asarray(table.T / length, bf16)
    me = links.origin()

    def by_sequence(array):
        return array.transpose(0, 2, 1, 3).reshape(seqs, rows, array.shape[3])

    def by_position(array):
        return array.reshape(micro, per_dev, rows, array.shape[2]).transpose(0, 2, 1, 3)

    def flat(array):
        return array.reshape(-1, array.shape[-1])

    def grouped(array, like):
        return array.reshape(like.shape[:-1] + (array.shape[-1],))

    positions = lax.axis_index("mp") * rows + jnp.arange(rows)
    valid = (positions[None, :] < lengths.reshape(seqs)[:, None]).astype(f32)[:, :, None]

    rows_in = by_sequence(tokens).astype(f32)
    scale_in = row_scale(rows_in)
    normed = (rows_in * scale_in * norm_gain).astype(bf16)
    coming = links.gather(normed)

    high = (STEP * jnp.arange(length // STEP)).astype(f32)[:, None, None]
    low = jnp.arange(STEP).astype(f32)[None, :, None]
    rate_t, freq_t, residue_t = filter_rate.T, filter_freq.T, filter_residue.T
    decay_high, turn_high = jnp.exp(-rate_t * high), freq_t * high
    decay_low, turn_low = jnp.exp(-rate_t[:, None, :] * low), freq_t[:, None, :] * low
    tables = (
        decay_high * jnp.cos(turn_high),
        decay_high * jnp.sin(turn_high),
        decay_low * jnp.cos(turn_low),
        decay_low * jnp.sin(turn_low),
    )
    filt_spec = make_filter(tables, residue_t, dft)
    grad_final = by_sequence(cotangent).astype(f32) * valid
    grad_final_low = grad_final.astype(bf16)
    blocks = lax.axis_size("mp")
    counts = links.counts(blocks)
    starts = [sum(counts[:i]) for i in range(len(counts))]

    def arrive(kernel, group, number, fixed, per_block, outputs, filled):
        if not group:
            return filled
        return on_arrival(kernel, me, group, starts[number], blocks, fixed, per_block, outputs, filled)

    def projected(group, number, filled):
        return arrive(project_kernel, group, number, (in_parts,), (), ((3 * chans, f32, False), (width, bf16, False)), filled)

    filled = projected(coming.near(), 0, ())
    filled, filt_spec, grad_final_low, in_flat = coming.tie(["side"], filled, filt_spec, grad_final_low, in_flat)
    coming.reach()
    filled = projected(coming.side(), 1, filled)
    filled, grad_final_low = coming.tie(["far"], filled, grad_final_low)
    grad_coming = links.gather(grad_final_low)
    proj, normed_all = projected(coming.far(), 2, filled)
    proj = proj.reshape(blocks, seqs, rows, 3 * chans)
    taps9 = short_taps.reshape(9, chans)
    skip = conv_skip.reshape(1, chans)
    gated, gated_ordered, response, spec = mixer(me, proj, taps9, skip, filt_spec, dft, inverse)
    (gated,) = grad_coming.tie(["side"], gated)
    grad_coming.reach()

    def mixed_out(part):
        return grouped(dot32(flat(part), out_proj).astype(bf16), part)

    def hidden_backed(group, number, filled):
        return arrive(hidden_back_kernel, group, number, (down_proj,), (), ((hidden_units, f32, True), (width, bf16, False)), filled)

    def beside_scatter():
        return hidden_backed(grad_coming.side(), 1, hidden_backed(grad_coming.near(), 0, ()))

    mixed_sum, filled = links.scatter(gated, mixed_out, grad_coming, beside_scatter)
    second = rows_in + mixed_sum
    scale_second = row_scale(second)
    mlp_normed = (second * scale_second * mlp_gain).astype(bf16)
    coming = links.gather(mlp_normed)
    grad_hidden, grad_final_all = hidden_backed(grad_coming.far(), 2, filled)

    def fed(group, number, filled):
        outputs = ((hidden_units, bf16, True),) * 3 + ((width, bf16, False),)
        return arrive(feed_kernel, group, number, (gate_t, up_t), (grad_hidden,), outputs, filled)

    (filled,) = coming.tie(["side"], fed(coming.near(), 0, ()))
    coming.reach()
    filled = fed(coming.side(), 1, filled)
    (filled,) = coming.tie(["far"], filled)
    hidden, grad_gate, grad_up, mlp_all = fed(coming.far(), 2, filled)

    def weight_gradient(left, right):
        return contract_rows(flat(left), flat(right)).astype(bf16)

    def blocked(array):
        return array.reshape(blocks, seqs, rows, array.shape[-1])

    grad_final_all, mlp_all = flat(grad_final_all), flat(mlp_all)
    links.hop(part=outer(hidden, grad_final_all, 0, 2))
    links.hop()
    grad_gate, grad_up, hidden = links.hop(
        grad_gate, grad_up, hidden, part=outer(hidden, grad_final_all, 1, 2)
    )
    mlp_back = blocked(sum_products(contract_rows, (gate_t, up_t), bf16, True)(blocks, grad_gate, grad_up))
    mlp_back, grad_gate = links.hop(mlp_back, grad_gate)
    grad_mlp_normed = scatter_whole(mlp_back)
    grad_gate, grad_up = links.hop(grad_gate, grad_up, part=outer(grad_gate, mlp_all, 0, 2))
    gate_two, grad_up = links.hop(outer(grad_gate, mlp_all, 1, 2), grad_up)
    up_one, grad_up = links.hop(outer(grad_up, mlp_all, 0, 2), grad_up, part=gate_two)
    up_two, second = links.hop(outer(grad_up, mlp_all, 1, 2), second)
    second, hidden = links.hop(second, hidden, part=up_one)
    grad_second = grad_final + norm_back(grad_mlp_normed, second, scale_second, mlp_gain)
    gain_two = jnp.sum(grad_mlp_normed * second * scale_second, axis=(0, 1))
    grad_branch_all = gather_whole(grad_second.astype(bf16))
    mlp_part = blocked(sum_products(contract_rows, (down_proj,), bf16, True)(blocks, hidden))
    mlp_part, gain_two = links.hop(mlp_part, gain_two)
    mlp_part, gated_ordered = links.hop(mlp_part, gated_ordered, part=up_two)
    mlp_part, gated_ordered = links.hop(mlp_part, gated_ordered)

    grad_gated = blocked(
        sum_products(contract_cols, (out_proj,), f32, False)(blocks, grad_branch_all.reshape(blocks, -1, width))
    )
    grad_out = weight_gradient(gated_ordered, grad_branch_all)
    grad_gated, mlp_part = links.hop(grad_gated, mlp_part, part=grad_out)
    mlp_out = scatter_whole(mlp_part)
    back = ()
    for number in range(seqs - 1):
        back = mixer_back(number, back, grad_gated, proj, response, spec, taps9, skip, filt_spec, dft, inverse)
    back, grad_gated = links.hop(back, grad_gated)
    grad_proj, grad_taps, grad_filt = mixer_back(
        seqs - 1, tuple(back), grad_gated, proj, response, spec, taps9, skip, filt_spec, dft, inverse
    )
    grad_in = weight_gradient(normed_all, grad_proj)
    grads_in = [grad_in[:, part * chans : (part + 1) * chans] for part in range(3)]
    grads_in, grad_proj, grad_filt = links.hop(grads_in, grad_proj, grad_filt, part=grads_in[0])
    grad_in_rows = blocked(contract_cols(flat(grad_proj), in_flat).astype(bf16).reshape(blocks, -1, width))
    grad_in_rows, grads_in = links.hop(grad_in_rows, grads_in)
    grads_in, grad_filt = links.hop(grads_in, grad_filt, part=grads_in[1])
    grad_normed = scatter_whole(grad_in_rows)

    ones = jnp.ones((8, chans), bf16)
    against = sum(
        contract_cols(ones, (grad.astype(f32) * part.astype(f32)).astype(bf16))[0]
        for grad, part in zip(grads_in, in_parts)
    )
    gains = jnp.stack([against / norm_gain, gain_two], axis=0)
    gains, grad_filt = links.hop(gains, grad_filt)
    pole_sum, pole_re, pole_im = pole_gradients(grad_filt, tables)
    gains, pole_sum = links.hop(links.sum_mp(gains), pole_sum, part=grads_in[2])
    poles = filter_residue.shape[1]
    small = [grad_taps, pole_sum, -residue_t * pole_re, -residue_t * pole_im, gains.reshape(-1, chans)]
    small = [jnp.pad(rows_of, ((0, -rows_of.shape[0] % 8), (0, 0))) for rows_of in small]
    bounds = np.cumsum([0] + [rows_of.shape[0] for rows_of in small])
    small = jnp.pad(jnp.concatenate(small, axis=0), ((0, -int(bounds[-1]) % 32), (0, 0))).astype(bf16)
    (small,) = links.hop(small)
    came = links.inward(small)
    links.hop()
    (came,) = links.hop(came)
    half, came = links.across(small, came)
    grad_second, mlp_out = links.hop(grad_second, mlp_out)
    layer_out = ((second + mlp_out) * valid).astype(bf16)
    half, came, layer_out, grad_second = links.hop(half, came, layer_out, grad_second, last=True)
    total, came = links.outward(half, came)
    if per_dev == 1:
        grad_tokens = token_grad(grad_normed, by_sequence(tokens), grad_second, norm_gain)
    else:
        grad_tokens = by_position(grad_second + norm_back(grad_normed, rows_in, scale_in, norm_gain))
    sum_down, sum_gate, sum_up, sum_out = (links.join(*at) for at in ((0, 2), (2, 4), (4, 6), (6, 7)))
    grad_tokens, total = links.hop(grad_tokens, total)
    came, sum_down, sum_gate, sum_up, sum_out = links.hop(came, sum_down, sum_gate, sum_up, sum_out)
    sum_small = links.settled(total, came)
    sum_in = links.join(7, 10).reshape(3, width, chans)
    small = [sum_small[low:high] for low, high in zip(bounds[:-1], bounds[1:])]
    gains = small[4][: 2 * width // chans].reshape(2, width)
    return (
        by_position(layer_out),
        grad_tokens,
        gains[0],
        sum_in.transpose(1, 0, 2),
        small[0][:9].reshape(3, 3, chans),
        small[0][9],
        small[1][:poles].T,
        small[2][:poles].T,
        small[3][:poles].T,
        sum_out,
        gains[1],
        sum_gate.T,
        sum_up.T,
        sum_down,
    )


def solution(mesh):
    square = mesh.shape["mp"] == 8 and mesh.shape["dp"] == 4
    links = Square() if square else Plain()
    wide = P(None, "mp", "dp", None)
    chan = P("mp", None)
    return jax.shard_map(
        partial(local, links),
        mesh=mesh,
        in_specs=(
            wide, P(None, "dp"), P(), P(None, None, "mp"), P(None, None, "mp"), P("mp"), chan, chan, chan,
            chan, P(), P(None, "mp"), P(None, "mp"), chan, wide,
        ),
        out_specs=(
            wide, wide, P(), P(None, None, "mp"), P(None, None, "mp"), P("mp"), chan, chan, chan,
            chan, P(), P(None, "mp"), P(None, "mp"), chan,
        ),
        check_vma=False,
    )
```
